128 devices in a mesh: dp: 8 (over y_hi, x), head: 8 (over z, core), pair: 2 (over y_lo).
Axes of the slice: x: 4, y: 4 (y_hi: 2, y_lo: 2; y = y_hi * 2 + y_lo), z: 4, core: 2. Of those that a mesh axis runs over, the one named last changes fastest.
Arguments:
- hidden: bfloat16 [8, 2, 384, 4096], P('dp', 'pair'), may hold values from -200 to 200
- d_out: bfloat16 [8, 2, 384, 4096], P('dp', 'pair'), may hold values from -0.59765625 to 0.59765625
- norm_gain: float32 [4096], replicated, may hold values from 0.1 to 1.9
- w_query: bfloat16 [4096, 4096], P(('dp', 'pair'), 'head'), may hold values from -1 to 1
- w_key: bfloat16 [4096, 1024], P(('dp', 'pair'), 'head'), may hold values from -1 to 1
- w_value: bfloat16 [4096, 1024], P(('dp', 'pair'), 'head'), may hold values from -0.25 to 0.25
- w_out: bfloat16 [4096, 4096], P('head', ('dp', 'pair')), may hold values from -0.5 to 0.5
- prompt_len: int32 [8], P('dp'), may hold values from 257 to 512, as said below
- resp_len: int32 [8, 2], P('dp', 'pair'), may hold values from 32 to 128, as said below
Outputs:
- branch: bfloat16 [8, 2, 384, 4096], P('dp', 'pair', None, 'head')
- grad_hidden: float32 [8, 2, 384, 4096], P('dp', 'pair', None, 'head')
- grad_w_query: float32 [4096, 4096], P(('dp', 'pair'), 'head')
- grad_w_key: float32 [4096, 1024], P(('dp', 'pair'), 'head')
- grad_w_value: float32 [4096, 1024], P(('dp', 'pair'), 'head')
- grad_w_out: float32 [4096, 4096], P('head', ('dp', 'pair'))
- grad_gain: float32 [4096], replicated
The draws below stay inside these ranges and needn't reach their ends.
Inputs may be any that keep to these rules, and one draw needn't show every extreme that they name: The live prompt of pair b is prompt slots 0 to prompt_len[b] - 1 of its 512; in every draw some pair's prompt fills all of them. The live response tokens are the first resp_len slots of that response; in every draw some response fills all 128.
All inputs are finite; a program needn't handle non-finite values.
Results may differ from the reference program's by a relative error of at most 0.02.
The reference program's roundings to bfloat16 on the way count: a program that leaves them out, or rounds other values in their place, can miss the bound.
Values may be sent and summed in bfloat16 or wider, within the bound.
A program may use at most 128 MiB of HBM per device.

```python
import jax
import jax.numpy as jnp
from jax import lax

D = 4096
HEADS = 32
KV_HEADS = 8
HEAD_DIM = 128
HALF = 256
RESP = 128
PAIRS = 8
SLOTS = 384
N_HEAD = 8


def draw_hidden(key, part):
    key = jax.random.fold_in(key, 11)
    keys = jax.random.split(key, 3)
    shape = (PAIRS, 2, SLOTS, D)
    row_scale = jnp.exp(jax.random.uniform(keys[0], (PAIRS, 2, SLOTS, 1), dtype=jnp.float32) * jnp.log(10.0))
    col_scale = jnp.exp(jax.random.uniform(keys[1], (D,), minval=-1.0, maxval=1.0, dtype=jnp.float32) * jnp.log(3.0))
    base = jnp.clip(jax.random.normal(keys[2], shape, dtype=jnp.float32), -6.0, 6.0)
    return (base * row_scale * col_scale).astype(jnp.bfloat16)


def draw_w_query(key, part):
    key = jax.random.fold_in(key, 12)
    keys = jax.random.split(key, 1)
    shape = (D, HEADS * HEAD_DIM)
    values = jnp.clip(jax.random.normal(keys[0], shape, dtype=jnp.float32), -6.0, 6.0) * D ** (-0.5)
    return values.astype(jnp.bfloat16)


def draw_w_key(key, part):
    key = jax.random.fold_in(key, 13)
    keys = jax.random.split(key, 1)
    shape = (D, KV_HEADS * HEAD_DIM)
    values = jnp.clip(jax.random.normal(keys[0], shape, dtype=jnp.float32), -6.0, 6.0) * D ** (-0.5)
    return values.astype(jnp.bfloat16)


def draw_prompt_len(key, part):
    key = jax.random.fold_in(key, 14)
    first, second = jax.random.split(key)
    lengths = jax.random.randint(first, (PAIRS,), HALF + 1, 2 * HALF + 1)
    full = jax.random.randint(second, (), 0, PAIRS)
    return jnp.where(jnp.arange(PAIRS) == full, 2 * HALF, lengths).astype(jnp.int32)


def draw_resp_len(key, part):
    key = jax.random.fold_in(key, 15)
    first, second = jax.random.split(key)
    lengths = jax.random.randint(first, (PAIRS * 2,), RESP // 4, RESP + 1)
    full = jax.random.randint(second, (), 0, PAIRS * 2)
    lengths = jnp.where(jnp.arange(PAIRS * 2) == full, RESP, lengths)
    return lengths.reshape(PAIRS, 2).astype(jnp.int32)


def block_scale(stream_key, extent, cuts, least, largest):
    gain, own = 1.0, jax.random.fold_in(stream_key, 6)
    for position, shards_of in cuts:
        draws = jnp.exp(jax.random.uniform(jax.random.fold_in(own, position), (shards_of,), jnp.float32, least / len(cuts), largest / len(cuts)))
        gain = gain * jnp.repeat(draws, extent[position] // shards_of).reshape([-1 if axis == position else 1 for axis in range(len(extent))])
    return gain


def normal_values(rng, shape, scale, reach, cuts=(), kind=jnp.bfloat16):
    result = scale * jax.random.normal(rng, shape, jnp.float32)
    if cuts:
        result = result * block_scale(rng, shape, cuts, -0.22, 0.18)
    return jnp.clip(result, -reach, reach).astype(kind)


def setup_inputs(seed: int = 0) -> dict:
    key_list = jax.random.split(jax.random.key(seed), 10)
    return {
        "hidden": draw_hidden(jax.random.fold_in(key_list[9], 71), 0),
        "d_out": normal_values(key_list[1], (PAIRS, 2, SLOTS, D), 0.1, 0.59765625, ((0, 8), (1, 2))),
        "norm_gain": jnp.clip(1.0 + 0.18 * jax.random.normal(key_list[2], (D,), jnp.float32), 0.1, 1.9),
        "w_query": draw_w_query(jax.random.fold_in(key_list[9], 71), 0),
        "w_key": draw_w_key(jax.random.fold_in(key_list[9], 71), 0),
        "w_value": normal_values(key_list[5], (D, KV_HEADS * HEAD_DIM), (D // 8) ** -0.5, 0.25, ((0, 16), (1, 8))),
        "w_out": normal_values(key_list[6], (HEADS * HEAD_DIM, D), HEAD_DIM ** -0.5, 0.5, ((0, 8), (1, 16))),
        "prompt_len": draw_prompt_len(jax.random.fold_in(key_list[9], 71), 0),
        "resp_len": draw_resp_len(jax.random.fold_in(key_list[9], 71), 0),
    }


EPS = 1e-05
BASE = 500000.0

def rope_tables(positions):
    half_dim = HEAD_DIM // 2
    steps = jnp.arange(half_dim, dtype=jnp.float32) * (2.0 / HEAD_DIM)
    freqs = jnp.exp(-steps * jnp.log(jnp.float32(BASE)))
    angles = positions.astype(jnp.float32)[..., None] * freqs
    return (jnp.cos(angles), jnp.sin(angles))

def rotate(values, cosine, sine):
    first = values[..., :HEAD_DIM // 2]
    second = values[..., HEAD_DIM // 2:]
    return jnp.concatenate([first * cosine - second * sine, second * cosine + first * sine], -1)

def unrotate(grads, cosine, sine):
    first = grads[..., :HEAD_DIM // 2]
    second = grads[..., HEAD_DIM // 2:]
    return jnp.concatenate([first * cosine + second * sine, second * cosine - first * sine], -1)

def positions_of(partner, prompt_length):
    slot_ids = jnp.arange(HALF + RESP, dtype=jnp.int32)
    return jnp.where(slot_ids < HALF, partner * HALF + slot_ids, prompt_length + slot_ids - HALF)

def allowed(q_partner, q_slot, k_partner, k_slot, prompt_length, resp_length):
    q_prompt = q_slot < HALF
    k_prompt = k_slot < HALF
    q_place = q_partner * HALF + q_slot
    k_place = k_partner * HALF + k_slot
    prompt_key = k_prompt & (k_place < prompt_length) & (~q_prompt | (k_place <= q_place))
    resp_key = ~k_prompt & ~q_prompt & (k_partner == q_partner) & (k_slot <= q_slot) & (k_slot - HALF < resp_length)
    return prompt_key | resp_key

def head_forward(query, keys, values, mask):
    scores = jnp.einsum('rsgd,td->grst', query.astype(jnp.float32), keys.astype(jnp.float32)) * HEAD_DIM ** (-0.5)
    scores = jnp.where(mask, scores, -jnp.inf)
    row_max = lax.optimization_barrier(jnp.max(scores, -1, keepdims=True))
    expo = jnp.exp(scores - row_max)
    probs = expo / lax.optimization_barrier(jnp.sum(expo, -1, keepdims=True))
    rounded = probs.astype(jnp.bfloat16)
    attended = jnp.einsum('grst,td->rsgd', rounded.astype(jnp.float32), values.astype(jnp.float32))
    return (probs, rounded, attended)

def round_term(term):
    return lax.optimization_barrier(term.astype(jnp.bfloat16)).astype(jnp.float32)

def pair_step(weights, item):
    w_query, w_key, w_value, w_out, norm_gain = weights
    normed, scaled_in, inverse_rms, cotangent, prompt_length, resp_length = item
    slots_all = HALF + RESP
    width = normed.shape[-1]
    group = HEADS // KV_HEADS
    partners = jnp.arange(2, dtype=jnp.int32)
    cosine, sine = rope_tables(positions_of(partners[:, None], prompt_length))
    cosine = cosine[:, :, None, :]
    sine = sine[:, :, None, :]
    flat = normed.reshape(2 * slots_all, width)
    query = jnp.dot(flat, w_query, preferred_element_type=jnp.float32).reshape(2, slots_all, HEADS, HEAD_DIM)
    query = rotate(query, cosine, sine).astype(jnp.bfloat16)
    keys = jnp.dot(flat, w_key, preferred_element_type=jnp.float32).reshape(2, slots_all, KV_HEADS, HEAD_DIM)
    keys = rotate(keys, cosine, sine).astype(jnp.bfloat16)
    values = jnp.dot(flat, w_value, preferred_element_type=jnp.float32).astype(jnp.bfloat16)
    values = values.reshape(2 * slots_all, KV_HEADS, HEAD_DIM)
    slot_ids = jnp.arange(slots_all, dtype=jnp.int32)
    key_partner = jnp.repeat(partners, slots_all)
    key_slot = jnp.tile(slot_ids, 2)
    mask = allowed(partners[:, None, None], slot_ids[None, :, None], key_partner[None, None, :], key_slot[None, None, :], prompt_length, resp_length[:, None, None])
    cot_flat = cotangent.reshape(2 * slots_all, width)
    grad_attended = jnp.dot(cot_flat, w_out.T, preferred_element_type=jnp.float32).astype(jnp.bfloat16)
    grad_heads = jnp.moveaxis(grad_attended.reshape(2, slots_all, KV_HEADS, group, HEAD_DIM), 2, 0)
    query_heads = jnp.moveaxis(query.reshape(2, slots_all, KV_HEADS, group, HEAD_DIM), 2, 0)
    key_heads = jnp.moveaxis(keys.reshape(2 * slots_all, KV_HEADS, HEAD_DIM), 1, 0)
    value_heads = jnp.moveaxis(values, 1, 0)

    def one_head(parts):
        q_head, k_head, v_head, g_head = parts
        probs, rounded, attended = head_forward(q_head, k_head, v_head, mask)
        d_probs = jnp.einsum('rsgd,td->grst', g_head.astype(jnp.float32), v_head.astype(jnp.float32))
        delta = jnp.einsum('rsgd,rsgd->grs', g_head.astype(jnp.float32), attended)[..., None]
        d_scores = (probs * (d_probs - delta) * HEAD_DIM ** (-0.5)).astype(jnp.bfloat16)
        d_query = jnp.einsum('grst,td->rsgd', d_scores.astype(jnp.float32), k_head.astype(jnp.float32))
        d_keys = jnp.einsum('grst,rsgd->td', d_scores.astype(jnp.float32), q_head.astype(jnp.float32))
        d_values = jnp.einsum('grst,rsgd->td', rounded.astype(jnp.float32), g_head.astype(jnp.float32))
        return (attended.astype(jnp.bfloat16), d_query, d_keys, d_values)
    attended, d_query, d_keys, d_values = lax.map(one_head, (query_heads, key_heads, value_heads, grad_heads))
    attended = jnp.moveaxis(attended, 0, 2).reshape(2, slots_all, HEADS * HEAD_DIM)
    d_query = jnp.moveaxis(d_query, 0, 2).reshape(2, slots_all, HEADS, HEAD_DIM)
    d_query = unrotate(d_query, cosine, sine).astype(jnp.bfloat16).reshape(2, slots_all, HEADS * HEAD_DIM)
    d_keys = jnp.moveaxis(d_keys, 0, 1).reshape(2, slots_all, KV_HEADS, HEAD_DIM)
    d_keys = unrotate(d_keys, cosine, sine).astype(jnp.bfloat16).reshape(2, slots_all, KV_HEADS * HEAD_DIM)
    d_values = jnp.moveaxis(d_values, 0, 1).astype(jnp.bfloat16).reshape(2, slots_all, KV_HEADS * HEAD_DIM)
    attended_flat = attended.reshape(2 * slots_all, HEADS * HEAD_DIM)
    share = HEADS * HEAD_DIM // N_HEAD
    branch = jnp.zeros((2 * slots_all, width), jnp.float32)
    for block in range(N_HEAD):
        term = jnp.dot(attended_flat[:, block * share:(block + 1) * share], w_out[block * share:(block + 1) * share], preferred_element_type=jnp.float32)
        branch = branch + round_term(term)
    branch = branch.astype(jnp.bfloat16).reshape(2, slots_all, width)
    d_proj = jnp.concatenate([d_query, d_keys, d_values], -1)
    qkv_term = round_term(jnp.dot(normed[0].T, d_proj[0], preferred_element_type=jnp.float32))
    qkv_term = qkv_term + round_term(jnp.dot(normed[1].T, d_proj[1], preferred_element_type=jnp.float32))
    out_term = round_term(jnp.dot(attended[0].T, cotangent[0], preferred_element_type=jnp.float32))
    out_term = out_term + round_term(jnp.dot(attended[1].T, cotangent[1], preferred_element_type=jnp.float32))
    w_joined = jnp.concatenate([w_query, w_key, w_value], 1)
    d_norm = jnp.dot(d_proj.reshape(2 * slots_all, -1), w_joined.T, preferred_element_type=jnp.float32)
    scaled_flat = scaled_in.reshape(2 * slots_all, width)
    d_scaled = d_norm * norm_gain
    stat = lax.optimization_barrier(jnp.mean(d_scaled * scaled_flat, -1, keepdims=True))
    d_input = inverse_rms.reshape(2 * slots_all, 1) * (d_scaled - scaled_flat * stat)
    gain_term = lax.optimization_barrier(jnp.sum(d_norm * scaled_flat, 0))
    return (branch, d_input.reshape(2, slots_all, width), qkv_term, out_term, gain_term)

def reference(hidden, d_out, norm_gain, w_query, w_key, w_value, w_out, prompt_len, resp_len):
    inputs = hidden.astype(jnp.float32)
    inverse_rms = lax.rsqrt(lax.optimization_barrier(jnp.mean(inputs * inputs, -1, keepdims=True)) + EPS)
    scaled_in = inputs * inverse_rms
    normed = (scaled_in * norm_gain).astype(jnp.bfloat16)
    weights = (w_query, w_key, w_value, w_out, norm_gain)
    total_cols = (HEADS + 2 * KV_HEADS) * HEAD_DIM

    def scan_body(carry, item):
        qkv_sum, out_sum, gain_sum = carry
        branch, d_input, qkv_term, out_term, gain_term = pair_step(weights, item)
        return ((qkv_sum + qkv_term, out_sum + out_term, gain_sum + gain_term), (branch, d_input))
    init = (jnp.zeros((D, total_cols), jnp.float32), jnp.zeros((HEADS * HEAD_DIM, D), jnp.float32), jnp.zeros((D,), jnp.float32))
    carry, outputs = lax.scan(scan_body, init, (normed, scaled_in, inverse_rms, d_out, prompt_len, resp_len))
    qkv_sum, out_sum, gain_sum = carry
    branch, d_input = outputs
    q_cols = HEADS * HEAD_DIM
    kv_cols = KV_HEADS * HEAD_DIM
    return (branch, d_input, qkv_sum[:, :q_cols], qkv_sum[:, q_cols:q_cols + kv_cols], qkv_sum[:, q_cols + kv_cols:], out_sum, gain_sum)
```

```python
import functools

import jax
import jax.numpy as jnp
from jax import lax
from jax.experimental import pallas as pl
from jax.experimental.pallas import tpu as pltpu
from jax.sharding import PartitionSpec as P

HEAD_DIM = 128
HALF = 256
RESP = 128
SLOTS = HALF + RESP
KEYS = 2 * HALF + RESP
EPS = 1e-05
BASE = 500000.0
SCALE = HEAD_DIM ** (-0.5)
GROUP = 4
QC = GROUP * HEAD_DIM
WC = QC + 2 * HEAD_DIM
SHARDS = 16
ROWS = 256
MESH = pl.DeviceIdType.MESH
F32 = jnp.float32
BF16 = jnp.bfloat16
PLANE = 20


def dot_nn(a, b):
    return lax.dot_general(a, b, (((1,), (0,)), ((), ())), preferred_element_type=F32)


def dot_nt(a, b):
    return lax.dot_general(a, b, (((1,), (1,)), ((), ())), preferred_element_type=F32)


def dot_tn(a, b):
    return lax.dot_general(a, b, (((0,), (0,)), ((), ())), preferred_element_type=F32)


def step(value, offset):
    return lax.rem(value + offset % 4, 4)


GROUPS = (
    (1, lambda i: (2, 2)),
    (4, lambda i: ((1 + 2 * lax.rem(i, 2)) * (1 - i // 2) + 2 * (i // 2), 2 * (1 - i // 2) + (1 + 2 * lax.rem(i, 2)) * (i // 2))),
    (2, lambda i: (2 * i, 2 * (1 - i))),
    (4, lambda i: (1 + 2 * lax.rem(i, 2), 1 + 2 * (i // 2))),
    (4, lambda i: ((1 + 2 * lax.rem(i, 2)) * (1 - i // 2), (1 + 2 * lax.rem(i, 2)) * (i // 2))),
    (1, lambda i: (0, 0)),
)


def kernel(
    hidden, d_out, gain, wq, wk, wv, wo, plen, rlen,
    branch, g_hidden, g_wq, g_wk, g_wv, g_wo, g_gain,
    wg, wog, hid, dout, normed, norm_t, go, qa, qb, qc, qd, oa, ob, oc, od,
    p_core, p_za, p_zb, n_core, n_za, n_zb,
    probs, bias, pacc, attf, att, att_t, gatt, qh, kall, vall, cosf, sinf, inv, hslice,
    dproj, dkv, kv_out, kv_in, rstat, gx, gy, gh,
    load_sem, send_sem, recv_sem, core_send, core_recv, small_send, small_recv,
):
    dp, head, pair = lax.axis_index("dp"), lax.axis_index("head"), lax.axis_index("pair")
    x, y = lax.rem(dp, 4), (dp // 4) * 2 + pair
    z, c = head // 2, lax.rem(head, 2)

    def place(px, py):
        return ((py // 2) * 4 + px) * 2 + lax.rem(py, 2)

    def shard(dx, dy):
        return place(lax.rem(x + dx, 4), lax.rem(y + dy, 4))

    def device(px=x, py=y, h=head):
        return ((py // 2) * 4 + px, h, lax.rem(py, 2))

    def along(axis, k):
        if axis == "x":
            return device(px=step(x, k))
        if axis == "y":
            return device(py=step(y, k))
        if axis == "z":
            return device(h=step(z, k) * 2 + c)
        return device(h=z * 2 + (1 - c))

    pending = []

    def sent():
        for copy in pending:
            copy.wait_send()
        pending.clear()

    def start(src, dst, sems, index, target):
        copy = pltpu.make_async_remote_copy(
            src_ref=src, dst_ref=dst, send_sem=sems[0].at[index], recv_sem=sems[1].at[index],
            device_id=target, device_id_type=MESH,
        )
        copy.start()
        pending.append(copy)

    def arrived(dst, sems, index):
        pltpu.make_async_remote_copy(
            src_ref=dst, dst_ref=dst, send_sem=sems[0].at[index], recv_sem=sems[1].at[index],
            device_id=along("x", 1), device_id_type=MESH,
        ).wait_recv()

    plane_sems = (send_sem, recv_sem)
    core_sems = (core_send, core_recv)
    small_sems = (small_send, small_recv)

    def spot(h, a, b):
        return shard(a % 4, b % 4) if h == 0 else shard(b % 4, a % 4)

    def ring(h, primary):
        return "x" if (h == 0) == primary else "y"

    def part(rows, h, s=None):
        if s is None:
            return pl.ds(h * rows // 2, rows // 2)
        return pl.ds(h * rows // 2 + s * rows // 4, rows // 4)

    def gather(buf, t, rows):
        def go_(h, m, a, b, s, primary, k):
            ref = buf.at[spot(h, a, b), part(rows, h, s)]
            start(ref, ref, plane_sems, (t * 2 + h) * PLANE + m, along(ring(h, primary), k))

        def got(h, m, a, b, s=None):
            arrived(buf.at[spot(h, a, b), part(rows, h, s)], plane_sems, (t * 2 + h) * PLANE + m)

        both = (0, 1)
        for h in both:
            go_(h, 0, 0, 0, None, True, 1)
            go_(h, 1, 0, 0, None, True, -1)
        for h in both:
            go_(h, 4, 0, 0, None, False, 1)
            go_(h, 5, 0, 0, None, False, -1)
        yield
        for h in both:
            got(h, 0, -1, 0)
            go_(h, 2, -1, 0, 0, True, 1)
            got(h, 1, 1, 0)
            go_(h, 3, 1, 0, 1, True, -1)
        for h in both:
            for k in (1, 3):
                go_(h, 4 + 4 * k, k, 0, None, False, 1)
                go_(h, 5 + 4 * k, k, 0, None, False, -1)
        yield
        for h in both:
            got(h, 4, 0, -1)
            go_(h, 6, 0, -1, 0, False, 1)
            got(h, 5, 0, 1)
            go_(h, 7, 0, 1, 1, False, -1)
        yield 4
        for h in both:
            got(h, 2, 2, 0, 0)
            got(h, 3, 2, 0, 1)
            go_(h, 12, 2, 0, None, False, 1)
            go_(h, 13, 2, 0, None, False, -1)
        yield
        for k in (1, 3):
            for h in both:
                got(h, 4 + 4 * k, k, -1)
                go_(h, 6 + 4 * k, k, -1, 0, False, 1)
                got(h, 5 + 4 * k, k, 1)
                go_(h, 7 + 4 * k, k, 1, 1, False, -1)
        yield 3
        for h in both:
            got(h, 6, 0, 2, 0)
            got(h, 7, 0, 2, 1)
        yield 2
        for h in both:
            got(h, 12, 2, -1)
            go_(h, 14, 2, -1, 0, False, 1)
            got(h, 13, 2, 1)
            go_(h, 15, 2, 1, 1, False, -1)
        for h in both:
            for k in (1, 3):
                got(h, 6 + 4 * k, k, 2, 0)
                got(h, 7 + 4 * k, k, 2, 1)
        yield 1
        for h in both:
            got(h, 14, 2, 2, 0)
            got(h, 15, 2, 2, 1)
        yield 0

    def reduce(buf, ra, rb, rc, rd, t, rows, finish):
        def send(h, m, a, b, s, dst, primary, k):
            src = buf.at[spot(h, a, b), part(rows, h, s)]
            start(src, dst, plane_sems, (t * 2 + h) * PLANE + m, along(ring(h, primary), k))

        def got(h, m, dst):
            arrived(dst, plane_sems, (t * 2 + h) * PLANE + m)

        def add(h, a, b, s, *terms):
            j, rows_ = spot(h, a, b), part(rows, h, s)
            total = buf[j, rows_].astype(F32)
            for term in terms:
                total = total + term.astype(F32)
            buf[j, rows_] = total.astype(BF16)

        both = (0, 1)

        def begin(k):
            for h in both:
                send(h, 4 + 4 * k, k, 2, 0, ra.at[h, k, 0], False, 1)
                send(h, 5 + 4 * k, k, 2, 1, ra.at[h, k, 1], False, -1)

        def middle(k):
            for h in both:
                for s, way in ((0, 1), (1, -1)):
                    got(h, 4 + 4 * k + s, ra.at[h, k, s])
                    add(h, k, way, s, ra[h, k, s])
                    send(h, 6 + 4 * k + s, k, way, None, rb.at[h, k, s], False, way)

        def close(k):
            for h in both:
                for s in (0, 1):
                    got(h, 6 + 4 * k + s, rb.at[h, k, s])
                add(h, k, 0, None, rb[h, k, 0], rb[h, k, 1])

        begin(2)
        yield
        for k in (1, 3):
            begin(k)
        yield
        middle(2)
        begin(0)
        yield
        for k in (1, 3):
            middle(k)
        yield
        close(2)
        for h in both:
            send(h, 0, 2, 0, 0, rc.at[h, 0], True, 1)
            send(h, 1, 2, 0, 1, rc.at[h, 1], True, -1)
        yield
        middle(0)
        yield
        for k in (1, 3):
            close(k)
        for h in both:
            for s, way in ((0, 1), (1, -1)):
                got(h, s, rc.at[h, s])
                add(h, way, 0, s, rc[h, s])
                send(h, 2 + s, way, 0, None, rd.at[h, s], True, way)
        yield
        for h in both:
            for s in (0, 1):
                got(h, 6 + s, rb.at[h, 0, s])
                got(h, 2 + s, rd.at[h, s])
            total = buf[spot(h, 0, 0), part(rows, h)].astype(F32)
            for term in (rb[h, 0, 0], rb[h, 0, 1], rd[h, 0], rd[h, 1]):
                total = total + term.astype(F32)
            finish(part(rows, h), total)
        yield

    def head_reduce(buf, r_core, r_za, r_zb, t, finish):
        def block(k, core):
            return pl.ds(2 * (step(z, k) * 2 + core), 2)

        def add(k, rows, term):
            buf[block(k, c), rows] = (buf[block(k, c), rows].astype(F32) + term.astype(F32)).astype(BF16)

        every = pl.ds(0, SLOTS)
        sub = (pl.ds(0, SLOTS // 2), pl.ds(SLOTS // 2, SLOTS // 2))
        for k in (2, 1, 3, 0):
            start(buf.at[block(k, 1 - c)], r_core.at[k], core_sems, t * 8 + k, along("core", 1))
        yield
        arrived(r_core.at[2], core_sems, t * 8 + 2)
        add(2, every, r_core[2])
        for s, way in ((0, 1), (1, -1)):
            start(buf.at[block(2, c), sub[s]], r_za.at[s], core_sems, t * 8 + 4 + s, along("z", way))
        yield
        for s, way in ((0, 1), (1, -1)):
            arrived(r_core.at[way % 4], core_sems, t * 8 + way % 4)
            add(way, every, r_core[way % 4])
            arrived(r_za.at[s], core_sems, t * 8 + 4 + s)
            add(way, sub[s], r_za[s])
            start(buf.at[block(way, c)], r_zb.at[s], core_sems, t * 8 + 6 + s, along("z", way))
        yield
        arrived(r_core.at[0], core_sems, t * 8)
        arrived(r_zb.at[0], core_sems, t * 8 + 6)
        arrived(r_zb.at[1], core_sems, t * 8 + 7)
        for i in range(2):
            total = buf[2 * head + i].astype(F32) + r_core[0, i].astype(F32)
            finish(i, total + r_zb[0, i].astype(F32) + r_zb[1, i].astype(F32))
        yield

    def each(group, body):
        count, offsets = GROUPS[group]
        if count == 1:
            body(shard(*offsets(0)))
            return

        @pl.loop(0, count)
        def _(i):
            body(shard(*offsets(i)))

    own = shard(0, 0)
    loads = []
    for n, (src, dst) in enumerate(((hidden, hid), (d_out, dout))):
        for j in range(SHARDS):
            copy = pltpu.make_async_copy(src.at[:, pl.ds(j * ROWS, ROWS)], dst.at[j], load_sem.at[n * SHARDS + j])
            copy.start()
            loads.append(copy)
    barrier = pltpu.get_barrier_semaphore()
    others = [along("x", k) for k in (1, 2, 3)] + [along("y", k) for k in (1, 2, 3)]
    head_others = [device(h=lax.rem(head + k, 8)) for k in range(1, 8)]
    for target in others + head_others:
        pl.semaphore_signal(barrier, inc=1, device_id=target, device_id_type=MESH)
    wg[own, :, 0:QC] = wq[...]
    wg[own, :, QC:QC + HEAD_DIM] = wk[...]
    wg[own, :, QC + HEAD_DIM:] = wv[...]
    wog[own] = wo[...]
    pl.semaphore_wait(barrier, 13)

    w_gather = gather(wg, 0, ROWS)
    o_gather = gather(wog, 1, QC)
    next(w_gather)

    for copy in loads[:SHARDS]:
        copy.wait()
    pacc[:, 0:ROWS] = jnp.zeros((SLOTS, ROWS), F32)

    @pl.loop(0, SHARDS)
    def _(j):
        block = hid[j].astype(F32)
        pacc[:, 0:ROWS] += block * block

    mean = jnp.sum(pacc[:, 0:ROWS], -1, keepdims=True) * (1.0 / (SHARDS * ROWS))
    inv[...] = jnp.broadcast_to(lax.rsqrt(mean + EPS), (SLOTS, ROWS))

    def norm_block(j):
        block = (hid[j].astype(F32) * inv[...] * gain[j]).astype(BF16)
        normed[j] = block
        norm_t[j] = block.T

    @pl.loop(0, SHARDS // 2)
    def _(j):
        norm_block(j)

    next(w_gather)

    @pl.loop(SHARDS // 2, SHARDS)
    def _(j):
        norm_block(j)

    for i in range(2):
        hslice[i] = hid[2 * head + i]

    prompt_length, resp_length = plen[0], rlen[0]
    slot = lax.broadcasted_iota(jnp.int32, (SLOTS, HEAD_DIM), 0)
    lane = lax.broadcasted_iota(jnp.int32, (8, HEAD_DIM), 1)
    entry = jnp.where(lane < HEAD_DIM // 2, lane, lane - HEAD_DIM // 2)
    freqs = jnp.exp(-(entry.astype(F32) * (2.0 / HEAD_DIM)) * jnp.log(jnp.full((8, HEAD_DIM), BASE, F32)))
    position = jnp.where(slot < HALF, pair * HALF + slot, prompt_length + slot - HALF).astype(F32)
    angle = position * freqs[0:1]
    cosf[...] = jnp.cos(angle)
    sign = jnp.where(lane[0:1] < HEAD_DIM // 2, -1.0, 1.0).astype(F32)
    sinf[...] = jnp.sin(angle) * sign
    s_id = lax.broadcasted_iota(jnp.int32, (SLOTS, KEYS), 0)
    t_id = lax.broadcasted_iota(jnp.int32, (SLOTS, KEYS), 1)
    prompt_key = (t_id < 2 * HALF) & (t_id < prompt_length) & ((s_id >= HALF) | (t_id <= pair * HALF + s_id))
    resp_id = t_id - 2 * HALF
    resp_key = (t_id >= 2 * HALF) & (s_id >= HALF) & (resp_id <= s_id - HALF) & (resp_id < resp_length)
    bias[...] = jnp.where(prompt_key | resp_key, 0.0, -1e30).astype(BF16)

    pacc[...] = dot_nn(normed[own], wg[own])

    def project(j):
        pacc[...] += dot_nn(normed[j], wg[j])

    def pump(gen, times=1, body=None):
        for _ in range(times):
            group = next(gen)
            if group is not None and body is not None:
                each(group, body)

    pump(w_gather, 3, project)
    next(o_gather)
    pump(w_gather, 3, project)
    pump(o_gather)

    def rotate(u):
        return u * cosf[...] + pltpu.roll(u, HEAD_DIM // 2, 1) * sinf[...]

    def unrotate(u):
        return u * cosf[...] - pltpu.roll(u, HEAD_DIM // 2, 1) * sinf[...]

    mine = pl.ds(pl.multiple_of(pair * HALF, HALF), HALF)
    theirs = pl.ds(pl.multiple_of((1 - pair) * HALF, HALF), HALF)
    partner = device(py=(y // 2) * 2 + 1 - pair)
    keys = rotate(pacc[:, QC:QC + HEAD_DIM]).astype(BF16)
    values = pacc[:, QC + HEAD_DIM:].astype(BF16)
    kall[mine] = keys[:HALF]
    kall[2 * HALF:] = keys[HALF:]
    vall[mine] = values[:HALF]
    vall[2 * HALF:] = values[HALF:]
    start(kall.at[mine], kall.at[mine], small_sems, 0, partner)
    start(vall.at[mine], vall.at[mine], small_sems, 1, partner)
    for g in range(GROUP):
        qh[g] = rotate(pacc[:, g * HEAD_DIM:(g + 1) * HEAD_DIM]).astype(BF16)
    for copy in loads[SHARDS:]:
        copy.wait()
    gacc = pacc.at[:, 0:QC]
    gacc[...] = dot_nt(dout[own], wog[own])

    def grad_attend(j):
        gacc[...] += dot_nt(dout[j], wog[j])

    pump(o_gather, 1, grad_attend)
    arrived(kall.at[theirs], small_sems, 0)
    arrived(vall.at[theirs], small_sems, 1)

    for g in range(GROUP):
        cols = slice(g * HEAD_DIM, (g + 1) * HEAD_DIM)
        scores = dot_nt(qh[g], kall[...]) * SCALE + bias[...].astype(F32)
        expo = jnp.exp(scores - jnp.max(scores, -1, keepdims=True))
        prob = expo / jnp.sum(expo, -1, keepdims=True)
        probs[g] = prob
        out = dot_nn(prob.astype(BF16), vall[...])
        attf[:, cols] = out
        rounded = out.astype(BF16)
        att[:, cols] = rounded
        att_t[cols, :] = rounded.T
        pump(o_gather, 1, grad_attend)

    def out_term(j):
        go[j] = dot_nn(att_t[...], dout[j]).astype(BF16)

    def out_finish(rows, total):
        g_wo[rows, :] = total

    o_reduce = reduce(go, oa, ob, oc, od, 3, QC, out_finish)
    each(0, out_term)
    next(o_reduce)
    pump(o_gather, 1, grad_attend)
    each(1, out_term)
    next(o_reduce)
    gatt[...] = gacc[...].astype(BF16)
    each(2, out_term)
    next(o_reduce)
    each(3, out_term)
    next(o_reduce)
    each(4, out_term)
    each(5, out_term)

    dkv[...] = jnp.zeros_like(dkv)
    for g in range(GROUP):
        cols = slice(g * HEAD_DIM, (g + 1) * HEAD_DIM)
        g_head = gatt[:, cols]
        prob = probs[g]
        d_prob = dot_nt(g_head, vall[...])
        delta = jnp.sum(g_head.astype(F32) * attf[:, cols], -1, keepdims=True)
        d_score = (prob * (d_prob - delta) * SCALE).astype(BF16)
        dproj[:, cols] = unrotate(dot_nn(d_score, kall[...])).astype(BF16)
        dkv[0] += dot_tn(d_score, qh[g])
        dkv[1] += dot_tn(prob.astype(BF16), g_head)
        next(o_reduce)
    kv_out[0] = dkv[0, theirs].astype(BF16)
    kv_out[1] = dkv[1, theirs].astype(BF16)
    start(kv_out, kv_in, small_sems, 2, partner)

    @pl.loop(0, SHARDS)
    def _(j):
        hid[j] = dot_nn(att[...], wog[j]).astype(BF16)

    def branch_finish(i, total):
        branch[:, i * ROWS:(i + 1) * ROWS] = total.astype(BF16)

    b_reduce = head_reduce(hid, p_core, p_za, p_zb, 0, branch_finish)
    next(b_reduce)
    arrived(kv_in, small_sems, 2)
    d_keys = jnp.concatenate([dkv[0, mine] + kv_in[0].astype(F32), dkv[0, 2 * HALF:]], 0)
    d_values = jnp.concatenate([dkv[1, mine] + kv_in[1].astype(F32), dkv[1, 2 * HALF:]], 0)
    dproj[:, QC:QC + HEAD_DIM] = unrotate(d_keys).astype(BF16)
    dproj[:, QC + HEAD_DIM:] = d_values.astype(BF16)

    def in_term(j):
        normed[j] = dot_nt(dproj[...], wg[j]).astype(BF16)
        wg[j] = dot_nn(norm_t[j], dproj[...]).astype(BF16)

    def in_finish(rows, total):
        g_wq[rows, :] = total[:, 0:QC]
        g_wk[rows, :] = total[:, QC:QC + HEAD_DIM]
        g_wv[rows, :] = total[:, QC + HEAD_DIM:]

    sent()
    w_reduce = reduce(wg, qa, qb, qc, qd, 2, ROWS, in_finish)
    each(0, in_term)
    next(w_reduce)
    each(1, in_term)
    next(w_reduce)
    each(2, in_term)
    next(w_reduce)
    each(3, in_term)
    next(w_reduce)
    next(b_reduce)
    shares = []

    def norm_finish(i, total):
        shares.append(total)

    each(4, in_term)
    each(5, in_term)
    n_reduce = head_reduce(normed, n_core, n_za, n_zb, 1, norm_finish)
    next(n_reduce)
    next(w_reduce)
    next(b_reduce)
    next(w_reduce)
    next(n_reduce)
    next(b_reduce)
    next(n_reduce)
    next(w_reduce)
    next(n_reduce)

    row_part = jnp.zeros((SLOTS, HEAD_DIM), F32)
    for i in range(2):
        scaled = hslice[i].astype(F32) * inv[...]
        gain_part = jnp.sum(shares[i] * scaled, 0, keepdims=True)
        gx[x, :, i * ROWS:(i + 1) * ROWS] = jnp.broadcast_to(gain_part, (8, ROWS))
        prod = shares[i] * gain[2 * head + i]
        g_hidden[:, i * ROWS:(i + 1) * ROWS] = prod
        prod = prod * scaled
        row_part = row_part + prod[:, :HEAD_DIM] + prod[:, HEAD_DIM:]
    row_sum = jnp.sum(row_part.T, 0, keepdims=True)
    rstat[head] = jnp.broadcast_to(row_sum, (8, SLOTS))
    for k in range(1, 8):
        start(rstat.at[head], rstat.at[head], small_sems, 2 + k, head_others[k - 1])
    for k in range(1, 4):
        start(gx.at[x], gx.at[x], small_sems, 9 + k, along("x", k))
    for k in range(1, 8):
        arrived(rstat.at[lax.rem(head + 8 - k, 8)], small_sems, 2 + k)
    total = jnp.sum(rstat[...], 0)[0:1]
    mean = jnp.broadcast_to(total, (HEAD_DIM, SLOTS)).T * (1.0 / (SHARDS * ROWS))
    for i in range(4):
        cols = slice(i * HEAD_DIM, (i + 1) * HEAD_DIM)
        half = slice((i % 2) * HEAD_DIM, (i % 2 + 1) * HEAD_DIM)
        factor = inv[:, half]
        scaled = hslice[i // 2, :, half].astype(F32) * factor
        g_hidden[:, cols] = factor * (g_hidden[:, cols] - scaled * mean)
    for k in range(1, 4):
        arrived(gx.at[step(x, -k)], small_sems, 9 + k)
    gy[y] = jnp.sum(gx[...], 0)
    for k in range(1, 4):
        start(gy.at[y], gy.at[y], small_sems, 12 + k, along("y", k))
    for k in range(1, 4):
        arrived(gy.at[step(y, -k)], small_sems, 12 + k)
    gh[head] = jnp.sum(gy[...], 0)
    for k in range(1, 8):
        start(gh.at[head], gh.at[head], small_sems, 15 + k, head_others[k - 1])
    next(w_reduce)
    for k in range(1, 8):
        arrived(gh.at[lax.rem(head + 8 - k, 8)], small_sems, 15 + k)
    for i in range(8):
        g_gain[i:i + 1, :] = gh[i, 0:1, :]
    sent()


def shards(hidden, d_out, norm_gain, w_query, w_key, w_value, w_out, prompt_len, resp_len):
    vmem = pl.BlockSpec(memory_space=pltpu.VMEM)
    smem = pl.BlockSpec(memory_space=pltpu.SMEM)
    anywhere = pl.BlockSpec(memory_space=pl.ANY)
    big = (SHARDS, SLOTS, ROWS)
    scratch = [
        pltpu.VMEM((SHARDS, ROWS, WC), BF16),
        pltpu.VMEM((SHARDS, QC, ROWS), BF16),
        pltpu.VMEM(big, BF16),
        pltpu.VMEM(big, BF16),
        pltpu.VMEM(big, BF16),
        pltpu.VMEM((SHARDS, ROWS, SLOTS), BF16),
        pltpu.VMEM((SHARDS, QC, ROWS), BF16),
    ]
    for rows, cols in ((ROWS, WC), (QC, ROWS)):
        scratch += [
            pltpu.VMEM((2, 4, 2, rows // 4, cols), BF16),
            pltpu.VMEM((2, 4, 2, rows // 2, cols), BF16),
            pltpu.VMEM((2, 2, rows // 4, cols), BF16),
            pltpu.VMEM((2, 2, rows // 2, cols), BF16),
        ]
    for _ in range(2):
        scratch += [
            pltpu.VMEM((4, 2, SLOTS, ROWS), BF16),
            pltpu.VMEM((2, 2, SLOTS // 2, ROWS), BF16),
            pltpu.VMEM((2, 2, SLOTS, ROWS), BF16),
        ]
    scratch += [
        pltpu.VMEM((GROUP, SLOTS, KEYS), F32),
        pltpu.VMEM((SLOTS, KEYS), BF16),
        pltpu.VMEM((SLOTS, WC), F32),
        pltpu.VMEM((SLOTS, QC), F32),
        pltpu.VMEM((SLOTS, QC), BF16),
        pltpu.VMEM((QC, SLOTS), BF16),
        pltpu.VMEM((SLOTS, QC), BF16),
        pltpu.VMEM((GROUP, SLOTS, HEAD_DIM), BF16),
        pltpu.VMEM((KEYS, HEAD_DIM), BF16),
        pltpu.VMEM((KEYS, HEAD_DIM), BF16),
        pltpu.VMEM((SLOTS, HEAD_DIM), F32),
        pltpu.VMEM((SLOTS, HEAD_DIM), F32),
        pltpu.VMEM((SLOTS, ROWS), F32),
        pltpu.VMEM((2, SLOTS, ROWS), BF16),
        pltpu.VMEM((SLOTS, WC), BF16),
        pltpu.VMEM((2, KEYS, HEAD_DIM), F32),
        pltpu.VMEM((2, HALF, HEAD_DIM), BF16),
        pltpu.VMEM((2, HALF, HEAD_DIM), BF16),
        pltpu.VMEM((8, 8, SLOTS), F32),
        pltpu.VMEM((4, 8, QC), F32),
        pltpu.VMEM((4, 8, QC), F32),
        pltpu.VMEM((8, 8, QC), F32),
        pltpu.SemaphoreType.DMA((2 * SHARDS,)),
        pltpu.SemaphoreType.DMA((8 * PLANE,)),
        pltpu.SemaphoreType.DMA((8 * PLANE,)),
        pltpu.SemaphoreType.DMA((16,)),
        pltpu.SemaphoreType.DMA((16,)),
        pltpu.SemaphoreType.DMA((24,)),
        pltpu.SemaphoreType.DMA((24,)),
    ]
    outs = pl.pallas_call(
        kernel,
        out_shape=(
            jax.ShapeDtypeStruct((SLOTS, QC), BF16),
            jax.ShapeDtypeStruct((SLOTS, QC), F32),
            jax.ShapeDtypeStruct((ROWS, QC), F32),
            jax.ShapeDtypeStruct((ROWS, HEAD_DIM), F32),
            jax.ShapeDtypeStruct((ROWS, HEAD_DIM), F32),
            jax.ShapeDtypeStruct((QC, ROWS), F32),
            jax.ShapeDtypeStruct((8, QC), F32),
        ),
        in_specs=[anywhere, anywhere, vmem, vmem, vmem, vmem, vmem, smem, smem],
        out_specs=(vmem,) * 7,
        scratch_shapes=scratch,
        compiler_params=pltpu.CompilerParams(
            collective_id=0, has_side_effects=True, vmem_limit_bytes=65011712
        ),
        name="attention_step",
    )(
        hidden[0, 0], d_out[0, 0], norm_gain.reshape(SHARDS, 1, ROWS),
        w_query, w_key, w_value, w_out, prompt_len, resp_len[0],
    )
    branch, g_hidden, g_wq, g_wk, g_wv, g_wo, g_gain = outs
    return (branch[None, None], g_hidden[None, None], g_wq, g_wk, g_wv, g_wo, g_gain.reshape(-1))


def solution(mesh):
    in_specs = (
        P("dp", "pair", None, None),
        P("dp", "pair", None, None),
        P(),
        P(("dp", "pair"), "head"),
        P(("dp", "pair"), "head"),
        P(("dp", "pair"), "head"),
        P("head", ("dp", "pair")),
        P("dp"),
        P("dp", "pair"),
    )
    out_specs = (
        P("dp", "pair", None, "head"),
        P("dp", "pair", None, "head"),
        P(("dp", "pair"), "head"),
        P(("dp", "pair"), "head"),
        P(("dp", "pair"), "head"),
        P("head", ("dp", "pair")),
        P(),
    )
    return jax.shard_map(shards, mesh=mesh, in_specs=in_specs, out_specs=out_specs, check_vma=False)
```

```python
import functools

import jax
import jax.numpy as jnp
from jax import lax
from jax.experimental import pallas as pl
from jax.experimental.pallas import tpu as pltpu
from jax.sharding import PartitionSpec as P

HEAD_DIM = 128
HALF = 256
RESP = 128
SLOTS = HALF + RESP
KEYS = 2 * HALF + RESP
EPS = 1e-05
BASE = 500000.0
SCALE = HEAD_DIM ** (-0.5)
GROUP = 4
QC = GROUP * HEAD_DIM
WC = QC + 2 * HEAD_DIM
SHARDS = 16
ROWS = 256
MESH = pl.DeviceIdType.MESH
F32 = jnp.float32
BF16 = jnp.bfloat16
PLANE = 20


def dot_nn(a, b):
    return lax.dot_general(a, b, (((1,), (0,)), ((), ())), preferred_element_type=F32)


def dot_nt(a, b):
    return lax.dot_general(a, b, (((1,), (1,)), ((), ())), preferred_element_type=F32)


def dot_tn(a, b):
    return lax.dot_general(a, b, (((0,), (0,)), ((), ())), preferred_element_type=F32)


def step(value, offset):
    return lax.rem(value + offset % 4, 4)


GROUPS = (
    (1, lambda i: (2, 2)),
    (4, lambda i: ((1 + 2 * lax.rem(i, 2)) * (1 - i // 2) + 2 * (i // 2), 2 * (1 - i // 2) + (1 + 2 * lax.rem(i, 2)) * (i // 2))),
    (2, lambda i: (2 * i, 2 * (1 - i))),
    (4, lambda i: (1 + 2 * lax.rem(i, 2), 1 + 2 * (i // 2))),
    (4, lambda i: ((1 + 2 * lax.rem(i, 2)) * (1 - i // 2), (1 + 2 * lax.rem(i, 2)) * (i // 2))),
    (1, lambda i: (0, 0)),
)


def kernel(
    hidden, d_out, gain, wq, wk, wv, wo, plen, rlen,
    branch, g_hidden, g_wq, g_wk, g_wv, g_wo, g_gain,
    wg, wog, hid, dout, normed, norm_t, go, gkv,
    oa, ob, oc, od, qa, qb, qc, qd, va, vb, vc, vd,
    p_core, p_za, p_zb, n_core, n_za, n_zb,
    probs, bias, pacc, attf, att, att_t, gatt, qh, kall, vall, cosf, sinf, inv, hslice,
    dproj, dkv, kv_out, kv_in, rstat, gx, gy, gh,
    load_sem, send_sem, recv_sem, core_send, core_recv, small_send, small_recv,
):
    dp, head, pair = lax.axis_index("dp"), lax.axis_index("head"), lax.axis_index("pair")
    x, y = lax.rem(dp, 4), (dp // 4) * 2 + pair
    z, c = head // 2, lax.rem(head, 2)

    def place(px, py):
        return ((py // 2) * 4 + px) * 2 + lax.rem(py, 2)

    def shard(dx, dy):
        return place(lax.rem(x + dx, 4), lax.rem(y + dy, 4))

    def device(px=x, py=y, h=head):
        return ((py // 2) * 4 + px, h, lax.rem(py, 2))

    def along(axis, k):
        if axis == "x":
            return device(px=step(x, k))
        if axis == "y":
            return device(py=step(y, k))
        if axis == "z":
            return device(h=step(z, k) * 2 + c)
        return device(h=z * 2 + (1 - c))

    pending = []

    def sent():
        for copy in pending:
            copy.wait_send()
        pending.clear()

    def start(src, dst, sems, index, target):
        copy = pltpu.make_async_remote_copy(
            src_ref=src, dst_ref=dst, send_sem=sems[0].at[index], recv_sem=sems[1].at[index],
            device_id=target, device_id_type=MESH,
        )
        copy.start()
        pending.append(copy)

    def arrived(dst, sems, index):
        pltpu.make_async_remote_copy(
            src_ref=dst, dst_ref=dst, send_sem=sems[0].at[index], recv_sem=sems[1].at[index],
            device_id=along("x", 1), device_id_type=MESH,
        ).wait_recv()

    plane_sems = (send_sem, recv_sem)
    core_sems = (core_send, core_recv)
    small_sems = (small_send, small_recv)

    def spot(h, a, b):
        return shard(a % 4, b % 4) if h == 0 else shard(b % 4, a % 4)

    def ring(h, primary):
        return "x" if (h == 0) == primary else "y"

    def part(rows, h, s=None):
        if s is None:
            return pl.ds(h * rows // 2, rows // 2)
        return pl.ds(h * rows // 2 + s * rows // 4, rows // 4)

    def gather(buf, t, rows):
        def go_(h, m, a, b, s, primary, k):
            ref = buf.at[spot(h, a, b), part(rows, h, s)]
            start(ref, ref, plane_sems, (t * 2 + h) * PLANE + m, along(ring(h, primary), k))

        def got(h, m, a, b, s=None):
            arrived(buf.at[spot(h, a, b), part(rows, h, s)], plane_sems, (t * 2 + h) * PLANE + m)

        both = (0, 1)
        for h in both:
            go_(h, 0, 0, 0, None, True, 1)
            go_(h, 1, 0, 0, None, True, -1)
        for h in both:
            go_(h, 4, 0, 0, None, False, 1)
            go_(h, 5, 0, 0, None, False, -1)
        yield
        for h in both:
            got(h, 0, -1, 0)
            go_(h, 2, -1, 0, 0, True, 1)
            got(h, 1, 1, 0)
            go_(h, 3, 1, 0, 1, True, -1)
        for h in both:
            for k in (1, 3):
                go_(h, 4 + 4 * k, k, 0, None, False, 1)
                go_(h, 5 + 4 * k, k, 0, None, False, -1)
        yield
        for h in both:
            got(h, 4, 0, -1)
            go_(h, 6, 0, -1, 0, False, 1)
            got(h, 5, 0, 1)
            go_(h, 7, 0, 1, 1, False, -1)
        yield 4
        for h in both:
            got(h, 2, 2, 0, 0)
            got(h, 3, 2, 0, 1)
            go_(h, 12, 2, 0, None, False, 1)
            go_(h, 13, 2, 0, None, False, -1)
        yield
        for k in (1, 3):
            for h in both:
                got(h, 4 + 4 * k, k, -1)
                go_(h, 6 + 4 * k, k, -1, 0, False, 1)
                got(h, 5 + 4 * k, k, 1)
                go_(h, 7 + 4 * k, k, 1, 1, False, -1)
        yield 3
        for h in both:
            got(h, 6, 0, 2, 0)
            got(h, 7, 0, 2, 1)
        yield 2
        for h in both:
            got(h, 12, 2, -1)
            go_(h, 14, 2, -1, 0, False, 1)
            got(h, 13, 2, 1)
            go_(h, 15, 2, 1, 1, False, -1)
        for h in both:
            for k in (1, 3):
                got(h, 6 + 4 * k, k, 2, 0)
                got(h, 7 + 4 * k, k, 2, 1)
        yield 1
        for h in both:
            got(h, 14, 2, 2, 0)
            got(h, 15, 2, 2, 1)
        yield 0

    class Reduce:
        def __init__(self, buf, ra, rb, rc, rd, t, rows, finish, halves=(0, 1)):
            self.buf, self.ra, self.rb, self.rc, self.rd = buf, ra, rb, rc, rd
            self.t, self.rows, self.write, self.halves = t, rows, finish, halves

        def send(self, h, m, a, b, s, dst, primary, k):
            src = self.buf.at[spot(h, a, b), part(self.rows, h, s)]
            start(src, dst, plane_sems, (self.t * 2 + h) * PLANE + m, along(ring(h, primary), k))

        def got(self, h, m, dst):
            arrived(dst, plane_sems, (self.t * 2 + h) * PLANE + m)

        def add(self, h, a, b, s, *terms):
            j, rows = spot(h, a, b), part(self.rows, h, s)
            total = self.buf[j, rows].astype(F32)
            for term in terms:
                total = total + term.astype(F32)
            self.buf[j, rows] = total.astype(BF16)

        def begin(self, *ks):
            for k in ks:
                for h in self.halves:
                    self.send(h, 4 + 4 * k, k, 2, 0, self.ra.at[h, k, 0], False, 1)
                    self.send(h, 5 + 4 * k, k, 2, 1, self.ra.at[h, k, 1], False, -1)

        def middle(self, *ks):
            for k in ks:
                for h in self.halves:
                    for s, way in ((0, 1), (1, -1)):
                        self.got(h, 4 + 4 * k + s, self.ra.at[h, k, s])
                        self.add(h, k, way, s, self.ra[h, k, s])
                        self.send(h, 6 + 4 * k + s, k, way, None, self.rb.at[h, k, s], False, way)

        def close(self, *ks):
            for k in ks:
                for h in self.halves:
                    for s in (0, 1):
                        self.got(h, 6 + 4 * k + s, self.rb.at[h, k, s])
                    self.add(h, k, 0, None, self.rb[h, k, 0], self.rb[h, k, 1])
                    if k == 2:
                        self.send(h, 0, 2, 0, 0, self.rc.at[h, 0], True, 1)
                        self.send(h, 1, 2, 0, 1, self.rc.at[h, 1], True, -1)

        def cross(self):
            for h in self.halves:
                for s, way in ((0, 1), (1, -1)):
                    self.got(h, s, self.rc.at[h, s])
                    self.add(h, way, 0, s, self.rc[h, s])
                    self.send(h, 2 + s, way, 0, None, self.rd.at[h, s], True, way)

        def finish(self):
            for h in self.halves:
                for s in (0, 1):
                    self.got(h, 6 + s, self.rb.at[h, 0, s])
                    self.got(h, 2 + s, self.rd.at[h, s])
                total = self.buf[spot(h, 0, 0), part(self.rows, h)].astype(F32)
                for term in (self.rb[h, 0, 0], self.rb[h, 0, 1], self.rd[h, 0], self.rd[h, 1]):
                    total = total + term.astype(F32)
                self.write(h, total)

    class HeadReduce:
        def __init__(self, buf, r_core, r_za, r_zb, t):
            self.buf, self.r_core, self.r_za, self.r_zb, self.base = buf, r_core, r_za, r_zb, t * 12

        def block(self, k, core):
            return 2 * (step(z, k) * 2 + core)

        def add(self, k, i, rows, term):
            j = self.block(k, c) + i
            self.buf[j, rows] = (self.buf[j, rows].astype(F32) + term.astype(F32)).astype(BF16)

        def swap(self, k):
            start(self.buf.at[pl.ds(self.block(k, 1 - c), 2)], self.r_core.at[k], core_sems, self.base + k, along("core", 1))

        def begin(self):
            arrived(self.r_core.at[2], core_sems, self.base + 2)
            for i in range(2):
                self.add(2, i, pl.ds(0, SLOTS), self.r_core[2, i])
                for s, way in ((0, 1), (1, -1)):
                    rows = pl.ds(s * SLOTS // 2, SLOTS // 2)
                    src = self.buf.at[self.block(2, c) + i, rows]
                    start(src, self.r_za.at[s, i], core_sems, self.base + 4 + 2 * s + i, along("z", way))

        def middle(self):
            for way in (1, -1):
                arrived(self.r_core.at[way % 4], core_sems, self.base + way % 4)
                for i in range(2):
                    self.add(way, i, pl.ds(0, SLOTS), self.r_core[way % 4, i])
            for i in range(2):
                for s, way in ((0, 1), (1, -1)):
                    arrived(self.r_za.at[s, i], core_sems, self.base + 4 + 2 * s + i)
                    self.add(way, i, pl.ds(s * SLOTS // 2, SLOTS // 2), self.r_za[s, i])
                    src = self.buf.at[self.block(way, c) + i]
                    start(src, self.r_zb.at[s, i], core_sems, self.base + 8 + 2 * s + i, along("z", way))

        def total(self, i):
            if i == 0:
                arrived(self.r_core.at[0], core_sems, self.base)
            for s in range(2):
                arrived(self.r_zb.at[s, i], core_sems, self.base + 8 + 2 * s + i)
            own_term = self.buf[2 * head + i].astype(F32) + self.r_core[0, i].astype(F32)
            return own_term + self.r_zb[0, i].astype(F32) + self.r_zb[1, i].astype(F32)

    def each(group, body):
        count, offsets = GROUPS[group]
        if count == 1:
            body(shard(*offsets(0)))
            return

        @pl.loop(0, count)
        def _(i):
            body(shard(*offsets(i)))

    own = shard(0, 0)
    loads = []
    for n, (src, dst) in enumerate(((hidden, hid), (d_out, dout))):
        for j in range(SHARDS):
            copy = pltpu.make_async_copy(src.at[:, pl.ds(j * ROWS, ROWS)], dst.at[j], load_sem.at[n * SHARDS + j])
            copy.start()
            loads.append(copy)
    barrier = pltpu.get_barrier_semaphore()
    others = [along("x", k) for k in (1, 2, 3)] + [along("y", k) for k in (1, 2, 3)]
    head_others = [device(h=lax.rem(head + k, 8)) for k in range(1, 8)]
    for target in others + head_others:
        pl.semaphore_signal(barrier, inc=1, device_id=target, device_id_type=MESH)
    wg[own, :, 0:QC] = wq[...]
    wg[own, :, QC:QC + HEAD_DIM] = wk[...]
    wg[own, :, QC + HEAD_DIM:] = wv[...]
    wog[own] = wo[...]
    pl.semaphore_wait(barrier, 13)

    w_gather = gather(wg, 0, ROWS)
    o_gather = gather(wog, 1, QC)
    next(w_gather)

    for copy in loads[:SHARDS]:
        copy.wait()
    pacc[:, 0:ROWS] = jnp.zeros((SLOTS, ROWS), F32)

    @pl.loop(0, SHARDS)
    def _(j):
        block = hid[j].astype(F32)
        pacc[:, 0:ROWS] += block * block

    mean = jnp.sum(pacc[:, 0:ROWS], -1, keepdims=True) * (1.0 / (SHARDS * ROWS))
    inv[...] = jnp.broadcast_to(lax.rsqrt(mean + EPS), (SLOTS, ROWS))

    def norm_block(j):
        block = (hid[j].astype(F32) * inv[...] * gain[j]).astype(BF16)
        normed[j] = block
        norm_t[j] = block.T

    @pl.loop(0, SHARDS)
    def _(j):
        norm_block(j)
    for i in range(2):
        hslice[i] = hid[2 * head + i]

    prompt_length, resp_length = plen[0], rlen[0]
    slot = lax.broadcasted_iota(jnp.int32, (SLOTS, HEAD_DIM), 0)
    lane = lax.broadcasted_iota(jnp.int32, (8, HEAD_DIM), 1)
    entry = jnp.where(lane < HEAD_DIM // 2, lane, lane - HEAD_DIM // 2)
    freqs = jnp.exp(-(entry.astype(F32) * (2.0 / HEAD_DIM)) * jnp.log(jnp.full((8, HEAD_DIM), BASE, F32)))
    position = jnp.where(slot < HALF, pair * HALF + slot, prompt_length + slot - HALF).astype(F32)
    angle = position * freqs[0:1]
    cosf[...] = jnp.cos(angle)
    sign = jnp.where(lane[0:1] < HEAD_DIM // 2, -1.0, 1.0).astype(F32)
    sinf[...] = jnp.sin(angle) * sign
    s_id = lax.broadcasted_iota(jnp.int32, (SLOTS, KEYS), 0)
    t_id = lax.broadcasted_iota(jnp.int32, (SLOTS, KEYS), 1)
    prompt_key = (t_id < 2 * HALF) & (t_id < prompt_length) & ((s_id >= HALF) | (t_id <= pair * HALF + s_id))
    resp_id = t_id - 2 * HALF
    resp_key = (t_id >= 2 * HALF) & (s_id >= HALF) & (resp_id <= s_id - HALF) & (resp_id < resp_length)
    bias[...] = jnp.where(prompt_key | resp_key, 0.0, -1e30).astype(BF16)

    next(w_gather)
    pacc[...] = dot_nn(normed[own], wg[own])

    def project(j):
        pacc[...] += dot_nn(normed[j], wg[j])

    def pump(gen, times=1, body=None):
        for _ in range(times):
            group = next(gen)
            if group is not None and body is not None:
                each(group, body)

    early = []
    for which in "wwwwwow":
        if which == "w":
            pump(w_gather, 1, project)
        else:
            early.append(next(o_gather))

    def rotate(u):
        return u * cosf[...] + pltpu.roll(u, HEAD_DIM // 2, 1) * sinf[...]

    def unrotate(u):
        return u * cosf[...] - pltpu.roll(u, HEAD_DIM // 2, 1) * sinf[...]

    mine = pl.ds(pl.multiple_of(pair * HALF, HALF), HALF)
    theirs = pl.ds(pl.multiple_of((1 - pair) * HALF, HALF), HALF)
    partner = device(py=(y // 2) * 2 + 1 - pair)
    keys = rotate(pacc[:, QC:QC + HEAD_DIM]).astype(BF16)
    values = pacc[:, QC + HEAD_DIM:].astype(BF16)
    kall[mine] = keys[:HALF]
    kall[2 * HALF:] = keys[HALF:]
    vall[mine] = values[:HALF]
    vall[2 * HALF:] = values[HALF:]
    start(kall.at[mine], kall.at[mine], small_sems, 0, partner)
    start(vall.at[mine], vall.at[mine], small_sems, 1, partner)
    for g in range(GROUP):
        qh[g] = rotate(pacc[:, g * HEAD_DIM:(g + 1) * HEAD_DIM]).astype(BF16)
    for copy in loads[SHARDS:]:
        copy.wait()
    gacc = pacc.at[:, 0:QC]
    gacc[...] = dot_nt(dout[own], wog[own])

    def grad_attend(j):
        gacc[...] += dot_nt(dout[j], wog[j])

    def branch_term(j):
        hid[j] = dot_nn(att[...], wog[j]).astype(BF16)

    def out_term(j):
        go[j] = dot_nn(att_t[...], dout[j]).astype(BF16)

    for group in early:
        if group is not None:
            each(group, grad_attend)
    pump(o_gather, 2, grad_attend)
    arrived(kall.at[theirs], small_sems, 0)
    arrived(vall.at[theirs], small_sems, 1)

    for g in range(GROUP):
        cols = slice(g * HEAD_DIM, (g + 1) * HEAD_DIM)
        scores = dot_nt(qh[g], kall[...]) * SCALE + bias[...].astype(F32)
        expo = jnp.exp(scores - jnp.max(scores, -1, keepdims=True))
        prob = expo / jnp.sum(expo, -1, keepdims=True)
        probs[g] = prob
        out = dot_nn(prob.astype(BF16), vall[...])
        attf[:, cols] = out
        rounded = out.astype(BF16)
        att[:, cols] = rounded
        att_t[cols, :] = rounded.T
        pump(o_gather, (1, 1, 1, 1)[g], grad_attend)

    def out_finish(h, total):
        g_wo[h * ROWS:(h + 1) * ROWS, :] = total

    out = Reduce(go, oa, ob, oc, od, 3, QC, out_finish)
    branch_sum = HeadReduce(hid, p_core, p_za, p_zb, 0)
    each(0, out_term)
    out.begin(2)
    each(1, out_term)
    out.begin(1, 3)
    each(2, out_term)
    out.begin(0)
    each(3, out_term)
    pump(o_gather, 1, grad_attend)
    gatt[...] = gacc[...].astype(BF16)
    gather_sent = list(pending)
    out.middle(2)

    dkv[...] = jnp.zeros_like(dkv)

    def backward(g):
        cols = slice(g * HEAD_DIM, (g + 1) * HEAD_DIM)
        g_head = gatt[:, cols]
        prob = probs[g]
        d_prob = dot_nt(g_head, vall[...])
        delta = jnp.sum(g_head.astype(F32) * attf[:, cols], -1, keepdims=True)
        d_score = (prob * (d_prob - delta) * SCALE).astype(BF16)
        dproj[:, cols] = unrotate(dot_nn(d_score, kall[...])).astype(BF16)
        dkv[0] += dot_tn(d_score, qh[g])
        dkv[1] += dot_tn(prob.astype(BF16), g_head)

    backward(0)
    backward(1)
    each(4, out_term)
    out.middle(1, 3)
    backward(2)
    backward(3)
    kv_out[0] = dkv[0, theirs].astype(BF16)
    kv_out[1] = dkv[1, theirs].astype(BF16)
    start(kv_out, kv_in, small_sems, 2, partner)
    out.middle(0)
    each(5, out_term)

    @pl.loop(0, SHARDS)
    def _(j):
        branch_term(j)

    for k in (2, 1, 3, 0):
        branch_sum.swap(k)

    for copy in gather_sent:
        copy.wait_send()
        pending.remove(copy)

    def query_term(j):
        for h in range(2):
            wog[j, h * ROWS:(h + 1) * ROWS] = dot_nn(norm_t[j], dproj[:, h * ROWS:(h + 1) * ROWS]).astype(BF16)

    def kv_term(j):
        gkv[j] = dot_nn(norm_t[j], dproj[:, QC:]).astype(BF16)

    def query_finish(h, total):
        g_wq[:, h * ROWS:(h + 1) * ROWS] = total

    def kv_finish(h, total):
        rows = slice(h * ROWS // 2, (h + 1) * ROWS // 2)
        g_wk[rows, :] = total[:, :HEAD_DIM]
        g_wv[rows, :] = total[:, HEAD_DIM:]

    query = Reduce(wog, qa, qb, qc, qd, 2, QC, query_finish)
    kv = Reduce(gkv, va, vb, vc, vd, 4, ROWS, kv_finish)
    each(0, query_term)
    query.begin(2)
    each(1, query_term)
    query.begin(1, 3)
    arrived(kv_in, small_sems, 2)
    d_keys = jnp.concatenate([dkv[0, mine] + kv_in[0].astype(F32), dkv[0, 2 * HALF:]], 0)
    d_values = jnp.concatenate([dkv[1, mine] + kv_in[1].astype(F32), dkv[1, 2 * HALF:]], 0)
    dproj[:, QC:QC + HEAD_DIM] = unrotate(d_keys).astype(BF16)
    dproj[:, QC + HEAD_DIM:] = d_values.astype(BF16)

    norm_sum = HeadReduce(normed, n_core, n_za, n_zb, 1)

    def norm_terms(k):
        first = 4 * step(z, k)

        @pl.loop(0, 4)
        def _(i):
            normed[first + i] = dot_nt(dproj[...], wg[first + i]).astype(BF16)
        norm_sum.swap(k)

    norm_terms(2)
    norm_terms(1)
    norm_terms(3)
    norm_sum.begin()
    out.close(2)
    norm_terms(0)
    each(2, query_term)
    query.begin(0)
    query.middle(2)
    each(3, query_term)
    query.middle(1, 3)
    norm_sum.middle()
    branch_sum.begin()
    out.close(1, 3)
    out.cross()
    each(0, kv_term)
    kv.begin(2)
    each(1, kv_term)
    kv.begin(1, 3)
    each(4, query_term)
    query.middle(0)
    each(5, query_term)
    query.close(2)
    each(2, kv_term)
    kv.begin(0)
    each(3, kv_term)
    kv.middle(2)
    branch_sum.middle()
    out.finish()
    shares = [norm_sum.total(i) for i in range(2)]

    row_part = jnp.zeros((SLOTS, HEAD_DIM), F32)
    for i in range(2):
        scaled = hslice[i].astype(F32) * inv[...]
        gain_part = jnp.sum(shares[i] * scaled, 0, keepdims=True)
        gx[x, :, i * ROWS:(i + 1) * ROWS] = jnp.broadcast_to(gain_part, (8, ROWS))
        prod = shares[i] * gain[2 * head + i]
        g_hidden[:, i * ROWS:(i + 1) * ROWS] = prod
        prod = prod * scaled
        row_part = row_part + prod[:, :HEAD_DIM] + prod[:, HEAD_DIM:]
    row_sum = jnp.sum(row_part.T, 0, keepdims=True)
    rstat[head] = jnp.broadcast_to(row_sum, (8, SLOTS))
    for k in range(1, 8):
        start(rstat.at[head], rstat.at[head], small_sems, 2 + k, head_others[k - 1])
    for k in range(1, 4):
        start(gx.at[x], gx.at[x], small_sems, 9 + k, along("x", k))
    kv.middle(1, 3)
    each(4, kv_term)
    kv.middle(0)
    each(5, kv_term)
    for k in range(1, 4):
        arrived(gx.at[step(x, -k)], small_sems, 9 + k)
    gy[y] = jnp.sum(gx[...], 0)
    for k in range(1, 4):
        start(gy.at[y], gy.at[y], small_sems, 12 + k, along("y", k))
    query.close(1, 3)
    query.cross()
    kv.close(2)
    for k in range(1, 8):
        arrived(rstat.at[lax.rem(head + 8 - k, 8)], small_sems, 2 + k)
    total = jnp.sum(rstat[...], 0)[0:1]
    mean = jnp.broadcast_to(total, (HEAD_DIM, SLOTS)).T * (1.0 / (SHARDS * ROWS))
    for i in range(4):
        cols = slice(i * HEAD_DIM, (i + 1) * HEAD_DIM)
        half = slice((i % 2) * HEAD_DIM, (i % 2 + 1) * HEAD_DIM)
        factor = inv[:, half]
        scaled = hslice[i // 2, :, half].astype(F32) * factor
        g_hidden[:, cols] = factor * (g_hidden[:, cols] - scaled * mean)
    for k in range(1, 4):
        arrived(gy.at[step(y, -k)], small_sems, 12 + k)
    gh[head] = jnp.sum(gy[...], 0)
    for k in range(1, 8):
        start(gh.at[head], gh.at[head], small_sems, 15 + k, head_others[k - 1])
    for i in range(2):
        branch[:, i * ROWS:(i + 1) * ROWS] = branch_sum.total(i).astype(BF16)
    kv.close(1, 3)
    kv.cross()
    query.finish()
    kv.finish()
    for k in range(1, 8):
        arrived(gh.at[lax.rem(head + 8 - k, 8)], small_sems, 15 + k)
    for i in range(8):
        g_gain[:, i * QC:(i + 1) * QC] = gh[i, 0:1, :]
    sent()


def place_kernel(*refs):
    count = len(refs) // 3
    sems = refs[-1]
    loads, stores = [], []
    for i in range(count):
        loads.append(pltpu.make_async_copy(refs[i], refs[2 * count + i], sems.at[i]))
        stores.append(pltpu.make_async_copy(refs[2 * count + i], refs[count + i], sems.at[count + i]))
    for load in loads:
        load.start()
    for load, store in zip(loads, stores):
        load.wait()
        store.start()
    for store in stores:
        store.wait()


def shards(hidden, d_out, norm_gain, w_query, w_key, w_value, w_out, prompt_len, resp_len):
    vmem = pl.BlockSpec(memory_space=pltpu.VMEM)
    smem = pl.BlockSpec(memory_space=pltpu.SMEM)
    anywhere = pl.BlockSpec(memory_space=pl.ANY)
    big = (SHARDS, SLOTS, ROWS)
    scratch = [
        pltpu.VMEM((SHARDS, ROWS, WC), BF16),
        pltpu.VMEM((SHARDS, QC, ROWS), BF16),
        pltpu.VMEM(big, BF16),
        pltpu.VMEM(big, BF16),
        pltpu.VMEM(big, BF16),
        pltpu.VMEM((SHARDS, ROWS, SLOTS), BF16),
        pltpu.VMEM((SHARDS, QC, ROWS), BF16),
        pltpu.VMEM((SHARDS, ROWS, ROWS), BF16),
    ]
    for rows, cols in ((QC, ROWS), (QC, ROWS), (ROWS, ROWS)):
        scratch += [
            pltpu.VMEM((2, 4, 2, rows // 4, cols), BF16),
            pltpu.VMEM((2, 4, 2, rows // 2, cols), BF16),
            pltpu.VMEM((2, 2, rows // 4, cols), BF16),
            pltpu.VMEM((2, 2, rows // 2, cols), BF16),
        ]
    for _ in range(2):
        scratch += [
            pltpu.VMEM((4, 2, SLOTS, ROWS), BF16),
            pltpu.VMEM((2, 2, SLOTS // 2, ROWS), BF16),
            pltpu.VMEM((2, 2, SLOTS, ROWS), BF16),
        ]
    scratch += [
        pltpu.VMEM((GROUP, SLOTS, KEYS), F32),
        pltpu.VMEM((SLOTS, KEYS), BF16),
        pltpu.VMEM((SLOTS, WC), F32),
        pltpu.VMEM((SLOTS, QC), F32),
        pltpu.VMEM((SLOTS, QC), BF16),
        pltpu.VMEM((QC, SLOTS), BF16),
        pltpu.VMEM((SLOTS, QC), BF16),
        pltpu.VMEM((GROUP, SLOTS, HEAD_DIM), BF16),
        pltpu.VMEM((KEYS, HEAD_DIM), BF16),
        pltpu.VMEM((KEYS, HEAD_DIM), BF16),
        pltpu.VMEM((SLOTS, HEAD_DIM), F32),
        pltpu.VMEM((SLOTS, HEAD_DIM), F32),
        pltpu.VMEM((SLOTS, ROWS), F32),
        pltpu.VMEM((2, SLOTS, ROWS), BF16),
        pltpu.VMEM((SLOTS, WC), BF16),
        pltpu.VMEM((2, KEYS, HEAD_DIM), F32),
        pltpu.VMEM((2, HALF, HEAD_DIM), BF16),
        pltpu.VMEM((2, HALF, HEAD_DIM), BF16),
        pltpu.VMEM((8, 8, SLOTS), F32),
        pltpu.VMEM((4, 8, QC), F32),
        pltpu.VMEM((4, 8, QC), F32),
        pltpu.VMEM((8, 8, QC), F32),
        pltpu.SemaphoreType.DMA((2 * SHARDS,)),
        pltpu.SemaphoreType.DMA((10 * PLANE,)),
        pltpu.SemaphoreType.DMA((10 * PLANE,)),
        pltpu.SemaphoreType.DMA((24,)),
        pltpu.SemaphoreType.DMA((24,)),
        pltpu.SemaphoreType.DMA((24,)),
        pltpu.SemaphoreType.DMA((24,)),
    ]
    outs = pl.pallas_call(
        kernel,
        out_shape=(
            jax.ShapeDtypeStruct((SLOTS, QC), BF16),
            jax.ShapeDtypeStruct((SLOTS, QC), F32),
            jax.ShapeDtypeStruct((ROWS, QC), F32),
            jax.ShapeDtypeStruct((ROWS, HEAD_DIM), F32),
            jax.ShapeDtypeStruct((ROWS, HEAD_DIM), F32),
            jax.ShapeDtypeStruct((QC, ROWS), F32),
            jax.ShapeDtypeStruct((1, 8 * QC), F32),
        ),
        in_specs=[anywhere, anywhere, vmem, vmem, vmem, vmem, vmem, smem, smem],
        out_specs=(vmem,) * 7,
        scratch_shapes=scratch,
        compiler_params=pltpu.CompilerParams(
            collective_id=0, has_side_effects=True, vmem_limit_bytes=65011712
        ),
        name="attention_step",
    )(
        hidden[0, 0], d_out[0, 0], norm_gain.reshape(SHARDS, 1, ROWS),
        w_query, w_key, w_value, w_out, prompt_len, resp_len[0],
    )
    branch, g_hidden, g_wq, g_wk, g_wv, g_wo, g_gain = pl.pallas_call(
        place_kernel,
        out_shape=tuple(jax.ShapeDtypeStruct(out.shape, out.dtype) for out in outs),
        in_specs=[anywhere] * 7,
        out_specs=(anywhere,) * 7,
        scratch_shapes=[pltpu.VMEM(out.shape, out.dtype) for out in outs] + [pltpu.SemaphoreType.DMA((14,))],
        name="place_results",
    )(*outs)
    return (branch[None, None], g_hidden[None, None], g_wq, g_wk, g_wv, g_wo, g_gain.reshape(-1))


def solution(mesh):
    in_specs = (
        P("dp", "pair", None, None),
        P("dp", "pair", None, None),
        P(),
        P(("dp", "pair"), "head"),
        P(("dp", "pair"), "head"),
        P(("dp", "pair"), "head"),
        P("head", ("dp", "pair")),
        P("dp"),
        P("dp", "pair"),
    )
    out_specs = (
        P("dp", "pair", None, "head"),
        P("dp", "pair", None, "head"),
        P(("dp", "pair"), "head"),
        P(("dp", "pair"), "head"),
        P(("dp", "pair"), "head"),
        P("head", ("dp", "pair")),
        P(),
    )
    return jax.shard_map(shards, mesh=mesh, in_specs=in_specs, out_specs=out_specs, check_vma=False)
```

```python
import functools

import jax
import jax.numpy as jnp
from jax import lax
from jax.experimental import pallas as pl
from jax.experimental.pallas import tpu as pltpu
from jax.sharding import PartitionSpec as P

HEAD_DIM = 128
HALF = 256
RESP = 128
SLOTS = HALF + RESP
KEYS = 2 * HALF + RESP
EPS = 1e-05
BASE = 500000.0
SCALE = HEAD_DIM ** (-0.5)
GROUP = 4
QC = GROUP * HEAD_DIM
WC = QC + 2 * HEAD_DIM
SHARDS = 16
ROWS = 256
MESH = pl.DeviceIdType.MESH
F32 = jnp.float32
BF16 = jnp.bfloat16
PLANE = 20
KV_CUT = 64


def dot_nn(a, b):
    return lax.dot_general(a, b, (((1,), (0,)), ((), ())), preferred_element_type=F32)


def dot_nt(a, b):
    return lax.dot_general(a, b, (((1,), (1,)), ((), ())), preferred_element_type=F32)


def dot_tn(a, b):
    return lax.dot_general(a, b, (((0,), (0,)), ((), ())), preferred_element_type=F32)


def step(value, offset):
    return lax.rem(value + offset % 4, 4)


GROUPS = (
    (1, lambda i: (2, 2)),
    (4, lambda i: ((1 + 2 * lax.rem(i, 2)) * (1 - i // 2) + 2 * (i // 2), 2 * (1 - i // 2) + (1 + 2 * lax.rem(i, 2)) * (i // 2))),
    (2, lambda i: (2 * i, 2 * (1 - i))),
    (4, lambda i: (1 + 2 * lax.rem(i, 2), 1 + 2 * (i // 2))),
    (4, lambda i: ((1 + 2 * lax.rem(i, 2)) * (1 - i // 2), (1 + 2 * lax.rem(i, 2)) * (i // 2))),
    (1, lambda i: (0, 0)),
)


def kernel(
    hidden, d_out, gain, wq, wk, wv, wo, plen, rlen,
    branch_out, g_hidden_out, g_wq_out, g_wk_out, g_wv_out, g_wo_out, g_gain_out,
    branch, g_hidden, g_wq, g_wk, g_wv, g_wo, g_gain,
    wg, wog, hid, dout, normed, norm_t, go, gkv,
    oa, ob, oc, od, qa, qb, qc, qd, va, vb, vc, vd,
    p_core, p_za, p_zb, n_core, n_za, n_zb,
    probs, bias, pacc, gacc, attf, att, att_t, gatt, qh, kall, vall, cosf, sinf, inv, hslice,
    dproj, dkv, kv_out, kv_in, rstat, gx, gy, gh,
    load_sem, store_sem, send_sem, recv_sem, core_send, core_recv, small_send, small_recv,
):
    dp, head, pair = lax.axis_index("dp"), lax.axis_index("head"), lax.axis_index("pair")
    x, y = lax.rem(dp, 4), (dp // 4) * 2 + pair
    z, c = head // 2, lax.rem(head, 2)

    def place(px, py):
        return ((py // 2) * 4 + px) * 2 + lax.rem(py, 2)

    def shard(dx, dy):
        return place(lax.rem(x + dx, 4), lax.rem(y + dy, 4))

    def device(px=x, py=y, h=head):
        return ((py // 2) * 4 + px, h, lax.rem(py, 2))

    def along(axis, k):
        if axis == "x":
            return device(px=step(x, k))
        if axis == "y":
            return device(py=step(y, k))
        if axis == "z":
            return device(h=step(z, k) * 2 + c)
        return device(h=z * 2 + (1 - c))

    pending, gathers = [], []

    def sent():
        for copy in pending:
            copy.wait_send()
        pending.clear()

    def start(src, dst, sems, index, target):
        copy = pltpu.make_async_remote_copy(
            src_ref=src, dst_ref=dst, send_sem=sems[0].at[index], recv_sem=sems[1].at[index],
            device_id=target, device_id_type=MESH,
        )
        copy.start()
        pending.append(copy)
        return copy

    def arrived(dst, sems, index):
        pltpu.make_async_remote_copy(
            src_ref=dst, dst_ref=dst, send_sem=sems[0].at[index], recv_sem=sems[1].at[index],
            device_id=along("x", 1), device_id_type=MESH,
        ).wait_recv()

    plane_sems = (send_sem, recv_sem)
    core_sems = (core_send, core_recv)
    small_sems = (small_send, small_recv)

    def spot(h, a, b):
        return shard(a % 4, b % 4) if h == 0 else shard(b % 4, a % 4)

    def ring(h, primary):
        return "x" if (h == 0) == primary else "y"

    def part(rows, h, s=None, cut=None):
        cut = rows // 2 if cut is None else cut
        first, count = (0, cut) if h == 0 else (cut, rows - cut)
        if s is None:
            return pl.ds(first, count)
        return pl.ds(first + s * count // 2, count // 2)

    def gather(buf, t, rows):
        def go_(h, m, a, b, s, primary, k):
            ref = buf.at[spot(h, a, b), part(rows, h, s)]
            start(ref, ref, plane_sems, (t * 2 + h) * PLANE + m, along(ring(h, primary), k))
            gathers.append(pending.pop())

        def got(h, m, a, b, s=None):
            arrived(buf.at[spot(h, a, b), part(rows, h, s)], plane_sems, (t * 2 + h) * PLANE + m)

        both = (0, 1)
        for h in both:
            go_(h, 0, 0, 0, None, True, 1)
            go_(h, 1, 0, 0, None, True, -1)
        for h in both:
            go_(h, 4, 0, 0, None, False, 1)
            go_(h, 5, 0, 0, None, False, -1)
        yield
        for h in both:
            got(h, 0, -1, 0)
            go_(h, 2, -1, 0, 0, True, 1)
            got(h, 1, 1, 0)
            go_(h, 3, 1, 0, 1, True, -1)
        for h in both:
            for k in (1, 3):
                go_(h, 4 + 4 * k, k, 0, None, False, 1)
                go_(h, 5 + 4 * k, k, 0, None, False, -1)
        yield
        for h in both:
            got(h, 4, 0, -1)
            go_(h, 6, 0, -1, 0, False, 1)
            got(h, 5, 0, 1)
            go_(h, 7, 0, 1, 1, False, -1)
        yield 4
        for h in both:
            got(h, 2, 2, 0, 0)
            got(h, 3, 2, 0, 1)
            go_(h, 12, 2, 0, None, False, 1)
            go_(h, 13, 2, 0, None, False, -1)
        yield
        for k in (1, 3):
            for h in both:
                got(h, 4 + 4 * k, k, -1)
                go_(h, 6 + 4 * k, k, -1, 0, False, 1)
                got(h, 5 + 4 * k, k, 1)
                go_(h, 7 + 4 * k, k, 1, 1, False, -1)
        yield 3
        for h in both:
            got(h, 6, 0, 2, 0)
            got(h, 7, 0, 2, 1)
        yield 2
        for h in both:
            got(h, 12, 2, -1)
            go_(h, 14, 2, -1, 0, False, 1)
            got(h, 13, 2, 1)
            go_(h, 15, 2, 1, 1, False, -1)
        for h in both:
            for k in (1, 3):
                got(h, 6 + 4 * k, k, 2, 0)
                got(h, 7 + 4 * k, k, 2, 1)
        yield 1
        for h in both:
            got(h, 14, 2, 2, 0)
            got(h, 15, 2, 2, 1)
        yield 0

    class Reduce:
        def __init__(self, buf, ra, rb, rc, rd, t, cut, finish):
            self.buf, self.ra, self.rb, self.rc, self.rd = buf, ra, rb, rc, rd
            self.t, self.cut, self.write = t, cut, finish

        def part(self, h, s=None):
            return part(self.buf.shape[1], h, s, self.cut)

        def land(self, ref, h, s, *index):
            return ref.at[h, *index, pl.ds(0, self.part(h, s).size)]

        def send(self, h, m, a, b, s, dst, primary, k):
            src = self.buf.at[spot(h, a, b), self.part(h, s)]
            start(src, dst, plane_sems, (self.t * 2 + h) * PLANE + m, along(ring(h, primary), k))

        def got(self, h, m, dst):
            arrived(dst, plane_sems, (self.t * 2 + h) * PLANE + m)

        def add(self, h, a, b, s, *terms):
            j, rows = spot(h, a, b), self.part(h, s)
            total = self.buf[j, rows].astype(F32)
            for term in terms:
                total = total + term[...].astype(F32)
            self.buf[j, rows] = total.astype(BF16)

        def begin(self, k):
            for h in (0, 1):
                for s, way in ((0, 1), (1, -1)):
                    self.send(h, 4 + 4 * k + s, k, 2, s, self.land(self.ra, h, s, k, s), False, way)

        def middle(self, k):
            for h in (0, 1):
                for s, way in ((0, 1), (1, -1)):
                    term = self.land(self.ra, h, s, k, s)
                    self.got(h, 4 + 4 * k + s, term)
                    self.add(h, k, way, s, term)
                    self.send(h, 6 + 4 * k + s, k, way, None, self.land(self.rb, h, None, k, s), False, way)

        def close(self, k):
            for h in (0, 1):
                terms = [self.land(self.rb, h, None, k, s) for s in (0, 1)]
                for s in (0, 1):
                    self.got(h, 6 + 4 * k + s, terms[s])
                self.add(h, k, 0, None, *terms)
                if k == 2:
                    for s, way in ((0, 1), (1, -1)):
                        self.send(h, s, 2, 0, s, self.land(self.rc, h, s, s), True, way)

        def cross(self):
            for h in (0, 1):
                for s, way in ((0, 1), (1, -1)):
                    term = self.land(self.rc, h, s, s)
                    self.got(h, s, term)
                    self.add(h, way, 0, s, term)
                    self.send(h, 2 + s, way, 0, None, self.land(self.rd, h, None, s), True, way)

        def finish(self):
            for h in (0, 1):
                terms = [self.land(self.rb, h, None, 0, s) for s in (0, 1)]
                terms += [self.land(self.rd, h, None, s) for s in (0, 1)]
                for s in (0, 1):
                    self.got(h, 6 + s, terms[s])
                    self.got(h, 2 + s, terms[2 + s])
                total = self.buf[spot(h, 0, 0), self.part(h)].astype(F32)
                for term in terms:
                    total = total + term[...].astype(F32)
                self.write(h, total)

    class HeadReduce:
        def __init__(self, buf, r_core, r_za, r_zb, t):
            self.buf, self.r_core, self.r_za, self.r_zb, self.base = buf, r_core, r_za, r_zb, t * 12

        def block(self, k, core):
            return 2 * (step(z, k) * 2 + core)

        def add(self, k, i, rows, term):
            j = self.block(k, c) + i
            self.buf[j, rows] = (self.buf[j, rows].astype(F32) + term.astype(F32)).astype(BF16)

        def swap(self, k):
            start(self.buf.at[pl.ds(self.block(k, 1 - c), 2)], self.r_core.at[k], core_sems, self.base + k, along("core", 1))

        def begin(self):
            arrived(self.r_core.at[2], core_sems, self.base + 2)
            for i in range(2):
                self.add(2, i, pl.ds(0, SLOTS), self.r_core[2, i])
                for s, way in ((0, 1), (1, -1)):
                    rows = pl.ds(s * SLOTS // 2, SLOTS // 2)
                    src = self.buf.at[self.block(2, c) + i, rows]
                    start(src, self.r_za.at[s, i], core_sems, self.base + 4 + 2 * s + i, along("z", way))

        def middle(self):
            for way in (1, -1):
                arrived(self.r_core.at[way % 4], core_sems, self.base + way % 4)
                for i in range(2):
                    self.add(way, i, pl.ds(0, SLOTS), self.r_core[way % 4, i])
            for i in range(2):
                for s, way in ((0, 1), (1, -1)):
                    arrived(self.r_za.at[s, i], core_sems, self.base + 4 + 2 * s + i)
                    self.add(way, i, pl.ds(s * SLOTS // 2, SLOTS // 2), self.r_za[s, i])
                    src = self.buf.at[self.block(way, c) + i]
                    start(src, self.r_zb.at[s, i], core_sems, self.base + 8 + 2 * s + i, along("z", way))

        def total(self, i):
            if i == 0:
                arrived(self.r_core.at[0], core_sems, self.base)
            for s in range(2):
                arrived(self.r_zb.at[s, i], core_sems, self.base + 8 + 2 * s + i)
            own_term = self.buf[2 * head + i].astype(F32) + self.r_core[0, i].astype(F32)
            return own_term + self.r_zb[0, i].astype(F32) + self.r_zb[1, i].astype(F32)

    def each(group, body):
        count, offsets = GROUPS[group]
        if count == 1:
            body(shard(*offsets(0)))
            return

        @pl.loop(0, count)
        def _(i):
            body(shard(*offsets(i)))

    own = shard(0, 0)
    barrier = pltpu.get_barrier_semaphore()
    others = [along("x", k) for k in (1, 2, 3)] + [along("y", k) for k in (1, 2, 3)]
    head_others = [device(h=lax.rem(head + k, 8)) for k in range(1, 8)]
    for target in others + head_others:
        pl.semaphore_signal(barrier, inc=1, device_id=target, device_id_type=MESH)
    weights = [
        (wq, wg.at[own, :, pl.ds(0, QC)]),
        (wk, wg.at[own, :, pl.ds(QC, HEAD_DIM)]),
        (wv, wg.at[own, :, pl.ds(QC + HEAD_DIM, HEAD_DIM)]),
        (wo, wog.at[own]),
    ]
    rows = [(hidden.at[:, pl.ds(j * ROWS, ROWS)], hid.at[j]) for j in range(SHARDS)]
    rows += [(d_out.at[:, pl.ds(j * ROWS, ROWS)], dout.at[j]) for j in range(SHARDS)]
    loads = [pltpu.make_async_copy(src, dst, load_sem.at[n]) for n, (src, dst) in enumerate(rows + weights)]
    for copy in loads[2 * SHARDS:]:
        copy.start()
    for copy in loads[2 * SHARDS:]:
        copy.wait()
    pl.semaphore_wait(barrier, 13)

    stores = []

    def store(n, src, dst):
        copy = pltpu.make_async_copy(src, dst, store_sem.at[n])
        copy.start()
        stores.append(copy)

    w_gather = gather(wg, 0, ROWS)
    o_gather = gather(wog, 1, QC)
    next(w_gather)
    for copy in loads[:2 * SHARDS]:
        copy.start()

    def rotate(u):
        return u * cosf[...] + pltpu.roll(u, HEAD_DIM // 2, 1) * sinf[...]

    def unrotate(u):
        return u * cosf[...] - pltpu.roll(u, HEAD_DIM // 2, 1) * sinf[...]

    mine = pl.ds(pl.multiple_of(pair * HALF, HALF), HALF)
    theirs = pl.ds(pl.multiple_of((1 - pair) * HALF, HALF), HALF)
    partner = device(py=(y // 2) * 2 + 1 - pair)

    def project(j):
        pacc[...] += dot_nn(normed[j], wg[j])

    def grad_attend(j):
        gacc[...] += dot_nt(dout[j], wog[j])

    def branch_terms(k):
        first = 4 * step(z, k)

        @pl.loop(0, 4)
        def _(i):
            hid[first + i] = dot_nn(att[...], wog[first + i]).astype(BF16)
        branch_sum.swap(k)

    def norm_terms(k):
        first = 4 * step(z, k)

        @pl.loop(0, 4)
        def _(i):
            normed[first + i] = dot_nt(dproj[...], wg[first + i]).astype(BF16)
        norm_sum.swap(k)

    def out_term(j):
        go[j] = dot_nn(att_t[...], dout[j]).astype(BF16)

    def query_term(j):
        for h in range(2):
            wog[j, h * ROWS:(h + 1) * ROWS] = dot_nn(norm_t[j], dproj[:, h * ROWS:(h + 1) * ROWS]).astype(BF16)

    def kv_term(j):
        gkv[j] = dot_nn(norm_t[j], dproj[:, QC:]).astype(BF16)

    def out_finish(h, total):
        g_wo[h * ROWS:(h + 1) * ROWS, :] = total
        if h == 1:
            store(5, g_wo, g_wo_out)

    def query_finish(h, total):
        g_wq[:, h * ROWS:(h + 1) * ROWS] = total
        if h == 1:
            store(2, g_wq, g_wq_out)

    def kv_finish(h, total):
        rows = slice(0, KV_CUT) if h == 0 else slice(KV_CUT, ROWS)
        g_wk[rows, :] = total[:, :HEAD_DIM]
        g_wv[rows, :] = total[:, HEAD_DIM:]
        if h == 1:
            store(3, g_wk, g_wk_out)
            store(4, g_wv, g_wv_out)

    out = Reduce(go, oa, ob, oc, od, 3, ROWS, out_finish)
    query = Reduce(wog, qa, qb, qc, qd, 2, ROWS, query_finish)
    kv = Reduce(gkv, va, vb, vc, vd, 4, KV_CUT, kv_finish)
    branch_sum = HeadReduce(hid, p_core, p_za, p_zb, 0)
    norm_sum = HeadReduce(normed, n_core, n_za, n_zb, 1)

    def forward(g):
        cols = slice(g * HEAD_DIM, (g + 1) * HEAD_DIM)
        scores = dot_nt(qh[g], kall[...]) * SCALE + bias[...].astype(F32)
        expo = jnp.exp(scores - jnp.max(scores, -1, keepdims=True))
        prob = expo / jnp.sum(expo, -1, keepdims=True)
        probs[g] = prob
        attended = dot_nn(prob.astype(BF16), vall[...])
        attf[:, cols] = attended
        rounded = attended.astype(BF16)
        att[:, cols] = rounded
        att_t[cols, :] = rounded.T

    def backward(g):
        cols = slice(g * HEAD_DIM, (g + 1) * HEAD_DIM)
        g_head = gatt[:, cols]
        prob = probs[g]
        d_prob = dot_nt(g_head, vall[...])
        delta = jnp.sum(g_head.astype(F32) * attf[:, cols], -1, keepdims=True)
        d_score = (prob * (d_prob - delta) * SCALE).astype(BF16)
        dproj[:, cols] = unrotate(dot_nn(d_score, kall[...])).astype(BF16)
        dkv[0] += dot_tn(d_score, qh[g])
        dkv[1] += dot_tn(prob.astype(BF16), g_head)

    for copy in loads[:SHARDS]:
        copy.wait()
    pacc[:, 0:ROWS] = jnp.zeros((SLOTS, ROWS), F32)

    @pl.loop(0, SHARDS)
    def _(j):
        block = hid[j].astype(F32)
        pacc[:, 0:ROWS] += block * block

    mean = jnp.sum(pacc[:, 0:ROWS], -1, keepdims=True) * (1.0 / (SHARDS * ROWS))
    inv[...] = jnp.broadcast_to(lax.rsqrt(mean + EPS), (SLOTS, ROWS))

    def norm_block(j):
        block = (hid[j].astype(F32) * inv[...] * gain[j]).astype(BF16)
        normed[j] = block
        norm_t[j] = block.T

    @pl.loop(0, SHARDS)
    def _(j):
        norm_block(j)
    for i in range(2):
        hslice[i] = hid[2 * head + i]
    next(w_gather)
    pacc[...] = dot_nn(normed[own], wg[own])
    next(w_gather)
    next(w_gather)
    next(w_gather)
    each(3, project)
    next(w_gather)
    each(2, project)
    each(4, project)
    prompt_length, resp_length = plen[0], rlen[0]
    slot = lax.broadcasted_iota(jnp.int32, (SLOTS, HEAD_DIM), 0)
    lane = lax.broadcasted_iota(jnp.int32, (8, HEAD_DIM), 1)
    entry = jnp.where(lane < HEAD_DIM // 2, lane, lane - HEAD_DIM // 2)
    freqs = jnp.exp(-(entry.astype(F32) * (2.0 / HEAD_DIM)) * jnp.log(jnp.full((8, HEAD_DIM), BASE, F32)))
    position = jnp.where(slot < HALF, pair * HALF + slot, prompt_length + slot - HALF).astype(F32)
    angle = position * freqs[0:1]
    cosf[...] = jnp.cos(angle)
    sign = jnp.where(lane[0:1] < HEAD_DIM // 2, -1.0, 1.0).astype(F32)
    sinf[...] = jnp.sin(angle) * sign
    s_id = lax.broadcasted_iota(jnp.int32, (SLOTS, KEYS), 0)
    t_id = lax.broadcasted_iota(jnp.int32, (SLOTS, KEYS), 1)
    prompt_key = (t_id < 2 * HALF) & (t_id < prompt_length) & ((s_id >= HALF) | (t_id <= pair * HALF + s_id))
    resp_id = t_id - 2 * HALF
    resp_key = (t_id >= 2 * HALF) & (s_id >= HALF) & (resp_id <= s_id - HALF) & (resp_id < resp_length)
    bias[...] = jnp.where(prompt_key | resp_key, 0.0, -1e30).astype(BF16)
    next(w_gather)
    next(o_gather)
    next(w_gather)
    each(1, project)
    each(0, project)
    keys = rotate(pacc[:, QC:QC + HEAD_DIM]).astype(BF16)
    values = pacc[:, QC + HEAD_DIM:].astype(BF16)
    kall[mine] = keys[:HALF]
    kall[2 * HALF:] = keys[HALF:]
    vall[mine] = values[:HALF]
    vall[2 * HALF:] = values[HALF:]
    start(kall.at[mine], kall.at[mine], small_sems, 0, partner)
    start(vall.at[mine], vall.at[mine], small_sems, 1, partner)
    next(o_gather)
    for copy in loads[SHARDS:2 * SHARDS]:
        copy.wait()
    gacc[...] = dot_nt(dout[own], wog[own])
    for g in range(GROUP):
        qh[g] = rotate(pacc[:, g * HEAD_DIM:(g + 1) * HEAD_DIM]).astype(BF16)
    next(o_gather)
    each(4, grad_attend)
    arrived(kall.at[theirs], small_sems, 0)
    arrived(vall.at[theirs], small_sems, 1)
    forward(0)
    forward(1)
    forward(2)
    next(o_gather)
    forward(3)
    each(2, out_term)
    each(1, out_term)
    next(o_gather)
    each(0, out_term)
    out.begin(3)
    out.begin(0)
    each(3, grad_attend)
    next(o_gather)
    each(2, grad_attend)
    each(4, out_term)
    each(3, out_term)
    each(5, out_term)
    next(o_gather)
    out.begin(2)
    each(1, grad_attend)
    out.begin(1)
    out.middle(3)
    out.middle(0)
    next(o_gather)
    each(0, grad_attend)
    gatt[...] = gacc[...].astype(BF16)
    dkv[...] = jnp.zeros_like(dkv)
    backward(0)
    backward(1)
    backward(2)
    backward(3)
    kv_out[0] = dkv[0, theirs].astype(BF16)
    kv_out[1] = dkv[1, theirs].astype(BF16)
    start(kv_out, kv_in, small_sems, 2, partner)
    out.middle(2)
    branch_terms(2)
    out.middle(1)
    branch_terms(3)
    branch_terms(1)
    for copy in gathers:
        copy.wait_send()
    branch_terms(0)
    each(0, query_term)
    query.begin(2)
    each(1, query_term)
    query.begin(1)
    arrived(kv_in, small_sems, 2)
    d_keys = jnp.concatenate([dkv[0, mine] + kv_in[0].astype(F32), dkv[0, 2 * HALF:]], 0)
    d_values = jnp.concatenate([dkv[1, mine] + kv_in[1].astype(F32), dkv[1, 2 * HALF:]], 0)
    dproj[:, QC:QC + HEAD_DIM] = unrotate(d_keys).astype(BF16)
    dproj[:, QC + HEAD_DIM:] = d_values.astype(BF16)
    query.begin(3)
    each(0, kv_term)
    kv.begin(2)
    each(1, kv_term)
    norm_terms(2)
    branch_sum.begin()
    out.close(2)
    kv.begin(3)
    norm_terms(1)
    kv.begin(1)
    each(2, query_term)
    each(3, kv_term)
    query.middle(2)
    norm_terms(3)
    query.begin(0)
    out.close(1)
    norm_sum.begin()
    each(3, query_term)
    query.middle(1)
    out.close(3)
    kv.middle(2)
    each(2, kv_term)
    each(5, query_term)
    norm_sum.middle()
    kv.begin(0)
    query.close(2)
    query.middle(3)
    kv.middle(1)
    norm_terms(0)
    kv.close(2)
    out.cross()
    each(4, query_term)
    each(4, kv_term)
    branch_sum.middle()
    kv.middle(3)
    shares = [norm_sum.total(i) for i in range(2)]
    row_part = jnp.zeros((SLOTS, HEAD_DIM), F32)
    for i in range(2):
        scaled = hslice[i].astype(F32) * inv[...]
        gain_part = jnp.sum(shares[i] * scaled, 0, keepdims=True)
        gx[x, :, i * ROWS:(i + 1) * ROWS] = jnp.broadcast_to(gain_part, (8, ROWS))
        prod = shares[i] * gain[2 * head + i]
        g_hidden[:, i * ROWS:(i + 1) * ROWS] = prod
        prod = prod * scaled
        row_part = row_part + prod[:, :HEAD_DIM] + prod[:, HEAD_DIM:]
    row_sum = jnp.sum(row_part.T, 0, keepdims=True)
    rstat[head] = jnp.broadcast_to(row_sum, (8, SLOTS))
    for k in range(1, 8):
        start(rstat.at[head], rstat.at[head], small_sems, 2 + k, head_others[k - 1])
    for k in range(1, 4):
        start(gx.at[x], gx.at[x], small_sems, 9 + k, along("x", k))
    query.middle(0)
    kv.close(1)
    query.close(1)
    kv.close(3)
    for k in range(1, 4):
        arrived(gx.at[step(x, -k)], small_sems, 9 + k)
    gy[y] = jnp.sum(gx[...], 0)
    for k in range(1, 4):
        start(gy.at[y], gy.at[y], small_sems, 12 + k, along("y", k))
    kv.cross()
    query.close(3)
    query.cross()
    kv.middle(0)
    for i in range(2):
        branch[:, i * ROWS:(i + 1) * ROWS] = branch_sum.total(i).astype(BF16)
    store(0, branch, branch_out)
    for k in range(1, 4):
        arrived(gy.at[step(y, -k)], small_sems, 12 + k)
    gh[head] = jnp.sum(gy[...], 0)
    for k in range(1, 8):
        start(gh.at[head], gh.at[head], small_sems, 15 + k, head_others[k - 1])
    each(5, kv_term)
    out.finish()
    for k in range(1, 8):
        arrived(rstat.at[lax.rem(head + 8 - k, 8)], small_sems, 2 + k)
    total = jnp.sum(rstat[...], 0)[0:1]
    mean = jnp.broadcast_to(total, (HEAD_DIM, SLOTS)).T * (1.0 / (SHARDS * ROWS))
    for i in range(4):
        cols = slice(i * HEAD_DIM, (i + 1) * HEAD_DIM)
        half = slice((i % 2) * HEAD_DIM, (i % 2 + 1) * HEAD_DIM)
        factor = inv[:, half]
        scaled = hslice[i // 2, :, half].astype(F32) * factor
        g_hidden[:, cols] = factor * (g_hidden[:, cols] - scaled * mean)
    store(1, g_hidden, g_hidden_out)
    query.finish()
    for k in range(1, 8):
        arrived(gh.at[lax.rem(head + 8 - k, 8)], small_sems, 15 + k)
    for i in range(8):
        g_gain[:, i * QC:(i + 1) * QC] = gh[i, 0:1, :]
    store(6, g_gain, g_gain_out)
    kv.finish()
    sent()
    for copy in stores:
        copy.wait()


def place_kernel(*refs):
    count = len(refs) // 3
    sems = refs[-1]
    loads, stores = [], []
    for i in range(count):
        loads.append(pltpu.make_async_copy(refs[i], refs[2 * count + i], sems.at[i]))
        stores.append(pltpu.make_async_copy(refs[2 * count + i], refs[count + i], sems.at[count + i]))
    for load in loads:
        load.start()
    for load, store in zip(loads, stores):
        load.wait()
        store.start()
    for store in stores:
        store.wait()


def shards(hidden, d_out, norm_gain, w_query, w_key, w_value, w_out, prompt_len, resp_len):
    vmem = pl.BlockSpec(memory_space=pltpu.VMEM)
    smem = pl.BlockSpec(memory_space=pltpu.SMEM)
    anywhere = pl.BlockSpec(memory_space=pl.ANY)
    big = (SHARDS, SLOTS, ROWS)
    results = (
        jax.ShapeDtypeStruct((SLOTS, QC), BF16),
        jax.ShapeDtypeStruct((SLOTS, QC), F32),
        jax.ShapeDtypeStruct((ROWS, QC), F32),
        jax.ShapeDtypeStruct((ROWS, HEAD_DIM), F32),
        jax.ShapeDtypeStruct((ROWS, HEAD_DIM), F32),
        jax.ShapeDtypeStruct((QC, ROWS), F32),
        jax.ShapeDtypeStruct((1, 8 * QC), F32),
    )
    scratch = [pltpu.VMEM(out.shape, out.dtype) for out in results]
    scratch += [
        pltpu.VMEM((SHARDS, ROWS, WC), BF16),
        pltpu.VMEM((SHARDS, QC, ROWS), BF16),
        pltpu.VMEM(big, BF16),
        pltpu.VMEM(big, BF16),
        pltpu.VMEM(big, BF16),
        pltpu.VMEM((SHARDS, ROWS, SLOTS), BF16),
        pltpu.VMEM((SHARDS, QC, ROWS), BF16),
        pltpu.VMEM((SHARDS, ROWS, ROWS), BF16),
    ]
    for rows, cols, cut in ((QC, ROWS, QC // 2), (QC, ROWS, QC // 2), (ROWS, ROWS, KV_CUT)):
        most = max(cut, rows - cut)
        scratch += [
            pltpu.VMEM((2, 4, 2, most // 2, cols), BF16),
            pltpu.VMEM((2, 4, 2, most, cols), BF16),
            pltpu.VMEM((2, 2, most // 2, cols), BF16),
            pltpu.VMEM((2, 2, most, cols), BF16),
        ]
    for _ in range(2):
        scratch += [
            pltpu.VMEM((4, 2, SLOTS, ROWS), BF16),
            pltpu.VMEM((2, 2, SLOTS // 2, ROWS), BF16),
            pltpu.VMEM((2, 2, SLOTS, ROWS), BF16),
        ]
    scratch += [
        pltpu.VMEM((GROUP, SLOTS, KEYS), F32),
        pltpu.VMEM((SLOTS, KEYS), BF16),
        pltpu.VMEM((SLOTS, WC), F32),
        pltpu.VMEM((SLOTS, QC), F32),
        pltpu.VMEM((SLOTS, QC), F32),
        pltpu.VMEM((SLOTS, QC), BF16),
        pltpu.VMEM((QC, SLOTS), BF16),
        pltpu.VMEM((SLOTS, QC), BF16),
        pltpu.VMEM((GROUP, SLOTS, HEAD_DIM), BF16),
        pltpu.VMEM((KEYS, HEAD_DIM), BF16),
        pltpu.VMEM((KEYS, HEAD_DIM), BF16),
        pltpu.VMEM((SLOTS, HEAD_DIM), F32),
        pltpu.VMEM((SLOTS, HEAD_DIM), F32),
        pltpu.VMEM((SLOTS, ROWS), F32),
        pltpu.VMEM((2, SLOTS, ROWS), BF16),
        pltpu.VMEM((SLOTS, WC), BF16),
        pltpu.VMEM((2, KEYS, HEAD_DIM), F32),
        pltpu.VMEM((2, HALF, HEAD_DIM), BF16),
        pltpu.VMEM((2, HALF, HEAD_DIM), BF16),
        pltpu.VMEM((8, 8, SLOTS), F32),
        pltpu.VMEM((4, 8, QC), F32),
        pltpu.VMEM((4, 8, QC), F32),
        pltpu.VMEM((8, 8, QC), F32),
        pltpu.SemaphoreType.DMA((2 * SHARDS + 4,)),
        pltpu.SemaphoreType.DMA((7,)),
        pltpu.SemaphoreType.DMA((10 * PLANE,)),
        pltpu.SemaphoreType.DMA((10 * PLANE,)),
        pltpu.SemaphoreType.DMA((24,)),
        pltpu.SemaphoreType.DMA((24,)),
        pltpu.SemaphoreType.DMA((24,)),
        pltpu.SemaphoreType.DMA((24,)),
    ]
    outs = pl.pallas_call(
        kernel,
        out_shape=results,
        in_specs=[anywhere, anywhere, vmem, anywhere, anywhere, anywhere, anywhere, smem, smem],
        out_specs=(anywhere,) * 7,
        scratch_shapes=scratch,
        compiler_params=pltpu.CompilerParams(
            collective_id=0, has_side_effects=True, vmem_limit_bytes=65011712
        ),
        name="attention_step",
    )(
        hidden[0, 0], d_out[0, 0], norm_gain.reshape(SHARDS, 1, ROWS),
        w_query, w_key, w_value, w_out, prompt_len, resp_len[0],
    )
    branch, g_hidden, g_wq, g_wk, g_wv, g_wo, g_gain = pl.pallas_call(
        place_kernel,
        out_shape=tuple(jax.ShapeDtypeStruct(out.shape, out.dtype) for out in outs),
        in_specs=[anywhere] * 7,
        out_specs=(anywhere,) * 7,
        scratch_shapes=[pltpu.VMEM(out.shape, out.dtype) for out in outs] + [pltpu.SemaphoreType.DMA((14,))],
        name="place_results",
    )(*outs)
    return (branch[None, None], g_hidden[None, None], g_wq, g_wk, g_wv, g_wo, g_gain.reshape(-1))


def solution(mesh):
    in_specs = (
        P("dp", "pair", None, None),
        P("dp", "pair", None, None),
        P(),
        P(("dp", "pair"), "head"),
        P(("dp", "pair"), "head"),
        P(("dp", "pair"), "head"),
        P("head", ("dp", "pair")),
        P("dp"),
        P("dp", "pair"),
    )
    out_specs = (
        P("dp", "pair", None, "head"),
        P("dp", "pair", None, "head"),
        P(("dp", "pair"), "head"),
        P(("dp", "pair"), "head"),
        P(("dp", "pair"), "head"),
        P("head", ("dp", "pair")),
        P(),
    )
    return jax.shard_map(shards, mesh=mesh, in_specs=in_specs, out_specs=out_specs, check_vma=False)
```

```python
import functools

import jax
import jax.numpy as jnp
from jax import lax
from jax.experimental import pallas as pl
from jax.experimental.pallas import tpu as pltpu
from jax.sharding import PartitionSpec as P

HEAD_DIM = 128
HALF = 256
RESP = 128
SLOTS = HALF + RESP
KEYS = 2 * HALF + RESP
EPS = 1e-05
BASE = 500000.0
SCALE = HEAD_DIM ** (-0.5)
GROUP = 4
QC = GROUP * HEAD_DIM
WC = QC + 2 * HEAD_DIM
SHARDS = 16
ROWS = 256
MESH = pl.DeviceIdType.MESH
F32 = jnp.float32
BF16 = jnp.bfloat16
PLANE = 20
WINDOW = 48
KV_CUT = 64


def dot_nn(a, b):
    return lax.dot_general(a, b, (((1,), (0,)), ((), ())), preferred_element_type=F32)


def dot_nt(a, b):
    return lax.dot_general(a, b, (((1,), (1,)), ((), ())), preferred_element_type=F32)


def dot_tn(a, b):
    return lax.dot_general(a, b, (((0,), (0,)), ((), ())), preferred_element_type=F32)


GROUPS = (
    (1, lambda i: (2, 2)),
    (4, lambda i: ((1 + 2 * lax.rem(i, 2)) * (1 - lax.div(i, 2)) + 2 * (lax.div(i, 2)), 2 * (1 - lax.div(i, 2)) + (1 + 2 * lax.rem(i, 2)) * (lax.div(i, 2)))),
    (2, lambda i: (2 * i, 2 * (1 - i))),
    (4, lambda i: (1 + 2 * lax.rem(i, 2), 1 + 2 * (lax.div(i, 2)))),
    (4, lambda i: ((1 + 2 * lax.rem(i, 2)) * (1 - lax.div(i, 2)), (1 + 2 * lax.rem(i, 2)) * (lax.div(i, 2)))),
    (1, lambda i: (0, 0)),
)


def kernel(
    hidden, d_out, gain_in, wq, wk, wv, wo, plen, rlen,
    branch_out, g_hidden_out, g_wq_out, g_wk_out, g_wv_out, g_wo_out, g_gain_out,
    branch, g_hidden, g_wq, g_wk, g_wv, g_wo, g_gain, gain,
    wg, wog, hid, dout, normed, norm_t, go, gkv,
    oa, ob, oc, od, qa, qb, qc, qd, va, vb, vc, vd,
    p_core, p_za, p_zb, n_core, n_za, n_zb,
    probs, bias, pacc, gacc, attf, att, att_t, gatt, qh, kall, vall, cosf, sinf, inv, hslice,
    dproj, dkv, kv_out, kv_in, rstat, gx, gy, gh,
    load_sem, store_sem, send_sem, recv_sem, core_send, core_recv, small_send, small_recv,
):
    dp, head, pair = lax.axis_index("dp"), lax.axis_index("head"), lax.axis_index("pair")
    x, y = lax.rem(dp, 4), lax.div(dp, 4) * 2 + pair
    z, c = lax.div(head, 2), lax.rem(head, 2)

    xs = [lax.rem(x + k, 4) for k in range(4)]
    ys = [lax.rem(y + k, 4) for k in range(4)]
    zs = [lax.rem(z + k, 4) for k in range(4)]
    highs = [lax.div(v, 2) * 8 for v in ys]
    lows = [lax.rem(v, 2) for v in ys]
    shards_at = {(a, b): highs[b] + xs[a] * 2 + lows[b] for a in range(4) for b in range(4)}

    def place(px, py):
        return (lax.div(py, 2) * 4 + px) * 2 + lax.rem(py, 2)

    def shard(dx, dy):
        if isinstance(dx, int) and isinstance(dy, int):
            return shards_at[dx % 4, dy % 4]
        return place(lax.rem(x + dx, 4), lax.rem(y + dy, 4))

    blocks = {(k, same): zs[k] * 4 + 2 * (c if same else 1 - c) for k in range(4) for same in (0, 1)}
    dps = [lax.div(v, 2) * 4 + x for v in ys]
    targets = {("x", k): (dps[0] - x + xs[k], head, pair) for k in range(1, 4)}
    targets.update({("y", k): (dps[k], head, lows[k]) for k in range(1, 4)})
    targets.update({("z", k): (dp, zs[k] * 2 + c, pair) for k in range(1, 4)})
    targets["core", 1] = (dp, z * 2 + (1 - c), pair)
    heads = [lax.rem(head + k, 8) for k in range(8)]

    def along(axis, k):
        return targets[axis, k % 4]

    pending, gathers = [], []

    def sent():
        for copy in pending:
            copy.wait_send()
        pending.clear()

    def start(src, dst, sems, index, target):
        copy = pltpu.make_async_remote_copy(
            src_ref=src, dst_ref=dst, send_sem=sems[0].at[index], recv_sem=sems[1].at[index],
            device_id=target, device_id_type=MESH,
        )
        copy.start()
        pending.append(copy)
        if len(pending) > WINDOW:
            pending.pop(0).wait_send()
        return copy

    def arrived(dst, sems, index):
        pltpu.make_async_remote_copy(
            src_ref=dst, dst_ref=dst, send_sem=sems[0].at[index], recv_sem=sems[1].at[index],
            device_id=along("x", 1), device_id_type=MESH,
        ).wait_recv()

    plane_sems = (send_sem, recv_sem)
    core_sems = (core_send, core_recv)
    small_sems = (small_send, small_recv)

    def spot(h, a, b):
        return shard(a % 4, b % 4) if h == 0 else shard(b % 4, a % 4)

    def ring(h, primary):
        return "x" if (h == 0) == primary else "y"

    def part(rows, h, s=None, cut=None):
        cut = rows // 2 if cut is None else cut
        first, count = (0, cut) if h == 0 else (cut, rows - cut)
        if s is None:
            return pl.ds(first, count)
        return pl.ds(first + s * count // 2, count // 2)

    def gather(buf, t, rows):
        def go_(h, m, a, b, s, primary, k):
            ref = buf.at[spot(h, a, b), part(rows, h, s)]
            start(ref, ref, plane_sems, (t * 2 + h) * PLANE + m, along(ring(h, primary), k))
            gathers.append(pending.pop())
            if len(gathers) > WINDOW:
                gathers.pop(0).wait_send()

        def got(h, m, a, b, s=None):
            arrived(buf.at[spot(h, a, b), part(rows, h, s)], plane_sems, (t * 2 + h) * PLANE + m)

        both = (0, 1)
        for h in both:
            go_(h, 0, 0, 0, None, True, 1)
            go_(h, 1, 0, 0, None, True, -1)
        for h in both:
            go_(h, 4, 0, 0, None, False, 1)
            go_(h, 5, 0, 0, None, False, -1)
        yield
        for h in both:
            got(h, 0, -1, 0)
            go_(h, 2, -1, 0, 0, True, 1)
            got(h, 1, 1, 0)
            go_(h, 3, 1, 0, 1, True, -1)
        for h in both:
            for k in (1, 3):
                go_(h, 4 + 4 * k, k, 0, None, False, 1)
                go_(h, 5 + 4 * k, k, 0, None, False, -1)
        yield
        for h in both:
            got(h, 4, 0, -1)
            go_(h, 6, 0, -1, 0, False, 1)
            got(h, 5, 0, 1)
            go_(h, 7, 0, 1, 1, False, -1)
        yield 4
        for h in both:
            got(h, 2, 2, 0, 0)
            got(h, 3, 2, 0, 1)
            go_(h, 12, 2, 0, None, False, 1)
            go_(h, 13, 2, 0, None, False, -1)
        yield
        for k in (1, 3):
            for h in both:
                got(h, 4 + 4 * k, k, -1)
                go_(h, 6 + 4 * k, k, -1, 0, False, 1)
                got(h, 5 + 4 * k, k, 1)
                go_(h, 7 + 4 * k, k, 1, 1, False, -1)
        yield 3
        for h in both:
            got(h, 6, 0, 2, 0)
            got(h, 7, 0, 2, 1)
        yield 2
        for h in both:
            got(h, 12, 2, -1)
            go_(h, 14, 2, -1, 0, False, 1)
            got(h, 13, 2, 1)
            go_(h, 15, 2, 1, 1, False, -1)
        for h in both:
            for k in (1, 3):
                got(h, 6 + 4 * k, k, 2, 0)
                got(h, 7 + 4 * k, k, 2, 1)
        yield 1
        for h in both:
            got(h, 14, 2, 2, 0)
            got(h, 15, 2, 2, 1)
        yield 0

    class Reduce:
        def __init__(self, buf, ra, rb, rc, rd, t, cut, finish):
            self.buf, self.ra, self.rb, self.rc, self.rd = buf, ra, rb, rc, rd
            self.t, self.cut, self.write = t, cut, finish

        def part(self, h, s=None):
            return part(self.buf.shape[1], h, s, self.cut)

        def land(self, ref, h, s, *index):
            return ref.at[h, *index, pl.ds(0, self.part(h, s).size)]

        def send(self, h, m, a, b, s, dst, primary, k):
            src = self.buf.at[spot(h, a, b), self.part(h, s)]
            start(src, dst, plane_sems, (self.t * 2 + h) * PLANE + m, along(ring(h, primary), k))

        def got(self, h, m, dst):
            arrived(dst, plane_sems, (self.t * 2 + h) * PLANE + m)

        def add(self, h, a, b, s, *terms):
            j, rows = spot(h, a, b), self.part(h, s)
            total = self.buf[j, rows].astype(F32)
            for term in terms:
                total = total + term[...].astype(F32)
            self.buf[j, rows] = total.astype(BF16)

        def begin(self, k, h):
            for s, way in ((0, 1), (1, -1)):
                self.send(h, 4 + 4 * k + s, k, 2, s, self.land(self.ra, h, s, k, s), False, way)

        def middle(self, k, h):
            for s, way in ((0, 1), (1, -1)):
                term = self.land(self.ra, h, s, k, s)
                self.got(h, 4 + 4 * k + s, term)
                self.add(h, k, way, s, term)
                self.send(h, 6 + 4 * k + s, k, way, None, self.land(self.rb, h, None, k, s), False, way)

        def close(self, k, h):
            terms = [self.land(self.rb, h, None, k, s) for s in (0, 1)]
            for s in (0, 1):
                self.got(h, 6 + 4 * k + s, terms[s])
            self.add(h, k, 0, None, *terms)
            if k == 2:
                for s, way in ((0, 1), (1, -1)):
                    self.send(h, s, 2, 0, s, self.land(self.rc, h, s, s), True, way)

        def cross(self, h):
            for s, way in ((0, 1), (1, -1)):
                term = self.land(self.rc, h, s, s)
                self.got(h, s, term)
                self.add(h, way, 0, s, term)
                self.send(h, 2 + s, way, 0, None, self.land(self.rd, h, None, s), True, way)

        def finish(self, h):
            terms = [self.land(self.rb, h, None, 0, s) for s in (0, 1)]
            terms += [self.land(self.rd, h, None, s) for s in (0, 1)]
            for s in (0, 1):
                self.got(h, 6 + s, terms[s])
                self.got(h, 2 + s, terms[2 + s])
            total = self.buf[spot(h, 0, 0), self.part(h)].astype(F32)
            for term in terms:
                total = total + term[...].astype(F32)
            self.write(h, total)

    class HeadReduce:
        def __init__(self, buf, r_core, r_za, r_zb, t):
            self.buf, self.r_core, self.r_za, self.r_zb, self.base = buf, r_core, r_za, r_zb, t * 12

        def block(self, k, same):
            return blocks[k % 4, same]

        def add(self, k, i, rows, term):
            j = self.block(k, 1) + i
            self.buf[j, rows] = (self.buf[j, rows].astype(F32) + term.astype(F32)).astype(BF16)

        def swap(self, k):
            start(self.buf.at[pl.ds(self.block(k, 0), 2)], self.r_core.at[k], core_sems, self.base + k, along("core", 1))

        def begin(self, i):
            if i == 0:
                arrived(self.r_core.at[2], core_sems, self.base + 2)
            self.add(2, i, pl.ds(0, SLOTS), self.r_core[2, i])
            for s, way in ((0, 1), (1, -1)):
                rows = pl.ds(s * SLOTS // 2, SLOTS // 2)
                src = self.buf.at[self.block(2, 1) + i, rows]
                start(src, self.r_za.at[s, i], core_sems, self.base + 4 + 2 * s + i, along("z", way))

        def middle(self, i):
            for s, way in ((0, 1), (1, -1)):
                if i == 0:
                    arrived(self.r_core.at[way % 4], core_sems, self.base + way % 4)
                self.add(way, i, pl.ds(0, SLOTS), self.r_core[way % 4, i])
                arrived(self.r_za.at[s, i], core_sems, self.base + 4 + 2 * s + i)
                self.add(way, i, pl.ds(s * SLOTS // 2, SLOTS // 2), self.r_za[s, i])
                src = self.buf.at[self.block(way, 1) + i]
                start(src, self.r_zb.at[s, i], core_sems, self.base + 8 + 2 * s + i, along("z", way))

        def total(self, i):
            if i == 0:
                arrived(self.r_core.at[0], core_sems, self.base)
            for s in range(2):
                arrived(self.r_zb.at[s, i], core_sems, self.base + 8 + 2 * s + i)
            own_term = self.buf[2 * head + i].astype(F32) + self.r_core[0, i].astype(F32)
            return own_term + self.r_zb[0, i].astype(F32) + self.r_zb[1, i].astype(F32)

    def each(group, body):
        count, offsets = GROUPS[group]
        if count == 1:
            body(shard(*offsets(0)))
            return

        @pl.loop(0, count)
        def _(i):
            body(shard(*offsets(i)))

    own = shard(0, 0)
    barrier = pltpu.get_barrier_semaphore()
    others = [along("x", k) for k in (1, 2, 3)] + [along("y", k) for k in (1, 2, 3)]
    head_others = [(dp, heads[k], pair) for k in range(1, 8)]
    for target in others + head_others:
        pl.semaphore_signal(barrier, inc=1, device_id=target, device_id_type=MESH)
    weights = [
        (wq, wg.at[own, :, pl.ds(0, QC)]),
        (wk, wg.at[own, :, pl.ds(QC, HEAD_DIM)]),
        (wv, wg.at[own, :, pl.ds(QC + HEAD_DIM, HEAD_DIM)]),
        (wo, wog.at[own]),
        (gain_in, gain),
    ]
    rows = [(hidden.at[:, pl.ds(j * ROWS, ROWS)], hid.at[j]) for j in range(SHARDS)]
    rows += [(d_out.at[:, pl.ds(j * ROWS, ROWS)], dout.at[j]) for j in range(SHARDS)]
    loads = [pltpu.make_async_copy(src, dst, load_sem.at[n]) for n, (src, dst) in enumerate(rows + weights)]
    for copy in loads[2 * SHARDS:]:
        copy.start()
    for copy in loads[2 * SHARDS:]:
        copy.wait()
    pl.semaphore_wait(barrier, 13)

    stores = []

    def store(n, src, dst):
        copy = pltpu.make_async_copy(src, dst, store_sem.at[n])
        copy.start()
        stores.append(copy)

    w_gather = gather(wg, 0, ROWS)
    o_gather = gather(wog, 1, QC)
    next(w_gather)
    for copy in loads[:2 * SHARDS]:
        copy.start()

    def rotate(u):
        return u * cosf[...] + pltpu.roll(u, HEAD_DIM // 2, 1) * sinf[...]

    def unrotate(u):
        return u * cosf[...] - pltpu.roll(u, HEAD_DIM // 2, 1) * sinf[...]

    mine = pl.ds(pl.multiple_of(pair * HALF, HALF), HALF)
    theirs = pl.ds(pl.multiple_of((1 - pair) * HALF, HALF), HALF)
    partner = (dp, head, 1 - pair)

    def project(j):
        pacc[...] += dot_nn(normed[j], wg[j])

    def grad_attend(j):
        gacc[...] += dot_nt(dout[j], wog[j])

    def branch_term(j):
        hid[j] = dot_nn(att[...], wog[j]).astype(BF16)

    def norm_terms(k):
        first = 4 * zs[k]

        @pl.loop(0, 4)
        def _(i):
            normed[first + i] = dot_nt(dproj[...], wg[first + i]).astype(BF16)
        norm_sum.swap(k)

    def out_term(h):
        rows = slice(h * ROWS, (h + 1) * ROWS)

        def term(j):
            go[j, rows] = dot_nn(att_t[rows], dout[j]).astype(BF16)

        return term

    def query_term(h):
        cols = slice(h * ROWS, (h + 1) * ROWS)

        def term(j):
            wog[j, cols] = dot_nn(norm_t[j], dproj[:, cols]).astype(BF16)

        return term

    def kv_term(j):
        gkv[j] = dot_nn(norm_t[j], dproj[:, QC:]).astype(BF16)

    def out_finish(h, total):
        g_wo[h * ROWS:(h + 1) * ROWS, :] = total
        store(5 + 2 * h, g_wo.at[pl.ds(h * ROWS, ROWS)], g_wo_out.at[pl.ds(h * ROWS, ROWS)])

    def query_finish(h, total):
        g_wq[:, h * ROWS:(h + 1) * ROWS] = total
        store(2 + 6 * h, g_wq.at[:, pl.ds(h * ROWS, ROWS)], g_wq_out.at[:, pl.ds(h * ROWS, ROWS)])

    def kv_finish(h, total):
        rows = slice(0, KV_CUT) if h == 0 else slice(KV_CUT, ROWS)
        g_wk[rows, :] = total[:, :HEAD_DIM]
        g_wv[rows, :] = total[:, HEAD_DIM:]
        piece = pl.ds(0, KV_CUT) if h == 0 else pl.ds(KV_CUT, ROWS - KV_CUT)
        store(3 + 6 * h, g_wk.at[piece], g_wk_out.at[piece])
        store(4 + 6 * h, g_wv.at[piece], g_wv_out.at[piece])

    out = Reduce(go, oa, ob, oc, od, 3, ROWS, out_finish)
    query = Reduce(wog, qa, qb, qc, qd, 2, ROWS, query_finish)
    kv = Reduce(gkv, va, vb, vc, vd, 4, KV_CUT, kv_finish)
    branch_sum = HeadReduce(hid, p_core, p_za, p_zb, 0)
    norm_sum = HeadReduce(normed, n_core, n_za, n_zb, 1)

    def forward(g):
        cols = slice(g * HEAD_DIM, (g + 1) * HEAD_DIM)
        scores = dot_nt(qh[g], kall[...]) * SCALE + bias[...].astype(F32)
        expo = jnp.exp(scores - jnp.max(scores, -1, keepdims=True))
        prob = expo / jnp.sum(expo, -1, keepdims=True)
        probs[g] = prob
        attended = dot_nn(prob.astype(BF16), vall[...])
        attf[:, cols] = attended
        rounded = attended.astype(BF16)
        att[:, cols] = rounded
        att_t[cols, :] = rounded.T

    def backward(g):
        cols = slice(g * HEAD_DIM, (g + 1) * HEAD_DIM)
        g_head = gatt[:, cols]
        prob = probs[g]
        d_prob = dot_nt(g_head, vall[...])
        delta = jnp.sum(g_head.astype(F32) * attf[:, cols], -1, keepdims=True)
        d_score = (prob * (d_prob - delta) * SCALE).astype(BF16)
        dproj[:, cols] = unrotate(dot_nn(d_score, kall[...])).astype(BF16)
        dkv[0] += dot_tn(d_score, qh[g])
        dkv[1] += dot_tn(prob.astype(BF16), g_head)

    for copy in loads[:SHARDS]:
        copy.wait()
    pacc[:, 0:ROWS] = jnp.zeros((SLOTS, ROWS), F32)

    @pl.loop(0, SHARDS)
    def _(j):
        block = hid[j].astype(F32)
        pacc[:, 0:ROWS] += block * block

    mean = jnp.sum(pacc[:, 0:ROWS], -1, keepdims=True) * (1.0 / (SHARDS * ROWS))
    inv[...] = jnp.broadcast_to(lax.rsqrt(mean + EPS), (SLOTS, ROWS))

    def norm_block(j):
        block = (hid[j].astype(F32) * inv[...] * gain[j]).astype(BF16)
        normed[j] = block
        norm_t[j] = block.T

    @pl.loop(0, SHARDS)
    def _(j):
        norm_block(j)
    for i in range(2):
        hslice[i] = hid[2 * head + i]
    pacc[...] = dot_nn(normed[own], wg[own])
    for copy in loads[SHARDS:2 * SHARDS]:
        copy.wait()
    gacc[...] = dot_nt(dout[own], wog[own])
    next(w_gather)
    next(w_gather)
    next(w_gather)
    next(w_gather)
    each(4, project)
    next(w_gather)
    each(3, project)
    prompt_length, resp_length = plen[0], rlen[0]
    slot = lax.broadcasted_iota(jnp.int32, (SLOTS, HEAD_DIM), 0)
    lane = lax.broadcasted_iota(jnp.int32, (8, HEAD_DIM), 1)
    entry = jnp.where(lane < HEAD_DIM // 2, lane, lane - HEAD_DIM // 2)
    freqs = jnp.exp(-(entry.astype(F32) * (2.0 / HEAD_DIM)) * jnp.log(jnp.full((8, HEAD_DIM), BASE, F32)))
    position = jnp.where(slot < HALF, pair * HALF + slot, prompt_length + slot - HALF).astype(F32)
    angle = position * freqs[0:1]
    cosf[...] = jnp.cos(angle)
    sign = jnp.where(lane[0:1] < HEAD_DIM // 2, -1.0, 1.0).astype(F32)
    sinf[...] = jnp.sin(angle) * sign
    s_id = lax.broadcasted_iota(jnp.int32, (SLOTS, KEYS), 0)
    t_id = lax.broadcasted_iota(jnp.int32, (SLOTS, KEYS), 1)
    prompt_key = (t_id < 2 * HALF) & (t_id < prompt_length) & ((s_id >= HALF) | (t_id <= pair * HALF + s_id))
    resp_id = t_id - 2 * HALF
    resp_key = (t_id >= 2 * HALF) & (s_id >= HALF) & (resp_id <= s_id - HALF) & (resp_id < resp_length)
    bias[...] = jnp.where(prompt_key | resp_key, 0.0, -1e30).astype(BF16)
    next(w_gather)
    next(o_gather)
    each(2, project)
    next(w_gather)
    each(0, project)
    each(1, project)
    keys = rotate(pacc[:, QC:QC + HEAD_DIM]).astype(BF16)
    values = pacc[:, QC + HEAD_DIM:].astype(BF16)
    kall[mine] = keys[:HALF]
    kall[2 * HALF:] = keys[HALF:]
    vall[mine] = values[:HALF]
    vall[2 * HALF:] = values[HALF:]
    start(kall.at[mine], kall.at[mine], small_sems, 0, partner)
    start(vall.at[mine], vall.at[mine], small_sems, 1, partner)
    next(o_gather)
    for g in range(GROUP):
        qh[g] = rotate(pacc[:, g * HEAD_DIM:(g + 1) * HEAD_DIM]).astype(BF16)
    next(o_gather)
    each(4, grad_attend)
    arrived(kall.at[theirs], small_sems, 0)
    arrived(vall.at[theirs], small_sems, 1)
    forward(0)
    forward(1)
    forward(2)
    forward(3)
    each(0, out_term(1))
    each(5, branch_term)
    next(o_gather)
    each(1, out_term(1))
    each(4, branch_term)
    out.begin(1, 1)
    each(0, out_term(0))
    out.begin(2, 1)
    next(o_gather)
    each(3, grad_attend)
    each(2, out_term(1))
    out.begin(3, 1)
    next(o_gather)
    each(2, branch_term)
    each(2, out_term(0))
    each(2, grad_attend)
    each(3, out_term(1))
    out.begin(2, 0)
    each(3, branch_term)
    next(o_gather)
    out.middle(1, 1)
    each(1, grad_attend)
    out.begin(0, 0)
    each(1, out_term(0))
    next(o_gather)
    out.begin(3, 0)
    out.middle(2, 1)
    out.middle(2, 0)
    each(0, grad_attend)
    gatt[...] = gacc[...].astype(BF16)
    out.middle(3, 1)
    for copy in gathers:
        copy.wait_send()
    each(1, branch_term)
    each(0, branch_term)
    dkv[...] = jnp.zeros_like(dkv)
    backward(0)
    out.begin(1, 0)
    backward(1)
    backward(2)
    branch_sum.swap(3)
    out.begin(0, 1)
    branch_sum.swap(2)
    branch_sum.swap(1)
    branch_sum.swap(0)
    each(0, query_term(0))
    query.begin(2, 0)
    backward(3)
    each(1, query_term(1))
    kv_out[0] = dkv[0, theirs].astype(BF16)
    kv_out[1] = dkv[1, theirs].astype(BF16)
    start(kv_out, kv_in, small_sems, 2, partner)
    each(1, query_term(0))
    out.close(2, 0)
    query.begin(3, 1)
    out.close(2, 1)
    each(4, out_term(1))
    each(0, query_term(1))
    query.begin(2, 1)
    each(2, query_term(1))
    query.middle(2, 0)
    each(3, out_term(0))
    out.middle(0, 1)
    out.middle(1, 0)
    query.begin(3, 0)
    each(2, query_term(0))
    arrived(kv_in, small_sems, 2)
    d_keys = jnp.concatenate([dkv[0, mine] + kv_in[0].astype(F32), dkv[0, 2 * HALF:]], 0)
    d_values = jnp.concatenate([dkv[1, mine] + kv_in[1].astype(F32), dkv[1, 2 * HALF:]], 0)
    dproj[:, QC:QC + HEAD_DIM] = unrotate(d_keys).astype(BF16)
    dproj[:, QC + HEAD_DIM:] = d_values.astype(BF16)
    query.begin(1, 1)
    each(1, kv_term)
    kv.begin(3, 0)
    each(5, query_term(1))
    each(3, query_term(0))
    norm_terms(2)
    query.begin(0, 1)
    query.middle(2, 1)
    norm_terms(1)
    kv.begin(1, 1)
    query.begin(1, 0)
    each(0, kv_term)
    query.begin(0, 0)
    out.close(3, 1)
    kv.begin(2, 1)
    kv.begin(1, 0)
    norm_sum.begin(0)
    norm_terms(3)
    each(3, query_term(1))
    norm_sum.begin(1)
    kv.begin(2, 0)
    out.middle(3, 0)
    query.middle(1, 1)
    each(4, query_term(0))
    norm_sum.middle(0)
    kv.begin(3, 1)
    query.middle(1, 0)
    query.middle(3, 1)
    branch_sum.begin(0)
    each(3, kv_term)
    each(2, kv_term)
    query.middle(3, 0)
    query.close(2, 0)
    kv.middle(1, 0)
    norm_terms(0)
    norm_sum.middle(1)
    each(5, kv_term)
    out.close(1, 1)
    each(4, out_term(0))
    kv.middle(3, 1)
    kv.middle(3, 0)
    out.close(1, 0)
    kv.middle(2, 0)
    branch_sum.begin(1)
    kv.begin(0, 1)
    each(5, query_term(0))
    out.cross(1)
    kv.middle(2, 1)
    out.middle(0, 0)
    each(4, query_term(1))
    out.close(3, 0)
    kv.begin(0, 0)
    each(5, out_term(1))
    branch_sum.middle(0)
    kv.close(2, 0)
    out.cross(0)
    query.middle(0, 0)
    query.close(2, 1)
    kv.middle(1, 1)
    shares = [norm_sum.total(i) for i in range(2)]
    row_part = jnp.zeros((SLOTS, HEAD_DIM), F32)
    for i in range(2):
        scaled = hslice[i].astype(F32) * inv[...]
        gain_part = jnp.sum(shares[i] * scaled, 0, keepdims=True)
        gx[x, :, i * ROWS:(i + 1) * ROWS] = jnp.broadcast_to(gain_part, (8, ROWS))
        prod = shares[i] * gain[2 * head + i]
        g_hidden[:, i * ROWS:(i + 1) * ROWS] = prod
        prod = prod * scaled
        row_part = row_part + prod[:, :HEAD_DIM] + prod[:, HEAD_DIM:]
    row_sum = jnp.sum(row_part.T, 0, keepdims=True)
    rstat[head] = jnp.broadcast_to(row_sum, (8, SLOTS))
    for k in range(1, 8):
        start(rstat.at[head], rstat.at[head], small_sems, 2 + k, head_others[k - 1])
    for k in range(1, 4):
        start(gx.at[x], gx.at[x], small_sems, 9 + k, along("x", k))
    query.close(3, 0)
    query.middle(0, 1)
    query.close(3, 1)
    kv.close(2, 1)
    query.close(1, 0)
    each(4, kv_term)
    query.cross(0)
    query.close(1, 1)
    kv.close(1, 0)
    branch_sum.middle(1)
    kv.middle(0, 0)
    kv.close(3, 0)
    kv.cross(0)
    for k in range(1, 4):
        arrived(gx.at[xs[-k % 4]], small_sems, 9 + k)
    gy[y] = jnp.sum(gx[...], 0)
    for k in range(1, 4):
        start(gy.at[y], gy.at[y], small_sems, 12 + k, along("y", k))
    kv.close(3, 1)
    kv.close(1, 1)
    query.cross(1)
    for k in range(1, 8):
        arrived(rstat.at[heads[8 - k]], small_sems, 2 + k)
    total = jnp.sum(rstat[...], 0)[0:1]
    mean = jnp.broadcast_to(total, (HEAD_DIM, SLOTS)).T * (1.0 / (SHARDS * ROWS))
    for i in range(4):
        cols = slice(i * HEAD_DIM, (i + 1) * HEAD_DIM)
        half = slice((i % 2) * HEAD_DIM, (i % 2 + 1) * HEAD_DIM)
        factor = inv[:, half]
        scaled = hslice[lax.div(i, 2), :, half].astype(F32) * factor
        g_hidden[:, cols] = factor * (g_hidden[:, cols] - scaled * mean)
    store(1, g_hidden, g_hidden_out)
    kv.cross(1)
    kv.middle(0, 1)
    for k in range(1, 4):
        arrived(gy.at[ys[-k % 4]], small_sems, 12 + k)
    gh[head] = jnp.sum(gy[...], 0)
    for k in range(1, 8):
        start(gh.at[head], gh.at[head], small_sems, 15 + k, head_others[k - 1])
    each(5, out_term(0))
    out.finish(0)
    out.finish(1)
    for i in range(2):
        branch[:, i * ROWS:(i + 1) * ROWS] = branch_sum.total(i).astype(BF16)
    store(0, branch, branch_out)
    kv.finish(0)
    query.finish(0)
    query.finish(1)
    for k in range(1, 8):
        arrived(gh.at[heads[8 - k]], small_sems, 15 + k)
    for i in range(8):
        g_gain[:, i * QC:(i + 1) * QC] = gh[i, 0:1, :]
    store(6, g_gain, g_gain_out)
    while len(pending) > 24:
        pending.pop(0).wait_send()
    kv.finish(1)
    sent()
    for copy in stores:
        copy.wait()


def place_kernel(*refs):
    count = len(refs) // 3
    sems = refs[-1]
    loads, stores = [], []
    for i in range(count):
        loads.append(pltpu.make_async_copy(refs[i], refs[2 * count + i], sems.at[i]))
        stores.append(pltpu.make_async_copy(refs[2 * count + i], refs[count + i], sems.at[count + i]))
    for load in loads:
        load.start()
    for load, store in zip(loads, stores):
        load.wait()
        store.start()
    for store in stores:
        store.wait()


def shards(hidden, d_out, norm_gain, w_query, w_key, w_value, w_out, prompt_len, resp_len):
    smem = pl.BlockSpec(memory_space=pltpu.SMEM)
    anywhere = pl.BlockSpec(memory_space=pl.ANY)
    big = (SHARDS, SLOTS, ROWS)
    results = (
        jax.ShapeDtypeStruct((SLOTS, QC), BF16),
        jax.ShapeDtypeStruct((SLOTS, QC), F32),
        jax.ShapeDtypeStruct((ROWS, QC), F32),
        jax.ShapeDtypeStruct((ROWS, HEAD_DIM), F32),
        jax.ShapeDtypeStruct((ROWS, HEAD_DIM), F32),
        jax.ShapeDtypeStruct((QC, ROWS), F32),
        jax.ShapeDtypeStruct((1, 8 * QC), F32),
    )
    scratch = [pltpu.VMEM(out.shape, out.dtype) for out in results]
    scratch += [
        pltpu.VMEM((SHARDS, 1, ROWS), F32),
        pltpu.VMEM((SHARDS, ROWS, WC), BF16),
        pltpu.VMEM((SHARDS, QC, ROWS), BF16),
        pltpu.VMEM(big, BF16),
        pltpu.VMEM(big, BF16),
        pltpu.VMEM(big, BF16),
        pltpu.VMEM((SHARDS, ROWS, SLOTS), BF16),
        pltpu.VMEM((SHARDS, QC, ROWS), BF16),
        pltpu.VMEM((SHARDS, ROWS, ROWS), BF16),
    ]
    for rows, cols, cut in ((QC, ROWS, QC // 2), (QC, ROWS, QC // 2), (ROWS, ROWS, KV_CUT)):
        most = max(cut, rows - cut)
        scratch += [
            pltpu.VMEM((2, 4, 2, most // 2, cols), BF16),
            pltpu.VMEM((2, 4, 2, most, cols), BF16),
            pltpu.VMEM((2, 2, most // 2, cols), BF16),
            pltpu.VMEM((2, 2, most, cols), BF16),
        ]
    for _ in range(2):
        scratch += [
            pltpu.VMEM((4, 2, SLOTS, ROWS), BF16),
            pltpu.VMEM((2, 2, SLOTS // 2, ROWS), BF16),
            pltpu.VMEM((2, 2, SLOTS, ROWS), BF16),
        ]
    scratch += [
        pltpu.VMEM((GROUP, SLOTS, KEYS), F32),
        pltpu.VMEM((SLOTS, KEYS), BF16),
        pltpu.VMEM((SLOTS, WC), F32),
        pltpu.VMEM((SLOTS, QC), F32),
        pltpu.VMEM((SLOTS, QC), F32),
        pltpu.VMEM((SLOTS, QC), BF16),
        pltpu.VMEM((QC, SLOTS), BF16),
        pltpu.VMEM((SLOTS, QC), BF16),
        pltpu.VMEM((GROUP, SLOTS, HEAD_DIM), BF16),
        pltpu.VMEM((KEYS, HEAD_DIM), BF16),
        pltpu.VMEM((KEYS, HEAD_DIM), BF16),
        pltpu.VMEM((SLOTS, HEAD_DIM), F32),
        pltpu.VMEM((SLOTS, HEAD_DIM), F32),
        pltpu.VMEM((SLOTS, ROWS), F32),
        pltpu.VMEM((2, SLOTS, ROWS), BF16),
        pltpu.VMEM((SLOTS, WC), BF16),
        pltpu.VMEM((2, KEYS, HEAD_DIM), F32),
        pltpu.VMEM((2, HALF, HEAD_DIM), BF16),
        pltpu.VMEM((2, HALF, HEAD_DIM), BF16),
        pltpu.VMEM((8, 8, SLOTS), F32),
        pltpu.VMEM((4, 8, QC), F32),
        pltpu.VMEM((4, 8, QC), F32),
        pltpu.VMEM((8, 8, QC), F32),
        pltpu.SemaphoreType.DMA((2 * SHARDS + 5,)),
        pltpu.SemaphoreType.DMA((12,)),
        pltpu.SemaphoreType.DMA((10 * PLANE,)),
        pltpu.SemaphoreType.DMA((10 * PLANE,)),
        pltpu.SemaphoreType.DMA((24,)),
        pltpu.SemaphoreType.DMA((24,)),
        pltpu.SemaphoreType.DMA((24,)),
        pltpu.SemaphoreType.DMA((24,)),
    ]
    outs = pl.pallas_call(
        kernel,
        out_shape=results,
        in_specs=[anywhere, anywhere, anywhere, anywhere, anywhere, anywhere, anywhere, smem, smem],
        out_specs=(anywhere,) * 7,
        scratch_shapes=scratch,
        compiler_params=pltpu.CompilerParams(
            collective_id=0, has_side_effects=True, vmem_limit_bytes=65011712
        ),
        name="attention_step",
    )(
        hidden[0, 0], d_out[0, 0], norm_gain.reshape(SHARDS, 1, ROWS),
        w_query, w_key, w_value, w_out, prompt_len, resp_len[0],
    )
    branch, g_hidden, g_wq, g_wk, g_wv, g_wo, g_gain = pl.pallas_call(
        place_kernel,
        out_shape=tuple(jax.ShapeDtypeStruct(out.shape, out.dtype) for out in outs),
        in_specs=[anywhere] * 7,
        out_specs=(anywhere,) * 7,
        scratch_shapes=[pltpu.VMEM(out.shape, out.dtype) for out in outs] + [pltpu.SemaphoreType.DMA((14,))],
        name="place_results",
    )(*outs)
    return (branch[None, None], g_hidden[None, None], g_wq, g_wk, g_wv, g_wo, g_gain.reshape(-1))


def solution(mesh):
    in_specs = (
        P("dp", "pair", None, None),
        P("dp", "pair", None, None),
        P(),
        P(("dp", "pair"), "head"),
        P(("dp", "pair"), "head"),
        P(("dp", "pair"), "head"),
        P("head", ("dp", "pair")),
        P("dp"),
        P("dp", "pair"),
    )
    out_specs = (
        P("dp", "pair", None, "head"),
        P("dp", "pair", None, "head"),
        P(("dp", "pair"), "head"),
        P(("dp", "pair"), "head"),
        P(("dp", "pair"), "head"),
        P("head", ("dp", "pair")),
        P(),
    )
    return jax.shard_map(shards, mesh=mesh, in_specs=in_specs, out_specs=out_specs, check_vma=False)
```

```python
import functools

import jax
import jax.numpy as jnp
from jax import lax
from jax.experimental import pallas as pl
from jax.experimental.pallas import tpu as pltpu
from jax.sharding import PartitionSpec as P

HEAD_DIM = 128
HALF = 256
RESP = 128
SLOTS = HALF + RESP
KEYS = 2 * HALF + RESP
EPS = 1e-05
BASE = 500000.0
SCALE = HEAD_DIM ** (-0.5)
GROUP = 4
QC = GROUP * HEAD_DIM
WC = QC + 2 * HEAD_DIM
SHARDS = 16
ROWS = 256
MESH = pl.DeviceIdType.MESH
F32 = jnp.float32
BF16 = jnp.bfloat16
SLOT = 10
KV_CUT = 64


def dot_nn(a, b):
    return lax.dot_general(a, b, (((1,), (0,)), ((), ())), preferred_element_type=F32)


def dot_nt(a, b):
    return lax.dot_general(a, b, (((1,), (1,)), ((), ())), preferred_element_type=F32)


def dot_tn(a, b):
    return lax.dot_general(a, b, (((0,), (0,)), ((), ())), preferred_element_type=F32)


GROUPS = (
    (1, lambda i: (2, 2)),
    (4, lambda i: ((1 + 2 * lax.rem(i, 2)) * (1 - lax.div(i, 2)) + 2 * (lax.div(i, 2)), 2 * (1 - lax.div(i, 2)) + (1 + 2 * lax.rem(i, 2)) * (lax.div(i, 2)))),
    (2, lambda i: (2 * i, 2 * (1 - i))),
    (4, lambda i: (1 + 2 * lax.rem(i, 2), 1 + 2 * (lax.div(i, 2)))),
    (4, lambda i: ((1 + 2 * lax.rem(i, 2)) * (1 - lax.div(i, 2)), (1 + 2 * lax.rem(i, 2)) * (lax.div(i, 2)))),
    (1, lambda i: (0, 0)),
)


def kernel(
    hidden, d_out, gain_in, wq, wk, wv, wo, plen, rlen,
    branch_out, g_hidden_out, g_wq_out, g_wk_out, g_wv_out, g_wo_out, g_gain_out,
    branch, g_hidden, g_wq, g_wk, g_wv, g_wo, g_gain, gain,
    wg, wog, hid, dout, normed, norm_t, go, gkv,
    oa, ob, oc, od, qa, qb, qc, qd, va, vb, vc, vd,
    p_core, p_za, p_zb, n_core, n_za, n_zb,
    probs, bias, pacc, gacc, attf, att, att_t, gatt, qh, kall, vall, cosf, sinf, inv, hslice,
    dproj, dkv, kv_out, kv_in, rstat, gx, gy, gh,
    load_sem, store_sem, send_sem, recv_sem, core_send, core_recv, small_send, small_recv,
):
    dp, head, pair = lax.axis_index("dp"), lax.axis_index("head"), lax.axis_index("pair")
    x, y = lax.rem(dp, 4), lax.div(dp, 4) * 2 + pair
    z, c = lax.div(head, 2), lax.rem(head, 2)

    xs = [lax.rem(x + k, 4) for k in range(4)]
    ys = [lax.rem(y + k, 4) for k in range(4)]
    zs = [lax.rem(z + k, 4) for k in range(4)]
    highs = [lax.div(v, 2) * 8 for v in ys]
    lows = [lax.rem(v, 2) for v in ys]
    shards_at = {(a, b): highs[b] + xs[a] * 2 + lows[b] for a in range(4) for b in range(4)}

    def place(px, py):
        return (lax.div(py, 2) * 4 + px) * 2 + lax.rem(py, 2)

    def shard(dx, dy):
        if isinstance(dx, int) and isinstance(dy, int):
            return shards_at[dx % 4, dy % 4]
        return place(lax.rem(x + dx, 4), lax.rem(y + dy, 4))

    blocks = {(k, same): zs[k] * 4 + 2 * (c if same else 1 - c) for k in range(4) for same in (0, 1)}
    dps = [lax.div(v, 2) * 4 + x for v in ys]
    targets = {("x", k): (dps[0] - x + xs[k], head, pair) for k in range(1, 4)}
    targets.update({("y", k): (dps[k], head, lows[k]) for k in range(1, 4)})
    targets.update({("z", k): (dp, zs[k] * 2 + c, pair) for k in range(1, 4)})
    targets["core", 1] = (dp, z * 2 + (1 - c), pair)
    heads = [lax.rem(head + k, 8) for k in range(8)]

    def along(axis, k):
        return targets[axis, k % 4]

    sems = {"plane": (send_sem, recv_sem), "core": (core_send, core_recv), "small": (small_send, small_recv)}

    def remote(src, dst, kind, leave, land, target):
        return pltpu.make_async_remote_copy(
            src_ref=src, dst_ref=dst, send_sem=sems[kind][0].at[leave], recv_sem=sems[kind][1].at[land],
            device_id=target, device_id_type=MESH,
        )

    def start(src, dst, kind, leave, land, target):
        remote(src, dst, kind, leave, land, target).start()

    def arrived(ref, kind, land):
        remote(ref, ref, kind, 0, land, along("x", 1)).wait_recv()

    def departed(ref, kind, leave):
        remote(ref, ref, kind, leave, 0, along("x", 1)).wait_send()

    def spot(h, a, b):
        return shard(a % 4, b % 4) if h == 0 else shard(b % 4, a % 4)

    def ring(h, primary):
        return "x" if (h == 0) == primary else "y"

    def part(rows, h, s=None, cut=None):
        cut = rows // 2 if cut is None else cut
        first, count = (0, cut) if h == 0 else (cut, rows - cut)
        if s is None:
            return pl.ds(first, count)
        return pl.ds(first + s * count // 2, count // 2)

    def gather(buf, t, rows):
        both = (0, 1)

        def go_(h, slot, a, b, s, primary, k):
            ref = buf.at[spot(h, a, b), part(rows, h, s)]
            start(ref, ref, "plane", t * 2 + h, (t * 2 + h) * SLOT + slot, along(ring(h, primary), k))

        def pair(h, slot):
            arrived(buf.at[pl.ds(0, 2), part(rows, h)], "plane", (t * 2 + h) * SLOT + slot)

        def whole(h, slot, a, b):
            arrived(buf.at[spot(h, a, b), part(rows, h)], "plane", (t * 2 + h) * SLOT + slot)

        def pass_on(h, slot, a, b, primary):
            for s, way in ((0, 1), (1, -1)):
                place_a, place_b = (-way, b) if primary else (a, -way)
                go_(h, slot, place_a, place_b, s, primary, way)

        for h in both:
            for way in (1, -1):
                go_(h, 0, 0, 0, None, True, way)
        for h in both:
            for way in (1, -1):
                go_(h, 2, 0, 0, None, False, way)
        yield
        for h in both:
            pair(h, 0)
            pass_on(h, 1, None, 0, True)
        for h in both:
            for k in (1, 3):
                for way in (1, -1):
                    go_(h, 2 + k, k, 0, None, False, way)
        yield
        for h in both:
            pair(h, 2)
            pass_on(h, 6, 0, None, False)
        yield 4
        for h in both:
            whole(h, 1, 2, 0)
            for way in (1, -1):
                go_(h, 4, 2, 0, None, False, way)
        yield
        for k in (1, 3):
            for h in both:
                pair(h, 2 + k)
                pass_on(h, 6 + k, k, None, False)
        yield 3
        for h in both:
            whole(h, 6, 0, 2)
        yield 2
        for h in both:
            pair(h, 4)
            pass_on(h, 8, 2, None, False)
        for h in both:
            for k in (1, 3):
                whole(h, 6 + k, k, 2)
        yield 1
        for h in both:
            whole(h, 8, 2, 2)
        yield 0

    class Reduce:
        def __init__(self, buf, ra, rb, rc, rd, t, cut, finish):
            self.buf, self.ra, self.rb, self.rc, self.rd = buf, ra, rb, rc, rd
            self.t, self.cut, self.write = t, cut, finish

        def part(self, h, s=None):
            return part(self.buf.shape[1], h, s, self.cut)

        def land(self, ref, h, s, *index):
            return ref.at[h, *index, pl.ds(0, self.part(h, s).size)]

        def send(self, h, slot, a, b, s, dst, primary, k):
            src = self.buf.at[spot(h, a, b), self.part(h, s)]
            start(src, dst, "plane", self.t * 2 + h, (self.t * 2 + h) * SLOT + slot, along(ring(h, primary), k))

        def got(self, h, slot, ref):
            arrived(ref, "plane", (self.t * 2 + h) * SLOT + slot)

        def add(self, h, a, b, s, *terms):
            j, rows = spot(h, a, b), self.part(h, s)
            total = self.buf[j, rows].astype(F32)
            for term in terms:
                total = total + term[...].astype(F32)
            self.buf[j, rows] = total.astype(BF16)

        def begin(self, k, h):
            for s, way in ((0, 1), (1, -1)):
                self.send(h, k, k, 2, s, self.land(self.ra, h, s, k, s), False, way)

        def middle(self, k, h):
            self.got(h, k, self.land(self.ra, h, 0, k, slice(None)))
            for s, way in ((0, 1), (1, -1)):
                self.add(h, k, way, s, self.land(self.ra, h, s, k, s))
                self.send(h, 4 + k, k, way, None, self.land(self.rb, h, None, k, s), False, way)

        def close(self, k, h):
            self.got(h, 4 + k, self.land(self.rb, h, None, k, slice(None)))
            self.add(h, k, 0, None, *[self.land(self.rb, h, None, k, s) for s in (0, 1)])
            if k == 2:
                for s, way in ((0, 1), (1, -1)):
                    self.send(h, 8, 2, 0, s, self.land(self.rc, h, s, s), True, way)

        def cross(self, h):
            self.got(h, 8, self.land(self.rc, h, 0, slice(None)))
            for s, way in ((0, 1), (1, -1)):
                self.add(h, way, 0, s, self.land(self.rc, h, s, s))
                self.send(h, 9, way, 0, None, self.land(self.rd, h, None, s), True, way)

        def finish(self, h):
            self.got(h, 4, self.land(self.rb, h, None, 0, slice(None)))
            self.got(h, 9, self.land(self.rd, h, None, slice(None)))
            terms = [self.land(self.rb, h, None, 0, s) for s in (0, 1)]
            terms += [self.land(self.rd, h, None, s) for s in (0, 1)]
            total = self.buf[spot(h, 0, 0), self.part(h)].astype(F32)
            for term in terms:
                total = total + term[...].astype(F32)
            self.write(h, total)

    class HeadReduce:
        def __init__(self, buf, r_core, r_za, r_zb, t):
            self.buf, self.r_core, self.r_za, self.r_zb, self.t = buf, r_core, r_za, r_zb, t

        def block(self, k, same):
            return blocks[k % 4, same]

        def add(self, k, i, rows, term):
            j = self.block(k, 1) + i
            self.buf[j, rows] = (self.buf[j, rows].astype(F32) + term.astype(F32)).astype(BF16)

        def swap(self, k):
            start(self.buf.at[pl.ds(self.block(k, 0), 2)], self.r_core.at[k], "core", self.t, self.t * 8 + k, along("core", 1))

        def got(self, slot, ref):
            arrived(ref, "core", self.t * 8 + slot)

        def begin(self, i):
            if i == 0:
                self.got(2, self.r_core.at[2])
            self.add(2, i, pl.ds(0, SLOTS), self.r_core[2, i])
            for s, way in ((0, 1), (1, -1)):
                rows = pl.ds(s * SLOTS // 2, SLOTS // 2)
                src = self.buf.at[self.block(2, 1) + i, rows]
                start(src, self.r_za.at[i, s], "core", self.t, self.t * 8 + 4 + i, along("z", way))

        def middle(self, i):
            if i == 0:
                self.got(1, self.r_core.at[1])
                self.got(3, self.r_core.at[3])
            self.got(4 + i, self.r_za.at[i])
            for s, way in ((0, 1), (1, -1)):
                self.add(way, i, pl.ds(0, SLOTS), self.r_core[way % 4, i])
                self.add(way, i, pl.ds(s * SLOTS // 2, SLOTS // 2), self.r_za[i, s])
                src = self.buf.at[self.block(way, 1) + i]
                start(src, self.r_zb.at[i, s], "core", self.t, self.t * 8 + 6 + i, along("z", way))

        def total(self, i):
            if i == 0:
                self.got(0, self.r_core.at[0])
            self.got(6 + i, self.r_zb.at[i])
            own_term = self.buf[2 * head + i].astype(F32) + self.r_core[0, i].astype(F32)
            return own_term + self.r_zb[i, 0].astype(F32) + self.r_zb[i, 1].astype(F32)

    def each(group, body):
        count, offsets = GROUPS[group]
        if count == 1:
            body(shard(*offsets(0)))
            return

        @pl.loop(0, count)
        def _(i):
            body(shard(*offsets(i)))

    own = shard(0, 0)
    barrier = pltpu.get_barrier_semaphore()
    others = [along("x", k) for k in (1, 2, 3)] + [along("y", k) for k in (1, 2, 3)]
    head_others = [(dp, heads[k], pair) for k in range(1, 8)]
    for target in others + head_others:
        pl.semaphore_signal(barrier, inc=1, device_id=target, device_id_type=MESH)
    weights = [
        (wq, wg.at[own, :, pl.ds(0, QC)]),
        (wk, wg.at[own, :, pl.ds(QC, HEAD_DIM)]),
        (wv, wg.at[own, :, pl.ds(QC + HEAD_DIM, HEAD_DIM)]),
        (wo, wog.at[own]),
        (gain_in, gain),
    ]
    loads = [pltpu.make_async_copy(src, dst, load_sem.at[2 + n]) for n, (src, dst) in enumerate(weights)]
    for copy in loads:
        copy.start()
    for copy in loads:
        copy.wait()
    pl.semaphore_wait(barrier, 13)

    stores = []

    def store(n, src, dst):
        copy = pltpu.make_async_copy(src, dst, store_sem.at[n])
        copy.start()
        stores.append(copy)

    w_gather = gather(wg, 0, ROWS)
    o_gather = gather(wog, 1, QC)
    next(w_gather)
    for n, (src, dst) in enumerate(((hidden, hid), (d_out, dout))):
        for j in range(SHARDS):
            pltpu.make_async_copy(src.at[:, pl.ds(j * ROWS, ROWS)], dst.at[j], load_sem.at[n]).start()

    def rotate(u):
        return u * cosf[...] + pltpu.roll(u, HEAD_DIM // 2, 1) * sinf[...]

    def unrotate(u):
        return u * cosf[...] - pltpu.roll(u, HEAD_DIM // 2, 1) * sinf[...]

    mine = pl.ds(pl.multiple_of(pair * HALF, HALF), HALF)
    theirs = pl.ds(pl.multiple_of((1 - pair) * HALF, HALF), HALF)
    partner = (dp, head, 1 - pair)

    def project(j):
        pacc[...] += dot_nn(normed[j], wg[j])

    def grad_attend(j):
        gacc[...] += dot_nt(dout[j], wog[j])

    def branch_term(j):
        hid[j] = dot_nn(att[...], wog[j]).astype(BF16)

    def norm_terms(k):
        first = 4 * zs[k]

        @pl.loop(0, 4)
        def _(i):
            normed[first + i] = dot_nt(dproj[...], wg[first + i]).astype(BF16)
        norm_sum.swap(k)

    def out_term(h):
        rows = slice(h * ROWS, (h + 1) * ROWS)

        def term(j):
            go[j, rows] = dot_nn(att_t[rows], dout[j]).astype(BF16)

        return term

    def query_term(h):
        cols = slice(h * ROWS, (h + 1) * ROWS)

        def term(j):
            wog[j, cols] = dot_nn(norm_t[j], dproj[:, cols]).astype(BF16)

        return term

    def kv_term(j):
        gkv[j] = dot_nn(norm_t[j], dproj[:, QC:]).astype(BF16)

    def out_finish(h, total):
        g_wo[h * ROWS:(h + 1) * ROWS, :] = total
        store(5 + 2 * h, g_wo.at[pl.ds(h * ROWS, ROWS)], g_wo_out.at[pl.ds(h * ROWS, ROWS)])

    def query_finish(h, total):
        g_wq[:, h * ROWS:(h + 1) * ROWS] = total
        store(2 + 6 * h, g_wq.at[:, pl.ds(h * ROWS, ROWS)], g_wq_out.at[:, pl.ds(h * ROWS, ROWS)])

    def kv_finish(h, total):
        rows = slice(0, KV_CUT) if h == 0 else slice(KV_CUT, ROWS)
        g_wk[rows, :] = total[:, :HEAD_DIM]
        g_wv[rows, :] = total[:, HEAD_DIM:]
        piece = pl.ds(0, KV_CUT) if h == 0 else pl.ds(KV_CUT, ROWS - KV_CUT)
        store(3 + 6 * h, g_wk.at[piece], g_wk_out.at[piece])
        store(4 + 6 * h, g_wv.at[piece], g_wv_out.at[piece])

    out = Reduce(go, oa, ob, oc, od, 3, ROWS, out_finish)
    query = Reduce(wog, qa, qb, qc, qd, 2, ROWS, query_finish)
    kv = Reduce(gkv, va, vb, vc, vd, 4, KV_CUT, kv_finish)
    branch_sum = HeadReduce(hid, p_core, p_za, p_zb, 0)
    norm_sum = HeadReduce(normed, n_core, n_za, n_zb, 1)

    def forward(g):
        cols = slice(g * HEAD_DIM, (g + 1) * HEAD_DIM)
        scores = dot_nt(qh[g], kall[...]) * SCALE + bias[...].astype(F32)
        expo = jnp.exp(scores - jnp.max(scores, -1, keepdims=True))
        prob = expo / jnp.sum(expo, -1, keepdims=True)
        probs[g] = prob
        attended = dot_nn(prob.astype(BF16), vall[...])
        attf[:, cols] = attended
        rounded = attended.astype(BF16)
        att[:, cols] = rounded
        att_t[cols, :] = rounded.T

    def backward(g):
        cols = slice(g * HEAD_DIM, (g + 1) * HEAD_DIM)
        g_head = gatt[:, cols]
        prob = probs[g]
        d_prob = dot_nt(g_head, vall[...])
        delta = jnp.sum(g_head.astype(F32) * attf[:, cols], -1, keepdims=True)
        d_score = (prob * (d_prob - delta) * SCALE).astype(BF16)
        dproj[:, cols] = unrotate(dot_nn(d_score, kall[...])).astype(BF16)
        dkv[0] += dot_tn(d_score, qh[g])
        dkv[1] += dot_tn(prob.astype(BF16), g_head)

    pltpu.make_async_copy(hid, hid, load_sem.at[0]).wait()
    pacc[:, 0:ROWS] = jnp.zeros((SLOTS, ROWS), F32)

    @pl.loop(0, SHARDS)
    def _(j):
        block = hid[j].astype(F32)
        pacc[:, 0:ROWS] += block * block

    mean = jnp.sum(pacc[:, 0:ROWS], -1, keepdims=True) * (1.0 / (SHARDS * ROWS))
    inv[...] = jnp.broadcast_to(lax.rsqrt(mean + EPS), (SLOTS, ROWS))

    def norm_block(j):
        block = (hid[j].astype(F32) * inv[...] * gain[j]).astype(BF16)
        normed[j] = block
        norm_t[j] = block.T

    @pl.loop(0, SHARDS)
    def _(j):
        norm_block(j)
    for i in range(2):
        hslice[i] = hid[2 * head + i]
    pacc[...] = dot_nn(normed[own], wg[own])
    next(w_gather)
    next(w_gather)
    next(w_gather)
    each(4, project)
    next(w_gather)
    each(3, project)
    next(w_gather)
    next(w_gather)
    next(o_gather)
    each(1, project)
    prompt_length, resp_length = plen[0], rlen[0]
    slot = lax.broadcasted_iota(jnp.int32, (SLOTS, HEAD_DIM), 0)
    lane = lax.broadcasted_iota(jnp.int32, (8, HEAD_DIM), 1)
    entry = jnp.where(lane < HEAD_DIM // 2, lane, lane - HEAD_DIM // 2)
    freqs = jnp.exp(-(entry.astype(F32) * (2.0 / HEAD_DIM)) * jnp.log(jnp.full((8, HEAD_DIM), BASE, F32)))
    position = jnp.where(slot < HALF, pair * HALF + slot, prompt_length + slot - HALF).astype(F32)
    angle = position * freqs[0:1]
    cosf[...] = jnp.cos(angle)
    sign = jnp.where(lane[0:1] < HEAD_DIM // 2, -1.0, 1.0).astype(F32)
    sinf[...] = jnp.sin(angle) * sign
    s_id = lax.broadcasted_iota(jnp.int32, (SLOTS, KEYS), 0)
    t_id = lax.broadcasted_iota(jnp.int32, (SLOTS, KEYS), 1)
    prompt_key = (t_id < 2 * HALF) & (t_id < prompt_length) & ((s_id >= HALF) | (t_id <= pair * HALF + s_id))
    resp_id = t_id - 2 * HALF
    resp_key = (t_id >= 2 * HALF) & (s_id >= HALF) & (resp_id <= s_id - HALF) & (resp_id < resp_length)
    bias[...] = jnp.where(prompt_key | resp_key, 0.0, -1e30).astype(BF16)
    next(w_gather)
    each(2, project)
    each(0, project)
    keys = rotate(pacc[:, QC:QC + HEAD_DIM]).astype(BF16)
    values = pacc[:, QC + HEAD_DIM:].astype(BF16)
    kall[mine] = keys[:HALF]
    kall[2 * HALF:] = keys[HALF:]
    vall[mine] = values[:HALF]
    vall[2 * HALF:] = values[HALF:]
    start(kall.at[mine], kall.at[mine], "small", 0, 0, partner)
    start(vall.at[mine], vall.at[mine], "small", 6, 6, partner)
    pltpu.make_async_copy(dout, dout, load_sem.at[1]).wait()
    gacc[...] = dot_nt(dout[own], wog[own])
    next(o_gather)
    for g in range(GROUP):
        qh[g] = rotate(pacc[:, g * HEAD_DIM:(g + 1) * HEAD_DIM]).astype(BF16)
    next(o_gather)
    each(4, grad_attend)
    arrived(kall.at[theirs], "small", 0)
    arrived(vall.at[theirs], "small", 6)
    forward(0)
    forward(1)
    forward(2)
    next(o_gather)
    forward(3)
    each(0, out_term(0))
    each(1, out_term(0))
    each(2, out_term(0))
    each(1, out_term(1))
    each(3, out_term(0))
    out.begin(1, 1)
    each(2, out_term(1))
    next(o_gather)
    each(3, out_term(1))
    out.begin(3, 0)
    out.begin(3, 1)
    each(3, grad_attend)
    each(4, branch_term)
    out.begin(1, 0)
    out.begin(0, 1)
    each(0, out_term(1))
    out.begin(2, 1)
    next(o_gather)
    each(3, branch_term)
    each(2, grad_attend)
    next(o_gather)
    out.middle(3, 1)
    each(5, branch_term)
    out.middle(3, 0)
    each(2, branch_term)
    out.middle(1, 1)
    each(1, branch_term)
    out.middle(2, 1)
    next(o_gather)
    each(0, branch_term)
    branch_sum.swap(1)
    out.middle(1, 0)
    out.begin(0, 0)
    out.begin(2, 0)
    branch_sum.swap(3)
    each(1, grad_attend)
    for t, buf, rows in ((0, wg, ROWS), (1, wog, QC)):
        for h in range(2):
            departed(buf.at[pl.ds(0, 15), part(rows, h)], "plane", t * 2 + h)
    each(0, grad_attend)
    branch_sum.swap(2)
    branch_sum.swap(0)
    gatt[...] = gacc[...].astype(BF16)
    dkv[...] = jnp.zeros_like(dkv)
    backward(0)
    backward(1)
    backward(2)
    backward(3)
    each(1, query_term(1))
    kv_out[0] = dkv[0, theirs].astype(BF16)
    kv_out[1] = dkv[1, theirs].astype(BF16)
    start(kv_out, kv_in, "small", 1, 1, partner)
    query.begin(3, 1)
    query.begin(1, 1)
    each(0, query_term(1))
    each(1, query_term(0))
    each(2, query_term(0))
    each(3, query_term(1))
    query.begin(2, 1)
    query.begin(3, 0)
    each(3, query_term(0))
    each(4, out_term(0))
    each(2, query_term(1))
    query.begin(0, 1)
    out.middle(0, 0)
    out.middle(2, 0)
    query.begin(1, 0)
    query.middle(1, 1)
    arrived(kv_in, "small", 1)
    d_keys = jnp.concatenate([dkv[0, mine] + kv_in[0].astype(F32), dkv[0, 2 * HALF:]], 0)
    d_values = jnp.concatenate([dkv[1, mine] + kv_in[1].astype(F32), dkv[1, 2 * HALF:]], 0)
    dproj[:, QC:QC + HEAD_DIM] = unrotate(d_keys).astype(BF16)
    dproj[:, QC + HEAD_DIM:] = d_values.astype(BF16)
    norm_terms(2)
    each(1, kv_term)
    query.middle(3, 1)
    query.middle(3, 0)
    each(2, kv_term)
    kv.begin(1, 1)
    each(4, out_term(1))
    out.close(3, 0)
    kv.begin(1, 0)
    branch_sum.begin(0)
    kv.begin(3, 1)
    out.middle(0, 1)
    norm_terms(3)
    branch_sum.begin(1)
    kv.begin(0, 0)
    each(0, query_term(0))
    kv.begin(3, 0)
    each(5, kv_term)
    norm_sum.begin(0)
    each(5, out_term(1))
    out.close(2, 0)
    query.middle(2, 1)
    each(0, kv_term)
    kv.begin(2, 0)
    norm_terms(1)
    kv.begin(2, 1)
    each(5, query_term(0))
    query.begin(0, 0)
    each(4, query_term(0))
    each(4, kv_term)
    out.close(1, 0)
    query.begin(2, 0)
    out.close(3, 1)
    query.middle(1, 0)
    norm_sum.begin(1)
    each(3, kv_term)
    out.close(2, 1)
    norm_sum.middle(0)
    kv.begin(0, 1)
    out.cross(0)
    kv.middle(2, 0)
    norm_terms(0)
    kv.middle(3, 1)
    norm_sum.middle(1)
    query.middle(2, 0)
    each(4, query_term(1))
    query.close(2, 1)
    branch_sum.middle(0)
    query.close(1, 0)
    query.close(3, 0)
    kv.middle(2, 1)
    query.close(1, 1)
    query.middle(0, 0)
    kv.middle(1, 0)
    query.close(2, 0)
    each(5, out_term(0))
    out.close(1, 1)
    kv.middle(1, 1)
    kv.middle(3, 0)
    kv.close(2, 0)
    out.cross(1)
    shares = [norm_sum.total(i) for i in range(2)]
    row_part = jnp.zeros((SLOTS, HEAD_DIM), F32)
    for i in range(2):
        scaled = hslice[i].astype(F32) * inv[...]
        gain_part = jnp.sum(shares[i] * scaled, 0, keepdims=True)
        gx[x, :, i * ROWS:(i + 1) * ROWS] = jnp.broadcast_to(gain_part, (8, ROWS))
        prod = shares[i] * gain[2 * head + i]
        g_hidden[:, i * ROWS:(i + 1) * ROWS] = prod
        prod = prod * scaled
        row_part = row_part + prod[:, :HEAD_DIM] + prod[:, HEAD_DIM:]
    row_sum = jnp.sum(row_part.T, 0, keepdims=True)
    rstat[head] = jnp.broadcast_to(row_sum, (8, SLOTS))
    for k in range(1, 8):
        start(rstat.at[head], rstat.at[head], "small", 2, 2, head_others[k - 1])
    for k in range(1, 4):
        start(gx.at[x], gx.at[x], "small", 3, 3, along("x", k))
    query.cross(0)
    query.close(3, 1)
    kv.close(2, 1)
    branch_sum.middle(1)
    kv.close(3, 0)
    query.middle(0, 1)
    kv.close(1, 0)
    arrived(gx.at[pl.ds(0, 3)], "small", 3)
    gy[y] = jnp.sum(gx[...], 0)
    for k in range(1, 4):
        start(gy.at[y], gy.at[y], "small", 4, 4, along("y", k))
    query.cross(1)
    kv.close(1, 1)
    kv.middle(0, 0)
    kv.close(3, 1)
    out.finish(0)
    kv.cross(0)
    arrived(gy.at[pl.ds(0, 3)], "small", 4)
    gh[head] = jnp.sum(gy[...], 0)
    for k in range(1, 8):
        start(gh.at[head], gh.at[head], "small", 5, 5, head_others[k - 1])
    query.finish(0)
    kv.cross(1)
    kv.middle(0, 1)
    each(5, query_term(1))
    out.finish(1)
    arrived(rstat.at[pl.ds(0, 7)], "small", 2)
    total = jnp.sum(rstat[...], 0)[0:1]
    mean = jnp.broadcast_to(total, (HEAD_DIM, SLOTS)).T * (1.0 / (SHARDS * ROWS))
    for i in range(4):
        cols = slice(i * HEAD_DIM, (i + 1) * HEAD_DIM)
        half = slice((i % 2) * HEAD_DIM, (i % 2 + 1) * HEAD_DIM)
        factor = inv[:, half]
        scaled = hslice[lax.div(i, 2), :, half].astype(F32) * factor
        g_hidden[:, cols] = factor * (g_hidden[:, cols] - scaled * mean)
    store(1, g_hidden, g_hidden_out)
    kv.finish(0)
    for i in range(2):
        branch[:, i * ROWS:(i + 1) * ROWS] = branch_sum.total(i).astype(BF16)
    store(0, branch, branch_out)
    query.finish(1)
    kv.finish(1)
    arrived(gh.at[pl.ds(0, 7)], "small", 5)
    for i in range(8):
        g_gain[:, i * QC:(i + 1) * QC] = gh[i, 0:1, :]
    store(6, g_gain, g_gain_out)
    for reduction in (out, query, kv):
        for h in range(2):
            departed(reduction.buf.at[pl.ds(0, 15), reduction.part(h)], "plane", reduction.t * 2 + h)
    for n, buf in enumerate((hid, normed)):
        departed(buf.at[pl.ds(0, 14)], "core", n)
    small = (kall.at[mine], kv_out, rstat.at[pl.ds(0, 7)], gx.at[pl.ds(0, 3)], gy.at[pl.ds(0, 3)], gh.at[pl.ds(0, 7)], vall.at[mine])
    for n, ref in enumerate(small):
        departed(ref, "small", n)
    for copy in stores:
        copy.wait()


def place_kernel(*refs):
    count = len(refs) // 3
    sems = refs[-1]
    loads, stores = [], []
    for i in range(count):
        loads.append(pltpu.make_async_copy(refs[i], refs[2 * count + i], sems.at[i]))
        stores.append(pltpu.make_async_copy(refs[2 * count + i], refs[count + i], sems.at[count + i]))
    for load in loads:
        load.start()
    for load, store in zip(loads, stores):
        load.wait()
        store.start()
    for store in stores:
        store.wait()


def shards(hidden, d_out, norm_gain, w_query, w_key, w_value, w_out, prompt_len, resp_len):
    smem = pl.BlockSpec(memory_space=pltpu.SMEM)
    anywhere = pl.BlockSpec(memory_space=pl.ANY)
    big = (SHARDS, SLOTS, ROWS)
    results = (
        jax.ShapeDtypeStruct((SLOTS, QC), BF16),
        jax.ShapeDtypeStruct((SLOTS, QC), F32),
        jax.ShapeDtypeStruct((ROWS, QC), F32),
        jax.ShapeDtypeStruct((ROWS, HEAD_DIM), F32),
        jax.ShapeDtypeStruct((ROWS, HEAD_DIM), F32),
        jax.ShapeDtypeStruct((QC, ROWS), F32),
        jax.ShapeDtypeStruct((1, 8 * QC), F32),
    )
    scratch = [pltpu.VMEM(out.shape, out.dtype) for out in results]
    scratch += [
        pltpu.VMEM((SHARDS, 1, ROWS), F32),
        pltpu.VMEM((SHARDS, ROWS, WC), BF16),
        pltpu.VMEM((SHARDS, QC, ROWS), BF16),
        pltpu.VMEM(big, BF16),
        pltpu.VMEM(big, BF16),
        pltpu.VMEM(big, BF16),
        pltpu.VMEM((SHARDS, ROWS, SLOTS), BF16),
        pltpu.VMEM((SHARDS, QC, ROWS), BF16),
        pltpu.VMEM((SHARDS, ROWS, ROWS), BF16),
    ]
    for rows, cols, cut in ((QC, ROWS, QC // 2), (QC, ROWS, QC // 2), (ROWS, ROWS, KV_CUT)):
        most = max(cut, rows - cut)
        scratch += [
            pltpu.VMEM((2, 4, 2, most // 2, cols), BF16),
            pltpu.VMEM((2, 4, 2, most, cols), BF16),
            pltpu.VMEM((2, 2, most // 2, cols), BF16),
            pltpu.VMEM((2, 2, most, cols), BF16),
        ]
    for _ in range(2):
        scratch += [
            pltpu.VMEM((4, 2, SLOTS, ROWS), BF16),
            pltpu.VMEM((2, 2, SLOTS // 2, ROWS), BF16),
            pltpu.VMEM((2, 2, SLOTS, ROWS), BF16),
        ]
    scratch += [
        pltpu.VMEM((GROUP, SLOTS, KEYS), F32),
        pltpu.VMEM((SLOTS, KEYS), BF16),
        pltpu.VMEM((SLOTS, WC), F32),
        pltpu.VMEM((SLOTS, QC), F32),
        pltpu.VMEM((SLOTS, QC), F32),
        pltpu.VMEM((SLOTS, QC), BF16),
        pltpu.VMEM((QC, SLOTS), BF16),
        pltpu.VMEM((SLOTS, QC), BF16),
        pltpu.VMEM((GROUP, SLOTS, HEAD_DIM), BF16),
        pltpu.VMEM((KEYS, HEAD_DIM), BF16),
        pltpu.VMEM((KEYS, HEAD_DIM), BF16),
        pltpu.VMEM((SLOTS, HEAD_DIM), F32),
        pltpu.VMEM((SLOTS, HEAD_DIM), F32),
        pltpu.VMEM((SLOTS, ROWS), F32),
        pltpu.VMEM((2, SLOTS, ROWS), BF16),
        pltpu.VMEM((SLOTS, WC), BF16),
        pltpu.VMEM((2, KEYS, HEAD_DIM), F32),
        pltpu.VMEM((2, HALF, HEAD_DIM), BF16),
        pltpu.VMEM((2, HALF, HEAD_DIM), BF16),
        pltpu.VMEM((8, 8, SLOTS), F32),
        pltpu.VMEM((4, 8, QC), F32),
        pltpu.VMEM((4, 8, QC), F32),
        pltpu.VMEM((8, 8, QC), F32),
        pltpu.SemaphoreType.DMA((7,)),
        pltpu.SemaphoreType.DMA((11,)),
        pltpu.SemaphoreType.DMA((10,)),
        pltpu.SemaphoreType.DMA((10 * SLOT,)),
        pltpu.SemaphoreType.DMA((2,)),
        pltpu.SemaphoreType.DMA((16,)),
        pltpu.SemaphoreType.DMA((7,)),
        pltpu.SemaphoreType.DMA((7,)),
    ]
    outs = pl.pallas_call(
        kernel,
        out_shape=results,
        in_specs=[anywhere, anywhere, anywhere, anywhere, anywhere, anywhere, anywhere, smem, smem],
        out_specs=(anywhere,) * 7,
        scratch_shapes=scratch,
        compiler_params=pltpu.CompilerParams(
            collective_id=0, has_side_effects=True, vmem_limit_bytes=65011712
        ),
        name="attention_step",
    )(
        hidden[0, 0], d_out[0, 0], norm_gain.reshape(SHARDS, 1, ROWS),
        w_query, w_key, w_value, w_out, prompt_len, resp_len[0],
    )
    branch, g_hidden, g_wq, g_wk, g_wv, g_wo, g_gain = pl.pallas_call(
        place_kernel,
        out_shape=tuple(jax.ShapeDtypeStruct(out.shape, out.dtype) for out in outs),
        in_specs=[anywhere] * 7,
        out_specs=(anywhere,) * 7,
        scratch_shapes=[pltpu.VMEM(out.shape, out.dtype) for out in outs] + [pltpu.SemaphoreType.DMA((14,))],
        name="place_results",
    )(*outs)
    return (branch[None, None], g_hidden[None, None], g_wq, g_wk, g_wv, g_wo, g_gain.reshape(-1))


def solution(mesh):
    in_specs = (
        P("dp", "pair", None, None),
        P("dp", "pair", None, None),
        P(),
        P(("dp", "pair"), "head"),
        P(("dp", "pair"), "head"),
        P(("dp", "pair"), "head"),
        P("head", ("dp", "pair")),
        P("dp"),
        P("dp", "pair"),
    )
    out_specs = (
        P("dp", "pair", None, "head"),
        P("dp", "pair", None, "head"),
        P(("dp", "pair"), "head"),
        P(("dp", "pair"), "head"),
        P(("dp", "pair"), "head"),
        P("head", ("dp", "pair")),
        P(),
    )
    return jax.shard_map(shards, mesh=mesh, in_specs=in_specs, out_specs=out_specs, check_vma=False)
```

```python
import functools

import jax
import jax.numpy as jnp
from jax import lax
from jax.experimental import pallas as pl
from jax.experimental.pallas import tpu as pltpu
from jax.sharding import PartitionSpec as P

HEAD_DIM = 128
HALF = 256
RESP = 128
SLOTS = HALF + RESP
KEYS = 2 * HALF + RESP
EPS = 1e-05
BASE = 500000.0
SCALE = HEAD_DIM ** (-0.5)
GROUP = 4
QC = GROUP * HEAD_DIM
WC = QC + 2 * HEAD_DIM
SHARDS = 16
ROWS = 256
MESH = pl.DeviceIdType.MESH
F32 = jnp.float32
BF16 = jnp.bfloat16
SLOT = 10
KV_CUT = 64


def dot_nn(a, b):
    return lax.dot_general(a, b, (((1,), (0,)), ((), ())), preferred_element_type=F32)


def dot_nt(a, b):
    return lax.dot_general(a, b, (((1,), (1,)), ((), ())), preferred_element_type=F32)


def dot_tn(a, b):
    return lax.dot_general(a, b, (((0,), (0,)), ((), ())), preferred_element_type=F32)


GROUPS = (
    (1, lambda i: (2, 2)),
    (4, lambda i: ((1 + 2 * lax.rem(i, 2)) * (1 - lax.div(i, 2)) + 2 * (lax.div(i, 2)), 2 * (1 - lax.div(i, 2)) + (1 + 2 * lax.rem(i, 2)) * (lax.div(i, 2)))),
    (2, lambda i: (2 * i, 2 * (1 - i))),
    (4, lambda i: (1 + 2 * lax.rem(i, 2), 1 + 2 * (lax.div(i, 2)))),
    (4, lambda i: ((1 + 2 * lax.rem(i, 2)) * (1 - lax.div(i, 2)), (1 + 2 * lax.rem(i, 2)) * (lax.div(i, 2)))),
    (1, lambda i: (0, 0)),
)


def kernel(
    hidden, d_out, gain_in, wq, wk, wv, wo, plen, rlen,
    branch_out, g_hidden_out, g_wq_out, g_wk_out, g_wv_out, g_wo_out, g_gain_out,
    branch, g_hidden, g_wq, g_wk, g_wv, g_wo, g_gain, gain,
    wg, wog, hid, dout, normed, norm_t, go, gkv,
    oa, ob, oc, od, qa, qb, qc, qd, va, vb, vc, vd,
    p_core, p_za, p_zb, n_core, n_za, n_zb,
    probs, bias, pacc, gacc, attf, att, att_t, gatt, qh, kall, vall, cosf, sinf, inv, hslice,
    dproj, dkv, kv_out, kv_in, rstat, gx, gy, gh,
    load_sem, store_sem, send_sem, recv_sem, core_send, core_recv, small_send, small_recv,
):
    dp, head, pair = lax.axis_index("dp"), lax.axis_index("head"), lax.axis_index("pair")
    x, y = lax.rem(dp, 4), lax.div(dp, 4) * 2 + pair
    z, c = lax.div(head, 2), lax.rem(head, 2)

    xs = [lax.rem(x + k, 4) for k in range(4)]
    ys = [lax.rem(y + k, 4) for k in range(4)]
    zs = [lax.rem(z + k, 4) for k in range(4)]
    highs = [lax.div(v, 2) * 8 for v in ys]
    lows = [lax.rem(v, 2) for v in ys]
    shards_at = {(a, b): highs[b] + xs[a] * 2 + lows[b] for a in range(4) for b in range(4)}

    def place(px, py):
        return (lax.div(py, 2) * 4 + px) * 2 + lax.rem(py, 2)

    def shard(dx, dy):
        if isinstance(dx, int) and isinstance(dy, int):
            return shards_at[dx % 4, dy % 4]
        return place(lax.rem(x + dx, 4), lax.rem(y + dy, 4))

    blocks = {(k, same): zs[k] * 4 + 2 * (c if same else 1 - c) for k in range(4) for same in (0, 1)}
    dps = [lax.div(v, 2) * 4 + x for v in ys]
    targets = {("x", k): (dps[0] - x + xs[k], head, pair) for k in range(1, 4)}
    targets.update({("y", k): (dps[k], head, lows[k]) for k in range(1, 4)})
    targets.update({("z", k): (dp, zs[k] * 2 + c, pair) for k in range(1, 4)})
    targets["core", 1] = (dp, z * 2 + (1 - c), pair)
    heads = [lax.rem(head + k, 8) for k in range(8)]

    def along(axis, k):
        return targets[axis, k % 4]

    sems = {"plane": (send_sem, recv_sem), "core": (core_send, core_recv), "small": (small_send, small_recv)}

    def remote(src, dst, kind, leave, land, target):
        return pltpu.make_async_remote_copy(
            src_ref=src, dst_ref=dst, send_sem=sems[kind][0].at[leave], recv_sem=sems[kind][1].at[land],
            device_id=target, device_id_type=MESH,
        )

    def start(src, dst, kind, leave, land, target):
        remote(src, dst, kind, leave, land, target).start()

    def arrived(ref, kind, land):
        remote(ref, ref, kind, 0, land, along("x", 1)).wait_recv()

    def departed(ref, kind, leave):
        remote(ref, ref, kind, leave, 0, along("x", 1)).wait_send()

    def spot(h, a, b):
        return shard(a % 4, b % 4) if h == 0 else shard(b % 4, a % 4)

    def ring(h, primary):
        return "x" if (h == 0) == primary else "y"

    def part(rows, h, s=None, cut=None):
        cut = rows // 2 if cut is None else cut
        first, count = (0, cut) if h == 0 else (cut, rows - cut)
        if s is None:
            return pl.ds(first, count)
        return pl.ds(first + s * count // 2, count // 2)

    def gather(buf, t, rows):
        both = (0, 1)

        def go_(h, slot, a, b, s, primary, k):
            ref = buf.at[spot(h, a, b), part(rows, h, s)]
            start(ref, ref, "plane", t * 2 + h, (t * 2 + h) * SLOT + slot, along(ring(h, primary), k))

        def pair(h, slot):
            arrived(buf.at[pl.ds(0, 2), part(rows, h)], "plane", (t * 2 + h) * SLOT + slot)

        def whole(h, slot, a, b):
            arrived(buf.at[spot(h, a, b), part(rows, h)], "plane", (t * 2 + h) * SLOT + slot)

        def pass_on(h, slot, a, b, primary):
            for s, way in ((0, 1), (1, -1)):
                place_a, place_b = (-way, b) if primary else (a, -way)
                go_(h, slot, place_a, place_b, s, primary, way)

        for h in both:
            for way in (1, -1):
                go_(h, 0, 0, 0, None, True, way)
        for h in both:
            for way in (1, -1):
                go_(h, 2, 0, 0, None, False, way)
        yield
        for h in both:
            pair(h, 0)
            pass_on(h, 1, None, 0, True)
        for h in both:
            for k in (1, 3):
                for way in (1, -1):
                    go_(h, 2 + k, k, 0, None, False, way)
        yield
        for h in both:
            pair(h, 2)
            pass_on(h, 6, 0, None, False)
        yield 4
        for h in both:
            whole(h, 1, 2, 0)
            for way in (1, -1):
                go_(h, 4, 2, 0, None, False, way)
        yield
        for k in (1, 3):
            for h in both:
                pair(h, 2 + k)
                pass_on(h, 6 + k, k, None, False)
        yield 3
        for h in both:
            whole(h, 6, 0, 2)
        yield 2
        for h in both:
            pair(h, 4)
            pass_on(h, 8, 2, None, False)
        for h in both:
            for k in (1, 3):
                whole(h, 6 + k, k, 2)
        yield 1
        for h in both:
            whole(h, 8, 2, 2)
        yield 0

    class Reduce:
        def __init__(self, buf, ra, rb, rc, rd, t, cut, finish):
            self.buf, self.ra, self.rb, self.rc, self.rd = buf, ra, rb, rc, rd
            self.t, self.cut, self.write = t, cut, finish

        def part(self, h, s=None):
            return part(self.buf.shape[1], h, s, self.cut)

        def land(self, ref, h, s, *index):
            return ref.at[h, *index, pl.ds(0, self.part(h, s).size)]

        def send(self, h, slot, a, b, s, dst, primary, k):
            src = self.buf.at[spot(h, a, b), self.part(h, s)]
            start(src, dst, "plane", self.t * 2 + h, (self.t * 2 + h) * SLOT + slot, along(ring(h, primary), k))

        def got(self, h, slot, ref):
            arrived(ref, "plane", (self.t * 2 + h) * SLOT + slot)

        def add(self, h, a, b, s, *terms):
            j, rows = spot(h, a, b), self.part(h, s)
            total = self.buf[j, rows].astype(F32)
            for term in terms:
                total = total + term[...].astype(F32)
            self.buf[j, rows] = total.astype(BF16)

        def begin(self, k, h):
            for s, way in ((0, 1), (1, -1)):
                self.send(h, k, k, 2, s, self.land(self.ra, h, s, k, s), False, way)

        def middle(self, k, h):
            self.got(h, k, self.land(self.ra, h, 0, k, slice(None)))
            for s, way in ((0, 1), (1, -1)):
                self.add(h, k, way, s, self.land(self.ra, h, s, k, s))
                self.send(h, 4 + k, k, way, None, self.land(self.rb, h, None, k, s), False, way)

        def close(self, k, h):
            self.got(h, 4 + k, self.land(self.rb, h, None, k, slice(None)))
            self.add(h, k, 0, None, *[self.land(self.rb, h, None, k, s) for s in (0, 1)])
            if k == 2:
                for s, way in ((0, 1), (1, -1)):
                    self.send(h, 8, 2, 0, s, self.land(self.rc, h, s, s), True, way)

        def cross(self, h):
            self.got(h, 8, self.land(self.rc, h, 0, slice(None)))
            for s, way in ((0, 1), (1, -1)):
                self.add(h, way, 0, s, self.land(self.rc, h, s, s))
                self.send(h, 9, way, 0, None, self.land(self.rd, h, None, s), True, way)

        def finish(self, h):
            self.got(h, 4, self.land(self.rb, h, None, 0, slice(None)))
            self.got(h, 9, self.land(self.rd, h, None, slice(None)))
            terms = [self.land(self.rb, h, None, 0, s) for s in (0, 1)]
            terms += [self.land(self.rd, h, None, s) for s in (0, 1)]
            total = self.buf[spot(h, 0, 0), self.part(h)].astype(F32)
            for term in terms:
                total = total + term[...].astype(F32)
            self.write(h, total)

    class HeadReduce:
        def __init__(self, buf, r_core, r_za, r_zb, t):
            self.buf, self.r_core, self.r_za, self.r_zb, self.t = buf, r_core, r_za, r_zb, t

        def block(self, k, same):
            return blocks[k % 4, same]

        def add(self, k, i, rows, term):
            j = self.block(k, 1) + i
            self.buf[j, rows] = (self.buf[j, rows].astype(F32) + term.astype(F32)).astype(BF16)

        def swap(self, k):
            start(self.buf.at[pl.ds(self.block(k, 0), 2)], self.r_core.at[k], "core", self.t, self.t * 8 + k, along("core", 1))

        def got(self, slot, ref):
            arrived(ref, "core", self.t * 8 + slot)

        def begin(self, i):
            if i == 0:
                self.got(2, self.r_core.at[2])
            self.add(2, i, pl.ds(0, SLOTS), self.r_core[2, i])
            for s, way in ((0, 1), (1, -1)):
                rows = pl.ds(s * SLOTS // 2, SLOTS // 2)
                src = self.buf.at[self.block(2, 1) + i, rows]
                start(src, self.r_za.at[i, s], "core", self.t, self.t * 8 + 4 + i, along("z", way))

        def middle(self, i):
            if i == 0:
                self.got(1, self.r_core.at[1])
                self.got(3, self.r_core.at[3])
            self.got(4 + i, self.r_za.at[i])
            for s, way in ((0, 1), (1, -1)):
                self.add(way, i, pl.ds(0, SLOTS), self.r_core[way % 4, i])
                self.add(way, i, pl.ds(s * SLOTS // 2, SLOTS // 2), self.r_za[i, s])
                src = self.buf.at[self.block(way, 1) + i]
                start(src, self.r_zb.at[i, s], "core", self.t, self.t * 8 + 6 + i, along("z", way))

        def total(self, i):
            if i == 0:
                self.got(0, self.r_core.at[0])
            self.got(6 + i, self.r_zb.at[i])
            own_term = self.buf[2 * head + i].astype(F32) + self.r_core[0, i].astype(F32)
            return own_term + self.r_zb[i, 0].astype(F32) + self.r_zb[i, 1].astype(F32)

    def each(group, body):
        count, offsets = GROUPS[group]
        if count == 1:
            body(shard(*offsets(0)))
            return

        @pl.loop(0, count, unroll=2)
        def _(i):
            body(shard(*offsets(i)))

    own = shard(0, 0)
    barrier = pltpu.get_barrier_semaphore()
    others = [along("x", k) for k in (1, 2, 3)] + [along("y", k) for k in (1, 2, 3)]
    head_others = [(dp, heads[k], pair) for k in range(1, 8)]
    for target in others + head_others:
        pl.semaphore_signal(barrier, inc=1, device_id=target, device_id_type=MESH)
    weights = [
        (wq, wg.at[own, :, pl.ds(0, QC)]),
        (wk, wg.at[own, :, pl.ds(QC, HEAD_DIM)]),
        (wv, wg.at[own, :, pl.ds(QC + HEAD_DIM, HEAD_DIM)]),
        (wo, wog.at[own]),
        (gain_in, gain),
    ]
    loads = [pltpu.make_async_copy(src, dst, load_sem.at[2 + n]) for n, (src, dst) in enumerate(weights)]
    for copy in loads:
        copy.start()
    for copy in loads:
        copy.wait()
    pl.semaphore_wait(barrier, 13)

    stores = []

    def store(n, src, dst):
        copy = pltpu.make_async_copy(src, dst, store_sem.at[n])
        copy.start()
        stores.append(copy)

    w_gather = gather(wg, 0, ROWS)
    o_gather = gather(wog, 1, QC)
    next(w_gather)
    for n, (src, dst) in enumerate(((hidden, hid), (d_out, dout))):
        for j in range(SHARDS):
            pltpu.make_async_copy(src.at[:, pl.ds(j * ROWS, ROWS)], dst.at[j], load_sem.at[n]).start()

    def rotate(u):
        return u * cosf[...] + pltpu.roll(u, HEAD_DIM // 2, 1) * sinf[...]

    def unrotate(u):
        return u * cosf[...] - pltpu.roll(u, HEAD_DIM // 2, 1) * sinf[...]

    mine = pl.ds(pl.multiple_of(pair * HALF, HALF), HALF)
    theirs = pl.ds(pl.multiple_of((1 - pair) * HALF, HALF), HALF)
    partner = (dp, head, 1 - pair)

    def project(j):
        pacc[...] += dot_nn(normed[j], wg[j])

    def grad_attend(j):
        gacc[...] += dot_nt(dout[j], wog[j])

    def branch_term(j):
        hid[j] = dot_nn(att[...], wog[j]).astype(BF16)

    def norm_terms(k):
        first = 4 * zs[k]

        @pl.loop(0, 4, unroll=2)
        def _(i):
            normed[first + i] = dot_nt(dproj[...], wg[first + i]).astype(BF16)
        norm_sum.swap(k)

    def out_term(h):
        rows = slice(h * ROWS, (h + 1) * ROWS)

        def term(j):
            go[j, rows] = dot_nn(att_t[rows], dout[j]).astype(BF16)

        return term

    def query_term(h):
        cols = slice(h * ROWS, (h + 1) * ROWS)

        def term(j):
            wog[j, cols] = dot_nn(norm_t[j], dproj[:, cols]).astype(BF16)

        return term

    def kv_term(j):
        gkv[j] = dot_nn(norm_t[j], dproj[:, QC:]).astype(BF16)

    def out_finish(h, total):
        g_wo[h * ROWS:(h + 1) * ROWS, :] = total
        store(5 + 2 * h, g_wo.at[pl.ds(h * ROWS, ROWS)], g_wo_out.at[pl.ds(h * ROWS, ROWS)])

    def query_finish(h, total):
        g_wq[:, h * ROWS:(h + 1) * ROWS] = total
        store(2 + 6 * h, g_wq.at[:, pl.ds(h * ROWS, ROWS)], g_wq_out.at[:, pl.ds(h * ROWS, ROWS)])

    def kv_finish(h, total):
        rows = slice(0, KV_CUT) if h == 0 else slice(KV_CUT, ROWS)
        g_wk[rows, :] = total[:, :HEAD_DIM]
        g_wv[rows, :] = total[:, HEAD_DIM:]
        piece = pl.ds(0, KV_CUT) if h == 0 else pl.ds(KV_CUT, ROWS - KV_CUT)
        store(3 + 6 * h, g_wk.at[piece], g_wk_out.at[piece])
        store(4 + 6 * h, g_wv.at[piece], g_wv_out.at[piece])

    out = Reduce(go, oa, ob, oc, od, 3, ROWS, out_finish)
    query = Reduce(wog, qa, qb, qc, qd, 2, ROWS, query_finish)
    kv = Reduce(gkv, va, vb, vc, vd, 4, KV_CUT, kv_finish)
    branch_sum = HeadReduce(hid, p_core, p_za, p_zb, 0)
    norm_sum = HeadReduce(normed, n_core, n_za, n_zb, 1)

    def forward(g):
        cols = slice(g * HEAD_DIM, (g + 1) * HEAD_DIM)
        scores = dot_nt(qh[g], kall[...]) * SCALE + bias[...].astype(F32)
        expo = jnp.exp(scores - jnp.max(scores, -1, keepdims=True))
        prob = expo / jnp.sum(expo, -1, keepdims=True)
        probs[g] = prob
        attended = dot_nn(prob.astype(BF16), vall[...])
        attf[:, cols] = attended
        rounded = attended.astype(BF16)
        att[:, cols] = rounded
        att_t[cols, :] = rounded.T

    def backward(g):
        cols = slice(g * HEAD_DIM, (g + 1) * HEAD_DIM)
        g_head = gatt[:, cols]
        prob = probs[g]
        d_prob = dot_nt(g_head, vall[...])
        delta = jnp.sum(g_head.astype(F32) * attf[:, cols], -1, keepdims=True)
        d_score = (prob * (d_prob - delta) * SCALE).astype(BF16)
        dproj[:, cols] = unrotate(dot_nn(d_score, kall[...])).astype(BF16)
        dkv[0] += dot_tn(d_score, qh[g])
        dkv[1] += dot_tn(prob.astype(BF16), g_head)

    pltpu.make_async_copy(hid, hid, load_sem.at[0]).wait()
    pacc[:, 0:ROWS] = jnp.zeros((SLOTS, ROWS), F32)

    @pl.loop(0, SHARDS)
    def _(j):
        block = hid[j].astype(F32)
        pacc[:, 0:ROWS] += block * block

    mean = jnp.sum(pacc[:, 0:ROWS], -1, keepdims=True) * (1.0 / (SHARDS * ROWS))
    inv[...] = jnp.broadcast_to(lax.rsqrt(mean + EPS), (SLOTS, ROWS))

    def norm_block(j):
        block = (hid[j].astype(F32) * inv[...] * gain[j]).astype(BF16)
        normed[j] = block
        norm_t[j] = block.T

    @pl.loop(0, SHARDS)
    def _(j):
        norm_block(j)
    for i in range(2):
        hslice[i] = hid[2 * head + i]
    pacc[...] = dot_nn(normed[own], wg[own])
    next(w_gather)
    next(w_gather)
    next(w_gather)
    each(4, project)
    next(w_gather)
    each(3, project)
    next(w_gather)
    next(w_gather)
    next(o_gather)
    each(1, project)
    prompt_length, resp_length = plen[0], rlen[0]
    slot = lax.broadcasted_iota(jnp.int32, (SLOTS, HEAD_DIM), 0)
    lane = lax.broadcasted_iota(jnp.int32, (8, HEAD_DIM), 1)
    entry = jnp.where(lane < HEAD_DIM // 2, lane, lane - HEAD_DIM // 2)
    freqs = jnp.exp(-(entry.astype(F32) * (2.0 / HEAD_DIM)) * jnp.log(jnp.full((8, HEAD_DIM), BASE, F32)))
    position = jnp.where(slot < HALF, pair * HALF + slot, prompt_length + slot - HALF).astype(F32)
    angle = position * freqs[0:1]
    cosf[...] = jnp.cos(angle)
    sign = jnp.where(lane[0:1] < HEAD_DIM // 2, -1.0, 1.0).astype(F32)
    sinf[...] = jnp.sin(angle) * sign
    s_id = lax.broadcasted_iota(jnp.int32, (SLOTS, KEYS), 0)
    t_id = lax.broadcasted_iota(jnp.int32, (SLOTS, KEYS), 1)
    prompt_key = (t_id < 2 * HALF) & (t_id < prompt_length) & ((s_id >= HALF) | (t_id <= pair * HALF + s_id))
    resp_id = t_id - 2 * HALF
    resp_key = (t_id >= 2 * HALF) & (s_id >= HALF) & (resp_id <= s_id - HALF) & (resp_id < resp_length)
    bias[...] = jnp.where(prompt_key | resp_key, 0.0, -1e30).astype(BF16)
    next(w_gather)
    each(2, project)
    each(0, project)
    keys = rotate(pacc[:, QC:QC + HEAD_DIM]).astype(BF16)
    values = pacc[:, QC + HEAD_DIM:].astype(BF16)
    kall[mine] = keys[:HALF]
    kall[2 * HALF:] = keys[HALF:]
    vall[mine] = values[:HALF]
    vall[2 * HALF:] = values[HALF:]
    start(kall.at[mine], kall.at[mine], "small", 0, 0, partner)
    start(vall.at[mine], vall.at[mine], "small", 6, 6, partner)
    pltpu.make_async_copy(dout, dout, load_sem.at[1]).wait()
    gacc[...] = dot_nt(dout[own], wog[own])
    next(o_gather)
    for g in range(GROUP):
        qh[g] = rotate(pacc[:, g * HEAD_DIM:(g + 1) * HEAD_DIM]).astype(BF16)
    next(o_gather)
    each(4, grad_attend)
    arrived(kall.at[theirs], "small", 0)
    arrived(vall.at[theirs], "small", 6)
    forward(0)
    forward(1)
    forward(2)
    next(o_gather)
    forward(3)
    each(0, out_term(0))
    each(1, out_term(0))
    each(2, out_term(0))
    each(1, out_term(1))
    each(3, out_term(0))
    out.begin(1, 1)
    each(2, out_term(1))
    next(o_gather)
    each(3, out_term(1))
    out.begin(3, 0)
    out.begin(3, 1)
    each(3, grad_attend)
    each(4, branch_term)
    out.begin(1, 0)
    out.begin(0, 1)
    each(0, out_term(1))
    out.begin(2, 1)
    next(o_gather)
    each(3, branch_term)
    each(2, grad_attend)
    next(o_gather)
    out.middle(3, 1)
    each(5, branch_term)
    out.middle(3, 0)
    each(2, branch_term)
    out.middle(1, 1)
    each(1, branch_term)
    out.middle(2, 1)
    next(o_gather)
    each(0, branch_term)
    branch_sum.swap(1)
    out.middle(1, 0)
    out.begin(0, 0)
    out.begin(2, 0)
    branch_sum.swap(3)
    each(1, grad_attend)
    for t, buf, rows in ((0, wg, ROWS), (1, wog, QC)):
        for h in range(2):
            departed(buf.at[pl.ds(0, 15), part(rows, h)], "plane", t * 2 + h)
    each(0, grad_attend)
    branch_sum.swap(2)
    branch_sum.swap(0)
    gatt[...] = gacc[...].astype(BF16)
    dkv[...] = jnp.zeros_like(dkv)
    backward(0)
    backward(1)
    backward(2)
    backward(3)
    each(1, query_term(1))
    kv_out[0] = dkv[0, theirs].astype(BF16)
    kv_out[1] = dkv[1, theirs].astype(BF16)
    start(kv_out, kv_in, "small", 1, 1, partner)
    query.begin(3, 1)
    query.begin(1, 1)
    each(0, query_term(1))
    each(1, query_term(0))
    each(2, query_term(0))
    each(3, query_term(1))
    query.begin(2, 1)
    query.begin(3, 0)
    each(3, query_term(0))
    each(4, out_term(0))
    each(2, query_term(1))
    query.begin(0, 1)
    out.middle(0, 0)
    out.middle(2, 0)
    query.begin(1, 0)
    query.middle(1, 1)
    arrived(kv_in, "small", 1)
    d_keys = jnp.concatenate([dkv[0, mine] + kv_in[0].astype(F32), dkv[0, 2 * HALF:]], 0)
    d_values = jnp.concatenate([dkv[1, mine] + kv_in[1].astype(F32), dkv[1, 2 * HALF:]], 0)
    dproj[:, QC:QC + HEAD_DIM] = unrotate(d_keys).astype(BF16)
    dproj[:, QC + HEAD_DIM:] = d_values.astype(BF16)
    norm_terms(2)
    each(1, kv_term)
    query.middle(3, 1)
    query.middle(3, 0)
    each(2, kv_term)
    kv.begin(1, 1)
    each(4, out_term(1))
    out.close(3, 0)
    kv.begin(1, 0)
    branch_sum.begin(0)
    kv.begin(3, 1)
    out.middle(0, 1)
    norm_terms(3)
    branch_sum.begin(1)
    kv.begin(0, 0)
    each(0, query_term(0))
    kv.begin(3, 0)
    each(5, kv_term)
    norm_sum.begin(0)
    each(5, out_term(1))
    out.close(2, 0)
    query.middle(2, 1)
    each(0, kv_term)
    kv.begin(2, 0)
    norm_terms(1)
    kv.begin(2, 1)
    each(5, query_term(0))
    query.begin(0, 0)
    each(4, query_term(0))
    each(4, kv_term)
    out.close(1, 0)
    query.begin(2, 0)
    out.close(3, 1)
    query.middle(1, 0)
    norm_sum.begin(1)
    each(3, kv_term)
    out.close(2, 1)
    norm_sum.middle(0)
    kv.begin(0, 1)
    out.cross(0)
    kv.middle(2, 0)
    norm_terms(0)
    kv.middle(3, 1)
    norm_sum.middle(1)
    query.middle(2, 0)
    each(4, query_term(1))
    query.close(2, 1)
    branch_sum.middle(0)
    query.close(1, 0)
    query.close(3, 0)
    kv.middle(2, 1)
    query.close(1, 1)
    query.middle(0, 0)
    kv.middle(1, 0)
    query.close(2, 0)
    each(5, out_term(0))
    out.close(1, 1)
    kv.middle(1, 1)
    kv.middle(3, 0)
    kv.close(2, 0)
    out.cross(1)
    shares = [norm_sum.total(i) for i in range(2)]
    row_part = jnp.zeros((SLOTS, HEAD_DIM), F32)
    for i in range(2):
        scaled = hslice[i].astype(F32) * inv[...]
        gain_part = jnp.sum(shares[i] * scaled, 0, keepdims=True)
        gx[x, :, i * ROWS:(i + 1) * ROWS] = jnp.broadcast_to(gain_part, (8, ROWS))
        prod = shares[i] * gain[2 * head + i]
        g_hidden[:, i * ROWS:(i + 1) * ROWS] = prod
        prod = prod * scaled
        row_part = row_part + prod[:, :HEAD_DIM] + prod[:, HEAD_DIM:]
    row_sum = jnp.sum(row_part.T, 0, keepdims=True)
    rstat[head] = jnp.broadcast_to(row_sum, (8, SLOTS))
    for k in range(1, 8):
        start(rstat.at[head], rstat.at[head], "small", 2, 2, head_others[k - 1])
    for k in range(1, 4):
        start(gx.at[x], gx.at[x], "small", 3, 3, along("x", k))
    query.cross(0)
    query.close(3, 1)
    kv.close(2, 1)
    branch_sum.middle(1)
    kv.close(3, 0)
    query.middle(0, 1)
    kv.close(1, 0)
    arrived(gx.at[pl.ds(0, 3)], "small", 3)
    gy[y] = jnp.sum(gx[...], 0)
    for k in range(1, 4):
        start(gy.at[y], gy.at[y], "small", 4, 4, along("y", k))
    query.cross(1)
    kv.close(1, 1)
    kv.middle(0, 0)
    kv.close(3, 1)
    out.finish(0)
    kv.cross(0)
    arrived(gy.at[pl.ds(0, 3)], "small", 4)
    gh[head] = jnp.sum(gy[...], 0)
    for k in range(1, 8):
        start(gh.at[head], gh.at[head], "small", 5, 5, head_others[k - 1])
    query.finish(0)
    kv.cross(1)
    kv.middle(0, 1)
    each(5, query_term(1))
    out.finish(1)
    arrived(rstat.at[pl.ds(0, 7)], "small", 2)
    total = jnp.sum(rstat[...], 0)[0:1]
    mean = jnp.broadcast_to(total, (HEAD_DIM, SLOTS)).T * (1.0 / (SHARDS * ROWS))
    for i in range(4):
        cols = slice(i * HEAD_DIM, (i + 1) * HEAD_DIM)
        half = slice((i % 2) * HEAD_DIM, (i % 2 + 1) * HEAD_DIM)
        factor = inv[:, half]
        scaled = hslice[lax.div(i, 2), :, half].astype(F32) * factor
        g_hidden[:, cols] = factor * (g_hidden[:, cols] - scaled * mean)
    store(1, g_hidden, g_hidden_out)
    kv.finish(0)
    for i in range(2):
        branch[:, i * ROWS:(i + 1) * ROWS] = branch_sum.total(i).astype(BF16)
    store(0, branch, branch_out)
    query.finish(1)
    kv.finish(1)
    arrived(gh.at[pl.ds(0, 7)], "small", 5)
    for i in range(8):
        g_gain[:, i * QC:(i + 1) * QC] = gh[i, 0:1, :]
    store(6, g_gain, g_gain_out)
    for reduction in (out, query, kv):
        for h in range(2):
            departed(reduction.buf.at[pl.ds(0, 15), reduction.part(h)], "plane", reduction.t * 2 + h)
    for n, buf in enumerate((hid, normed)):
        departed(buf.at[pl.ds(0, 14)], "core", n)
    small = (kall.at[mine], kv_out, rstat.at[pl.ds(0, 7)], gx.at[pl.ds(0, 3)], gy.at[pl.ds(0, 3)], gh.at[pl.ds(0, 7)], vall.at[mine])
    for n, ref in enumerate(small):
        departed(ref, "small", n)
    for copy in stores:
        copy.wait()


def place_kernel(*refs):
    count = len(refs) // 3
    sems = refs[-1]
    loads, stores = [], []
    for i in range(count):
        loads.append(pltpu.make_async_copy(refs[i], refs[2 * count + i], sems.at[i]))
        stores.append(pltpu.make_async_copy(refs[2 * count + i], refs[count + i], sems.at[count + i]))
    for load in loads:
        load.start()
    for load, store in zip(loads, stores):
        load.wait()
        store.start()
    for store in stores:
        store.wait()


def shards(hidden, d_out, norm_gain, w_query, w_key, w_value, w_out, prompt_len, resp_len):
    smem = pl.BlockSpec(memory_space=pltpu.SMEM)
    anywhere = pl.BlockSpec(memory_space=pl.ANY)
    big = (SHARDS, SLOTS, ROWS)
    results = (
        jax.ShapeDtypeStruct((SLOTS, QC), BF16),
        jax.ShapeDtypeStruct((SLOTS, QC), F32),
        jax.ShapeDtypeStruct((ROWS, QC), F32),
        jax.ShapeDtypeStruct((ROWS, HEAD_DIM), F32),
        jax.ShapeDtypeStruct((ROWS, HEAD_DIM), F32),
        jax.ShapeDtypeStruct((QC, ROWS), F32),
        jax.ShapeDtypeStruct((1, 8 * QC), F32),
    )
    scratch = [pltpu.VMEM(out.shape, out.dtype) for out in results]
    scratch += [
        pltpu.VMEM((SHARDS, 1, ROWS), F32),
        pltpu.VMEM((SHARDS, ROWS, WC), BF16),
        pltpu.VMEM((SHARDS, QC, ROWS), BF16),
        pltpu.VMEM(big, BF16),
        pltpu.VMEM(big, BF16),
        pltpu.VMEM(big, BF16),
        pltpu.VMEM((SHARDS, ROWS, SLOTS), BF16),
        pltpu.VMEM((SHARDS, QC, ROWS), BF16),
        pltpu.VMEM((SHARDS, ROWS, ROWS), BF16),
    ]
    for rows, cols, cut in ((QC, ROWS, QC // 2), (QC, ROWS, QC // 2), (ROWS, ROWS, KV_CUT)):
        most = max(cut, rows - cut)
        scratch += [
            pltpu.VMEM((2, 4, 2, most // 2, cols), BF16),
            pltpu.VMEM((2, 4, 2, most, cols), BF16),
            pltpu.VMEM((2, 2, most // 2, cols), BF16),
            pltpu.VMEM((2, 2, most, cols), BF16),
        ]
    for _ in range(2):
        scratch += [
            pltpu.VMEM((4, 2, SLOTS, ROWS), BF16),
            pltpu.VMEM((2, 2, SLOTS // 2, ROWS), BF16),
            pltpu.VMEM((2, 2, SLOTS, ROWS), BF16),
        ]
    scratch += [
        pltpu.VMEM((GROUP, SLOTS, KEYS), F32),
        pltpu.VMEM((SLOTS, KEYS), BF16),
        pltpu.VMEM((SLOTS, WC), F32),
        pltpu.VMEM((SLOTS, QC), F32),
        pltpu.VMEM((SLOTS, QC), F32),
        pltpu.VMEM((SLOTS, QC), BF16),
        pltpu.VMEM((QC, SLOTS), BF16),
        pltpu.VMEM((SLOTS, QC), BF16),
        pltpu.VMEM((GROUP, SLOTS, HEAD_DIM), BF16),
        pltpu.VMEM((KEYS, HEAD_DIM), BF16),
        pltpu.VMEM((KEYS, HEAD_DIM), BF16),
        pltpu.VMEM((SLOTS, HEAD_DIM), F32),
        pltpu.VMEM((SLOTS, HEAD_DIM), F32),
        pltpu.VMEM((SLOTS, ROWS), F32),
        pltpu.VMEM((2, SLOTS, ROWS), BF16),
        pltpu.VMEM((SLOTS, WC), BF16),
        pltpu.VMEM((2, KEYS, HEAD_DIM), F32),
        pltpu.VMEM((2, HALF, HEAD_DIM), BF16),
        pltpu.VMEM((2, HALF, HEAD_DIM), BF16),
        pltpu.VMEM((8, 8, SLOTS), F32),
        pltpu.VMEM((4, 8, QC), F32),
        pltpu.VMEM((4, 8, QC), F32),
        pltpu.VMEM((8, 8, QC), F32),
        pltpu.SemaphoreType.DMA((7,)),
        pltpu.SemaphoreType.DMA((11,)),
        pltpu.SemaphoreType.DMA((10,)),
        pltpu.SemaphoreType.DMA((10 * SLOT,)),
        pltpu.SemaphoreType.DMA((2,)),
        pltpu.SemaphoreType.DMA((16,)),
        pltpu.SemaphoreType.DMA((7,)),
        pltpu.SemaphoreType.DMA((7,)),
    ]
    outs = pl.pallas_call(
        kernel,
        out_shape=results,
        in_specs=[anywhere, anywhere, anywhere, anywhere, anywhere, anywhere, anywhere, smem, smem],
        out_specs=(anywhere,) * 7,
        scratch_shapes=scratch,
        compiler_params=pltpu.CompilerParams(
            collective_id=0, has_side_effects=True, vmem_limit_bytes=65011712
        ),
        name="attention_step",
    )(
        hidden[0, 0], d_out[0, 0], norm_gain.reshape(SHARDS, 1, ROWS),
        w_query, w_key, w_value, w_out, prompt_len, resp_len[0],
    )
    branch, g_hidden, g_wq, g_wk, g_wv, g_wo, g_gain = pl.pallas_call(
        place_kernel,
        out_shape=tuple(jax.ShapeDtypeStruct(out.shape, out.dtype) for out in outs),
        in_specs=[anywhere] * 7,
        out_specs=(anywhere,) * 7,
        scratch_shapes=[pltpu.VMEM(out.shape, out.dtype) for out in outs] + [pltpu.SemaphoreType.DMA((14,))],
        name="place_results",
    )(*outs)
    return (branch[None, None], g_hidden[None, None], g_wq, g_wk, g_wv, g_wo, g_gain.reshape(-1))


def solution(mesh):
    in_specs = (
        P("dp", "pair", None, None),
        P("dp", "pair", None, None),
        P(),
        P(("dp", "pair"), "head"),
        P(("dp", "pair"), "head"),
        P(("dp", "pair"), "head"),
        P("head", ("dp", "pair")),
        P("dp"),
        P("dp", "pair"),
    )
    out_specs = (
        P("dp", "pair", None, "head"),
        P("dp", "pair", None, "head"),
        P(("dp", "pair"), "head"),
        P(("dp", "pair"), "head"),
        P(("dp", "pair"), "head"),
        P("head", ("dp", "pair")),
        P(),
    )
    return jax.shard_map(shards, mesh=mesh, in_specs=in_specs, out_specs=out_specs, check_vma=False)
```

```python
import functools

import jax
import jax.numpy as jnp
from jax import lax
from jax.experimental import pallas as pl
from jax.experimental.pallas import tpu as pltpu
from jax.sharding import PartitionSpec as P

HEAD_DIM = 128
HALF = 256
RESP = 128
SLOTS = HALF + RESP
KEYS = 2 * HALF + RESP
EPS = 1e-05
BASE = 500000.0
SCALE = HEAD_DIM ** (-0.5)
GROUP = 4
QC = GROUP * HEAD_DIM
WC = QC + 2 * HEAD_DIM
SHARDS = 16
ROWS = 256
MESH = pl.DeviceIdType.MESH
F32 = jnp.float32
BF16 = jnp.bfloat16
SLOT = 10
KV_CUT = 64


def dot_nn(a, b):
    return lax.dot_general(a, b, (((1,), (0,)), ((), ())), preferred_element_type=F32)


def dot_nt(a, b):
    return lax.dot_general(a, b, (((1,), (1,)), ((), ())), preferred_element_type=F32)


def dot_tn(a, b):
    return lax.dot_general(a, b, (((0,), (0,)), ((), ())), preferred_element_type=F32)


GROUPS = (
    (1, lambda i: (2, 2)),
    (4, lambda i: ((1 + 2 * lax.rem(i, 2)) * (1 - lax.div(i, 2)) + 2 * (lax.div(i, 2)), 2 * (1 - lax.div(i, 2)) + (1 + 2 * lax.rem(i, 2)) * (lax.div(i, 2)))),
    (2, lambda i: (2 * i, 2 * (1 - i))),
    (4, lambda i: (1 + 2 * lax.rem(i, 2), 1 + 2 * (lax.div(i, 2)))),
    (4, lambda i: ((1 + 2 * lax.rem(i, 2)) * (1 - lax.div(i, 2)), (1 + 2 * lax.rem(i, 2)) * (lax.div(i, 2)))),
    (1, lambda i: (0, 0)),
)


def kernel(
    hidden, d_out, gain_in, wq, wk, wv, wo, plen, rlen,
    branch_out, g_hidden_out, g_wq_out, g_wk_out, g_wv_out, g_wo_out, g_gain_out,
    branch, g_hidden, g_wq, g_wk, g_wv, g_wo, g_gain, gain,
    wg, wog, hid, dout, normed, norm_t, go, gkv,
    oa, ob, oc, od, qa, qb, qc, qd, va, vb, vc, vd,
    p_core, p_za, p_zb, n_core, n_za, n_zb,
    probs, bias, pacc, gacc, attf, att, att_t, gatt, qh, kall, vall, cosf, sinf, inv, hslice,
    dproj, dkv, kv_out, kv_in, rstat, gx, gy, gh,
    load_sem, store_sem, send_sem, recv_sem, core_send, core_recv, small_send, small_recv,
):
    dp, head, pair = lax.axis_index("dp"), lax.axis_index("head"), lax.axis_index("pair")
    x, y = lax.rem(dp, 4), lax.div(dp, 4) * 2 + pair
    z, c = lax.div(head, 2), lax.rem(head, 2)

    xs = [lax.rem(x + k, 4) for k in range(4)]
    ys = [lax.rem(y + k, 4) for k in range(4)]
    zs = [lax.rem(z + k, 4) for k in range(4)]
    highs = [lax.div(v, 2) * 8 for v in ys]
    lows = [lax.rem(v, 2) for v in ys]
    shards_at = {(a, b): highs[b] + xs[a] * 2 + lows[b] for a in range(4) for b in range(4)}

    def place(px, py):
        return (lax.div(py, 2) * 4 + px) * 2 + lax.rem(py, 2)

    def shard(dx, dy):
        if isinstance(dx, int) and isinstance(dy, int):
            return shards_at[dx % 4, dy % 4]
        return place(lax.rem(x + dx, 4), lax.rem(y + dy, 4))

    blocks = {(k, same): zs[k] * 4 + 2 * (c if same else 1 - c) for k in range(4) for same in (0, 1)}
    dps = [lax.div(v, 2) * 4 + x for v in ys]
    targets = {("x", k): (dps[0] - x + xs[k], head, pair) for k in range(1, 4)}
    targets.update({("y", k): (dps[k], head, lows[k]) for k in range(1, 4)})
    targets.update({("z", k): (dp, zs[k] * 2 + c, pair) for k in range(1, 4)})
    targets["core", 1] = (dp, z * 2 + (1 - c), pair)
    heads = [lax.rem(head + k, 8) for k in range(8)]

    def along(axis, k):
        return targets[axis, k % 4]

    sems = {"plane": (send_sem, recv_sem), "core": (core_send, core_recv), "small": (small_send, small_recv)}

    def remote(src, dst, kind, leave, land, target):
        return pltpu.make_async_remote_copy(
            src_ref=src, dst_ref=dst, send_sem=sems[kind][0].at[leave], recv_sem=sems[kind][1].at[land],
            device_id=target, device_id_type=MESH,
        )

    def start(src, dst, kind, leave, land, target):
        remote(src, dst, kind, leave, land, target).start()

    def arrived(ref, kind, land):
        remote(ref, ref, kind, 0, land, along("x", 1)).wait_recv()

    def departed(ref, kind, leave):
        remote(ref, ref, kind, leave, 0, along("x", 1)).wait_send()

    def spot(h, a, b):
        return shard(a % 4, b % 4) if h == 0 else shard(b % 4, a % 4)

    def ring(h, primary):
        return "x" if (h == 0) == primary else "y"

    def part(rows, h, s=None, cut=None):
        cut = rows // 2 if cut is None else cut
        first, count = (0, cut) if h == 0 else (cut, rows - cut)
        if s is None:
            return pl.ds(first, count)
        return pl.ds(first + s * count // 2, count // 2)

    def gather(buf, t, rows):
        both = (0, 1)

        def go_(h, slot, a, b, s, primary, k):
            ref = buf.at[spot(h, a, b), part(rows, h, s)]
            start(ref, ref, "plane", t * 2 + h, (t * 2 + h) * SLOT + slot, along(ring(h, primary), k))

        def pair(h, slot):
            arrived(buf.at[pl.ds(0, 2), part(rows, h)], "plane", (t * 2 + h) * SLOT + slot)

        def whole(h, slot, a, b):
            arrived(buf.at[spot(h, a, b), part(rows, h)], "plane", (t * 2 + h) * SLOT + slot)

        def pass_on(h, slot, a, b, primary):
            for s, way in ((0, 1), (1, -1)):
                place_a, place_b = (-way, b) if primary else (a, -way)
                go_(h, slot, place_a, place_b, s, primary, way)

        for h in both:
            for way in (1, -1):
                go_(h, 0, 0, 0, None, True, way)
        for h in both:
            for way in (1, -1):
                go_(h, 2, 0, 0, None, False, way)
        yield
        for h in both:
            pair(h, 0)
            pass_on(h, 1, None, 0, True)
        for h in both:
            for k in (1, 3):
                for way in (1, -1):
                    go_(h, 2 + k, k, 0, None, False, way)
        yield
        for h in both:
            pair(h, 2)
            pass_on(h, 6, 0, None, False)
        yield 4
        for h in both:
            whole(h, 1, 2, 0)
            for way in (1, -1):
                go_(h, 4, 2, 0, None, False, way)
        yield
        for k in (1, 3):
            for h in both:
                pair(h, 2 + k)
                pass_on(h, 6 + k, k, None, False)
        yield 3
        for h in both:
            whole(h, 6, 0, 2)
        yield 2
        for h in both:
            pair(h, 4)
            pass_on(h, 8, 2, None, False)
        for h in both:
            for k in (1, 3):
                whole(h, 6 + k, k, 2)
        yield 1
        for h in both:
            whole(h, 8, 2, 2)
        yield 0

    class Reduce:
        def __init__(self, buf, ra, rb, rc, rd, t, cut, finish):
            self.buf, self.ra, self.rb, self.rc, self.rd = buf, ra, rb, rc, rd
            self.t, self.cut, self.write = t, cut, finish

        def part(self, h, s=None):
            return part(self.buf.shape[1], h, s, self.cut)

        def land(self, ref, h, s, *index):
            return ref.at[h, *index, pl.ds(0, self.part(h, s).size)]

        def send(self, h, slot, a, b, s, dst, primary, k):
            src = self.buf.at[spot(h, a, b), self.part(h, s)]
            start(src, dst, "plane", self.t * 2 + h, (self.t * 2 + h) * SLOT + slot, along(ring(h, primary), k))

        def got(self, h, slot, ref):
            arrived(ref, "plane", (self.t * 2 + h) * SLOT + slot)

        def add(self, h, a, b, s, *terms):
            j, rows = spot(h, a, b), self.part(h, s)
            if len(terms) == 1:
                self.buf[j, rows] += terms[0][...]
                return
            total = self.buf[j, rows].astype(F32)
            for term in terms:
                total = total + term[...].astype(F32)
            self.buf[j, rows] = total.astype(BF16)

        def begin(self, k, h):
            for s, way in ((0, 1), (1, -1)):
                self.send(h, k, k, 2, s, self.land(self.ra, h, s, k, s), False, way)

        def middle(self, k, h):
            self.got(h, k, self.land(self.ra, h, 0, k, slice(None)))
            for s, way in ((0, 1), (1, -1)):
                self.add(h, k, way, s, self.land(self.ra, h, s, k, s))
                self.send(h, 4 + k, k, way, None, self.land(self.rb, h, None, k, s), False, way)

        def close(self, k, h):
            self.got(h, 4 + k, self.land(self.rb, h, None, k, slice(None)))
            self.add(h, k, 0, None, *[self.land(self.rb, h, None, k, s) for s in (0, 1)])
            if k == 2:
                for s, way in ((0, 1), (1, -1)):
                    self.send(h, 8, 2, 0, s, self.land(self.rc, h, s, s), True, way)

        def cross(self, h):
            self.got(h, 8, self.land(self.rc, h, 0, slice(None)))
            for s, way in ((0, 1), (1, -1)):
                self.add(h, way, 0, s, self.land(self.rc, h, s, s))
                self.send(h, 9, way, 0, None, self.land(self.rd, h, None, s), True, way)

        def finish(self, h):
            self.got(h, 4, self.land(self.rb, h, None, 0, slice(None)))
            self.got(h, 9, self.land(self.rd, h, None, slice(None)))
            terms = [self.land(self.rb, h, None, 0, s) for s in (0, 1)]
            terms += [self.land(self.rd, h, None, s) for s in (0, 1)]
            total = self.buf[spot(h, 0, 0), self.part(h)].astype(F32)
            for term in terms:
                total = total + term[...].astype(F32)
            self.write(h, total)

    class HeadReduce:
        def __init__(self, buf, r_core, r_za, r_zb, t):
            self.buf, self.r_core, self.r_za, self.r_zb, self.t = buf, r_core, r_za, r_zb, t

        def block(self, k, same):
            return blocks[k % 4, same]

        def add(self, k, i, rows, term):
            j = self.block(k, 1) + i
            self.buf[j, rows] += term

        def swap(self, k):
            start(self.buf.at[pl.ds(self.block(k, 0), 2)], self.r_core.at[k], "core", self.t, self.t * 8 + k, along("core", 1))

        def got(self, slot, ref):
            arrived(ref, "core", self.t * 8 + slot)

        def begin(self, i):
            if i == 0:
                self.got(2, self.r_core.at[2])
            self.add(2, i, pl.ds(0, SLOTS), self.r_core[2, i])
            for s, way in ((0, 1), (1, -1)):
                rows = pl.ds(s * SLOTS // 2, SLOTS // 2)
                src = self.buf.at[self.block(2, 1) + i, rows]
                start(src, self.r_za.at[i, s], "core", self.t, self.t * 8 + 4 + i, along("z", way))

        def middle(self, i):
            if i == 0:
                self.got(1, self.r_core.at[1])
                self.got(3, self.r_core.at[3])
            self.got(4 + i, self.r_za.at[i])
            for s, way in ((0, 1), (1, -1)):
                self.add(way, i, pl.ds(0, SLOTS), self.r_core[way % 4, i])
                self.add(way, i, pl.ds(s * SLOTS // 2, SLOTS // 2), self.r_za[i, s])
                src = self.buf.at[self.block(way, 1) + i]
                start(src, self.r_zb.at[i, s], "core", self.t, self.t * 8 + 6 + i, along("z", way))

        def total(self, i):
            if i == 0:
                self.got(0, self.r_core.at[0])
            self.got(6 + i, self.r_zb.at[i])
            own_term = self.buf[2 * head + i].astype(F32) + self.r_core[0, i].astype(F32)
            return own_term + self.r_zb[i, 0].astype(F32) + self.r_zb[i, 1].astype(F32)

    def each(group, body):
        count, offsets = GROUPS[group]
        if count == 1:
            body(shard(*offsets(0)))
            return

        @pl.loop(0, count, unroll=2)
        def _(i):
            body(shard(*offsets(i)))

    own = shard(0, 0)
    barrier = pltpu.get_barrier_semaphore()
    others = [along("x", k) for k in (1, 2, 3)] + [along("y", k) for k in (1, 2, 3)]
    head_others = [(dp, heads[k], pair) for k in range(1, 8)]
    for target in others + head_others:
        pl.semaphore_signal(barrier, inc=1, device_id=target, device_id_type=MESH)
    weights = [
        (wq, wg.at[own, :, pl.ds(0, QC)]),
        (wk, wg.at[own, :, pl.ds(QC, HEAD_DIM)]),
        (wv, wg.at[own, :, pl.ds(QC + HEAD_DIM, HEAD_DIM)]),
        (wo, wog.at[own]),
        (gain_in, gain),
    ]
    loads = [pltpu.make_async_copy(src, dst, load_sem.at[2 + n]) for n, (src, dst) in enumerate(weights)]
    for copy in loads:
        copy.start()
    for copy in loads:
        copy.wait()
    pl.semaphore_wait(barrier, 13)

    stores = []

    def store(n, src, dst):
        copy = pltpu.make_async_copy(src, dst, store_sem.at[n])
        copy.start()
        stores.append(copy)

    w_gather = gather(wg, 0, ROWS)
    o_gather = gather(wog, 1, QC)
    next(w_gather)
    for n, (src, dst) in enumerate(((hidden, hid), (d_out, dout))):
        for j in range(SHARDS):
            pltpu.make_async_copy(src.at[:, pl.ds(j * ROWS, ROWS)], dst.at[j], load_sem.at[n]).start()

    def rotate(u):
        return u * cosf[...] + pltpu.roll(u, HEAD_DIM // 2, 1) * sinf[...]

    def unrotate(u):
        return u * cosf[...] - pltpu.roll(u, HEAD_DIM // 2, 1) * sinf[...]

    mine = pl.ds(pl.multiple_of(pair * HALF, HALF), HALF)
    theirs = pl.ds(pl.multiple_of((1 - pair) * HALF, HALF), HALF)
    partner = (dp, head, 1 - pair)

    def project(j):
        pacc[...] += dot_nn(normed[j], wg[j])

    def grad_attend(j):
        gacc[...] += dot_nt(dout[j], wog[j])

    def branch_term(j):
        hid[j] = dot_nn(att[...], wog[j]).astype(BF16)

    def norm_terms(k):
        first = 4 * zs[k]

        @pl.loop(0, 4, unroll=2)
        def _(i):
            normed[first + i] = dot_nt(dproj[...], wg[first + i]).astype(BF16)
        norm_sum.swap(k)

    def out_term(h):
        rows = slice(h * ROWS, (h + 1) * ROWS)

        def term(j):
            go[j, rows] = dot_nn(att_t[rows], dout[j]).astype(BF16)

        return term

    def query_term(h):
        cols = slice(h * ROWS, (h + 1) * ROWS)

        def term(j):
            wog[j, cols] = dot_nn(norm_t[j], dproj[:, cols]).astype(BF16)

        return term

    def kv_term(j):
        gkv[j] = dot_nn(norm_t[j], dproj[:, QC:]).astype(BF16)

    def out_finish(h, total):
        g_wo[h * ROWS:(h + 1) * ROWS, :] = total
        store(5 + 2 * h, g_wo.at[pl.ds(h * ROWS, ROWS)], g_wo_out.at[pl.ds(h * ROWS, ROWS)])

    def query_finish(h, total):
        g_wq[:, h * ROWS:(h + 1) * ROWS] = total
        store(2 + 6 * h, g_wq.at[:, pl.ds(h * ROWS, ROWS)], g_wq_out.at[:, pl.ds(h * ROWS, ROWS)])

    def kv_finish(h, total):
        rows = slice(0, KV_CUT) if h == 0 else slice(KV_CUT, ROWS)
        g_wk[rows, :] = total[:, :HEAD_DIM]
        g_wv[rows, :] = total[:, HEAD_DIM:]
        piece = pl.ds(0, KV_CUT) if h == 0 else pl.ds(KV_CUT, ROWS - KV_CUT)
        store(3 + 6 * h, g_wk.at[piece], g_wk_out.at[piece])
        store(4 + 6 * h, g_wv.at[piece], g_wv_out.at[piece])

    out = Reduce(go, oa, ob, oc, od, 3, ROWS, out_finish)
    query = Reduce(wog, qa, qb, qc, qd, 2, ROWS, query_finish)
    kv = Reduce(gkv, va, vb, vc, vd, 4, KV_CUT, kv_finish)
    branch_sum = HeadReduce(hid, p_core, p_za, p_zb, 0)
    norm_sum = HeadReduce(normed, n_core, n_za, n_zb, 1)

    def forward(g):
        cols = slice(g * HEAD_DIM, (g + 1) * HEAD_DIM)
        scores = dot_nt(qh[g], kall[...]) * SCALE + bias[...].astype(F32)
        expo = jnp.exp(scores - jnp.max(scores, -1, keepdims=True))
        prob = expo / jnp.sum(expo, -1, keepdims=True)
        probs[g] = prob
        attended = dot_nn(prob.astype(BF16), vall[...])
        attf[:, cols] = attended
        rounded = attended.astype(BF16)
        att[:, cols] = rounded
        att_t[cols, :] = rounded.T

    def backward(g):
        cols = slice(g * HEAD_DIM, (g + 1) * HEAD_DIM)
        g_head = gatt[:, cols]
        prob = probs[g]
        d_prob = dot_nt(g_head, vall[...])
        delta = jnp.sum(g_head.astype(F32) * attf[:, cols], -1, keepdims=True)
        d_score = (prob * (d_prob - delta) * SCALE).astype(BF16)
        dproj[:, cols] = unrotate(dot_nn(d_score, kall[...])).astype(BF16)
        dkv[0] += dot_tn(d_score, qh[g])
        dkv[1] += dot_tn(prob.astype(BF16), g_head)

    pltpu.make_async_copy(hid, hid, load_sem.at[0]).wait()
    pacc[:, 0:ROWS] = jnp.zeros((SLOTS, ROWS), F32)

    @pl.loop(0, SHARDS)
    def _(j):
        block = hid[j].astype(F32)
        pacc[:, 0:ROWS] += block * block

    mean = jnp.sum(pacc[:, 0:ROWS], -1, keepdims=True) * (1.0 / (SHARDS * ROWS))
    inv[...] = jnp.broadcast_to(lax.rsqrt(mean + EPS), (SLOTS, ROWS))

    def norm_block(j):
        block = (hid[j].astype(F32) * inv[...] * gain[j]).astype(BF16)
        normed[j] = block
        norm_t[j] = block.T

    @pl.loop(0, SHARDS)
    def _(j):
        norm_block(j)
    for i in range(2):
        hslice[i] = hid[2 * head + i]
    pacc[...] = dot_nn(normed[own], wg[own])
    next(w_gather)
    next(w_gather)
    next(w_gather)
    each(4, project)
    next(w_gather)
    each(3, project)
    next(w_gather)
    next(w_gather)
    next(o_gather)
    each(1, project)
    prompt_length, resp_length = plen[0], rlen[0]
    slot = lax.broadcasted_iota(jnp.int32, (SLOTS, HEAD_DIM), 0)
    lane = lax.broadcasted_iota(jnp.int32, (8, HEAD_DIM), 1)
    entry = jnp.where(lane < HEAD_DIM // 2, lane, lane - HEAD_DIM // 2)
    freqs = jnp.exp(-(entry.astype(F32) * (2.0 / HEAD_DIM)) * jnp.log(jnp.full((8, HEAD_DIM), BASE, F32)))
    position = jnp.where(slot < HALF, pair * HALF + slot, prompt_length + slot - HALF).astype(F32)
    angle = position * freqs[0:1]
    cosf[...] = jnp.cos(angle)
    sign = jnp.where(lane[0:1] < HEAD_DIM // 2, -1.0, 1.0).astype(F32)
    sinf[...] = jnp.sin(angle) * sign
    s_id = lax.broadcasted_iota(jnp.int32, (SLOTS, KEYS), 0)
    t_id = lax.broadcasted_iota(jnp.int32, (SLOTS, KEYS), 1)
    prompt_key = (t_id < 2 * HALF) & (t_id < prompt_length) & ((s_id >= HALF) | (t_id <= pair * HALF + s_id))
    resp_id = t_id - 2 * HALF
    resp_key = (t_id >= 2 * HALF) & (s_id >= HALF) & (resp_id <= s_id - HALF) & (resp_id < resp_length)
    bias[...] = jnp.where(prompt_key | resp_key, 0.0, -1e30).astype(BF16)
    next(w_gather)
    each(2, project)
    each(0, project)
    keys = rotate(pacc[:, QC:QC + HEAD_DIM]).astype(BF16)
    values = pacc[:, QC + HEAD_DIM:].astype(BF16)
    kall[mine] = keys[:HALF]
    kall[2 * HALF:] = keys[HALF:]
    vall[mine] = values[:HALF]
    vall[2 * HALF:] = values[HALF:]
    start(kall.at[mine], kall.at[mine], "small", 0, 0, partner)
    start(vall.at[mine], vall.at[mine], "small", 6, 6, partner)
    pltpu.make_async_copy(dout, dout, load_sem.at[1]).wait()
    gacc[...] = dot_nt(dout[own], wog[own])
    next(o_gather)
    for g in range(GROUP):
        qh[g] = rotate(pacc[:, g * HEAD_DIM:(g + 1) * HEAD_DIM]).astype(BF16)
    next(o_gather)
    each(4, grad_attend)
    arrived(kall.at[theirs], "small", 0)
    arrived(vall.at[theirs], "small", 6)
    forward(0)
    forward(1)
    forward(2)
    next(o_gather)
    forward(3)
    each(0, out_term(0))
    each(1, out_term(0))
    each(2, out_term(0))
    each(1, out_term(1))
    each(3, out_term(0))
    out.begin(1, 1)
    each(2, out_term(1))
    next(o_gather)
    each(3, out_term(1))
    out.begin(3, 0)
    out.begin(3, 1)
    each(3, grad_attend)
    each(4, branch_term)
    out.begin(1, 0)
    out.begin(0, 1)
    each(0, out_term(1))
    out.begin(2, 1)
    next(o_gather)
    each(3, branch_term)
    each(2, grad_attend)
    next(o_gather)
    out.middle(3, 1)
    each(5, branch_term)
    out.middle(3, 0)
    each(2, branch_term)
    out.middle(1, 1)
    each(1, branch_term)
    out.middle(2, 1)
    next(o_gather)
    each(0, branch_term)
    branch_sum.swap(1)
    out.middle(1, 0)
    out.begin(0, 0)
    out.begin(2, 0)
    branch_sum.swap(3)
    each(1, grad_attend)
    for t, buf, rows in ((0, wg, ROWS), (1, wog, QC)):
        for h in range(2):
            departed(buf.at[pl.ds(0, 15), part(rows, h)], "plane", t * 2 + h)
    each(0, grad_attend)
    branch_sum.swap(2)
    branch_sum.swap(0)
    gatt[...] = gacc[...].astype(BF16)
    dkv[...] = jnp.zeros_like(dkv)
    backward(0)
    backward(1)
    backward(2)
    backward(3)
    each(1, query_term(1))
    kv_out[0] = dkv[0, theirs].astype(BF16)
    kv_out[1] = dkv[1, theirs].astype(BF16)
    start(kv_out, kv_in, "small", 1, 1, partner)
    query.begin(3, 1)
    query.begin(1, 1)
    each(0, query_term(1))
    each(1, query_term(0))
    each(2, query_term(0))
    each(3, query_term(1))
    query.begin(2, 1)
    query.begin(3, 0)
    each(3, query_term(0))
    each(4, out_term(0))
    each(2, query_term(1))
    query.begin(0, 1)
    out.middle(0, 0)
    out.middle(2, 0)
    query.begin(1, 0)
    query.middle(1, 1)
    arrived(kv_in, "small", 1)
    d_keys = jnp.concatenate([dkv[0, mine] + kv_in[0].astype(F32), dkv[0, 2 * HALF:]], 0)
    d_values = jnp.concatenate([dkv[1, mine] + kv_in[1].astype(F32), dkv[1, 2 * HALF:]], 0)
    dproj[:, QC:QC + HEAD_DIM] = unrotate(d_keys).astype(BF16)
    dproj[:, QC + HEAD_DIM:] = d_values.astype(BF16)
    norm_terms(2)
    each(1, kv_term)
    query.middle(3, 1)
    query.middle(3, 0)
    each(2, kv_term)
    kv.begin(1, 1)
    each(4, out_term(1))
    out.close(3, 0)
    kv.begin(1, 0)
    branch_sum.begin(0)
    kv.begin(3, 1)
    out.middle(0, 1)
    norm_terms(3)
    branch_sum.begin(1)
    kv.begin(0, 0)
    each(0, query_term(0))
    kv.begin(3, 0)
    each(5, kv_term)
    norm_sum.begin(0)
    each(5, out_term(1))
    out.close(2, 0)
    query.middle(2, 1)
    each(0, kv_term)
    kv.begin(2, 0)
    norm_terms(1)
    kv.begin(2, 1)
    each(5, query_term(0))
    query.begin(0, 0)
    each(4, query_term(0))
    each(4, kv_term)
    out.close(1, 0)
    query.begin(2, 0)
    out.close(3, 1)
    query.middle(1, 0)
    norm_sum.begin(1)
    each(3, kv_term)
    out.close(2, 1)
    norm_sum.middle(0)
    kv.begin(0, 1)
    out.cross(0)
    kv.middle(2, 0)
    norm_terms(0)
    kv.middle(3, 1)
    norm_sum.middle(1)
    query.middle(2, 0)
    each(4, query_term(1))
    query.close(2, 1)
    branch_sum.middle(0)
    query.close(1, 0)
    query.close(3, 0)
    kv.middle(2, 1)
    query.close(1, 1)
    query.middle(0, 0)
    kv.middle(1, 0)
    query.close(2, 0)
    each(5, out_term(0))
    out.close(1, 1)
    kv.middle(1, 1)
    kv.middle(3, 0)
    kv.close(2, 0)
    out.cross(1)
    shares = [norm_sum.total(i) for i in range(2)]
    row_part = jnp.zeros((SLOTS, HEAD_DIM), F32)
    for i in range(2):
        scaled = hslice[i].astype(F32) * inv[...]
        gain_part = jnp.sum(shares[i] * scaled, 0, keepdims=True)
        gx[x, :, i * ROWS:(i + 1) * ROWS] = jnp.broadcast_to(gain_part, (8, ROWS))
        prod = shares[i] * gain[2 * head + i]
        g_hidden[:, i * ROWS:(i + 1) * ROWS] = prod
        prod = prod * scaled
        row_part = row_part + prod[:, :HEAD_DIM] + prod[:, HEAD_DIM:]
    row_sum = jnp.sum(row_part.T, 0, keepdims=True)
    rstat[head] = jnp.broadcast_to(row_sum, (8, SLOTS))
    for k in range(1, 8):
        start(rstat.at[head], rstat.at[head], "small", 2, 2, head_others[k - 1])
    for k in range(1, 4):
        start(gx.at[x], gx.at[x], "small", 3, 3, along("x", k))
    query.cross(0)
    query.close(3, 1)
    kv.close(2, 1)
    branch_sum.middle(1)
    kv.close(3, 0)
    query.middle(0, 1)
    kv.close(1, 0)
    arrived(gx.at[pl.ds(0, 3)], "small", 3)
    gy[y] = jnp.sum(gx[...], 0)
    for k in range(1, 4):
        start(gy.at[y], gy.at[y], "small", 4, 4, along("y", k))
    query.cross(1)
    kv.close(1, 1)
    kv.middle(0, 0)
    kv.close(3, 1)
    out.finish(0)
    kv.cross(0)
    arrived(gy.at[pl.ds(0, 3)], "small", 4)
    gh[head] = jnp.sum(gy[...], 0)
    for k in range(1, 8):
        start(gh.at[head], gh.at[head], "small", 5, 5, head_others[k - 1])
    query.finish(0)
    kv.cross(1)
    kv.middle(0, 1)
    each(5, query_term(1))
    out.finish(1)
    arrived(rstat.at[pl.ds(0, 7)], "small", 2)
    total = jnp.sum(rstat[...], 0)[0:1]
    mean = jnp.broadcast_to(total, (HEAD_DIM, SLOTS)).T * (1.0 / (SHARDS * ROWS))
    for i in range(4):
        cols = slice(i * HEAD_DIM, (i + 1) * HEAD_DIM)
        half = slice((i % 2) * HEAD_DIM, (i % 2 + 1) * HEAD_DIM)
        factor = inv[:, half]
        scaled = hslice[lax.div(i, 2), :, half].astype(F32) * factor
        g_hidden[:, cols] = factor * (g_hidden[:, cols] - scaled * mean)
    store(1, g_hidden, g_hidden_out)
    kv.finish(0)
    for i in range(2):
        branch[:, i * ROWS:(i + 1) * ROWS] = branch_sum.total(i).astype(BF16)
    store(0, branch, branch_out)
    query.finish(1)
    kv.finish(1)
    arrived(gh.at[pl.ds(0, 7)], "small", 5)
    for i in range(8):
        g_gain[:, i * QC:(i + 1) * QC] = gh[i, 0:1, :]
    store(6, g_gain, g_gain_out)
    for reduction in (out, query, kv):
        for h in range(2):
            departed(reduction.buf.at[pl.ds(0, 15), reduction.part(h)], "plane", reduction.t * 2 + h)
    for n, buf in enumerate((hid, normed)):
        departed(buf.at[pl.ds(0, 14)], "core", n)
    small = (kall.at[mine], kv_out, rstat.at[pl.ds(0, 7)], gx.at[pl.ds(0, 3)], gy.at[pl.ds(0, 3)], gh.at[pl.ds(0, 7)], vall.at[mine])
    for n, ref in enumerate(small):
        departed(ref, "small", n)
    for copy in stores:
        copy.wait()


def place_kernel(*refs):
    count = len(refs) // 3
    sems = refs[-1]
    loads, stores = [], []
    for i in range(count):
        loads.append(pltpu.make_async_copy(refs[i], refs[2 * count + i], sems.at[i]))
        stores.append(pltpu.make_async_copy(refs[2 * count + i], refs[count + i], sems.at[count + i]))
    for load in loads:
        load.start()
    for load, store in zip(loads, stores):
        load.wait()
        store.start()
    for store in stores:
        store.wait()


def shards(hidden, d_out, norm_gain, w_query, w_key, w_value, w_out, prompt_len, resp_len):
    smem = pl.BlockSpec(memory_space=pltpu.SMEM)
    anywhere = pl.BlockSpec(memory_space=pl.ANY)
    big = (SHARDS, SLOTS, ROWS)
    results = (
        jax.ShapeDtypeStruct((SLOTS, QC), BF16),
        jax.ShapeDtypeStruct((SLOTS, QC), F32),
        jax.ShapeDtypeStruct((ROWS, QC), F32),
        jax.ShapeDtypeStruct((ROWS, HEAD_DIM), F32),
        jax.ShapeDtypeStruct((ROWS, HEAD_DIM), F32),
        jax.ShapeDtypeStruct((QC, ROWS), F32),
        jax.ShapeDtypeStruct((1, 8 * QC), F32),
    )
    scratch = [pltpu.VMEM(out.shape, out.dtype) for out in results]
    scratch += [
        pltpu.VMEM((SHARDS, 1, ROWS), F32),
        pltpu.VMEM((SHARDS, ROWS, WC), BF16),
        pltpu.VMEM((SHARDS, QC, ROWS), BF16),
        pltpu.VMEM(big, BF16),
        pltpu.VMEM(big, BF16),
        pltpu.VMEM(big, BF16),
        pltpu.VMEM((SHARDS, ROWS, SLOTS), BF16),
        pltpu.VMEM((SHARDS, QC, ROWS), BF16),
        pltpu.VMEM((SHARDS, ROWS, ROWS), BF16),
    ]
    for rows, cols, cut in ((QC, ROWS, QC // 2), (QC, ROWS, QC // 2), (ROWS, ROWS, KV_CUT)):
        most = max(cut, rows - cut)
        scratch += [
            pltpu.VMEM((2, 4, 2, most // 2, cols), BF16),
            pltpu.VMEM((2, 4, 2, most, cols), BF16),
            pltpu.VMEM((2, 2, most // 2, cols), BF16),
            pltpu.VMEM((2, 2, most, cols), BF16),
        ]
    for _ in range(2):
        scratch += [
            pltpu.VMEM((4, 2, SLOTS, ROWS), BF16),
            pltpu.VMEM((2, 2, SLOTS // 2, ROWS), BF16),
            pltpu.VMEM((2, 2, SLOTS, ROWS), BF16),
        ]
    scratch += [
        pltpu.VMEM((GROUP, SLOTS, KEYS), F32),
        pltpu.VMEM((SLOTS, KEYS), BF16),
        pltpu.VMEM((SLOTS, WC), F32),
        pltpu.VMEM((SLOTS, QC), F32),
        pltpu.VMEM((SLOTS, QC), F32),
        pltpu.VMEM((SLOTS, QC), BF16),
        pltpu.VMEM((QC, SLOTS), BF16),
        pltpu.VMEM((SLOTS, QC), BF16),
        pltpu.VMEM((GROUP, SLOTS, HEAD_DIM), BF16),
        pltpu.VMEM((KEYS, HEAD_DIM), BF16),
        pltpu.VMEM((KEYS, HEAD_DIM), BF16),
        pltpu.VMEM((SLOTS, HEAD_DIM), F32),
        pltpu.VMEM((SLOTS, HEAD_DIM), F32),
        pltpu.VMEM((SLOTS, ROWS), F32),
        pltpu.VMEM((2, SLOTS, ROWS), BF16),
        pltpu.VMEM((SLOTS, WC), BF16),
        pltpu.VMEM((2, KEYS, HEAD_DIM), F32),
        pltpu.VMEM((2, HALF, HEAD_DIM), BF16),
        pltpu.VMEM((2, HALF, HEAD_DIM), BF16),
        pltpu.VMEM((8, 8, SLOTS), F32),
        pltpu.VMEM((4, 8, QC), F32),
        pltpu.VMEM((4, 8, QC), F32),
        pltpu.VMEM((8, 8, QC), F32),
        pltpu.SemaphoreType.DMA((7,)),
        pltpu.SemaphoreType.DMA((11,)),
        pltpu.SemaphoreType.DMA((10,)),
        pltpu.SemaphoreType.DMA((10 * SLOT,)),
        pltpu.SemaphoreType.DMA((2,)),
        pltpu.SemaphoreType.DMA((16,)),
        pltpu.SemaphoreType.DMA((7,)),
        pltpu.SemaphoreType.DMA((7,)),
    ]
    outs = pl.pallas_call(
        kernel,
        out_shape=results,
        in_specs=[anywhere, anywhere, anywhere, anywhere, anywhere, anywhere, anywhere, smem, smem],
        out_specs=(anywhere,) * 7,
        scratch_shapes=scratch,
        compiler_params=pltpu.CompilerParams(
            collective_id=0, has_side_effects=True, vmem_limit_bytes=65011712
        ),
        name="attention_step",
    )(
        hidden[0, 0], d_out[0, 0], norm_gain.reshape(SHARDS, 1, ROWS),
        w_query, w_key, w_value, w_out, prompt_len, resp_len[0],
    )
    branch, g_hidden, g_wq, g_wk, g_wv, g_wo, g_gain = pl.pallas_call(
        place_kernel,
        out_shape=tuple(jax.ShapeDtypeStruct(out.shape, out.dtype) for out in outs),
        in_specs=[anywhere] * 7,
        out_specs=(anywhere,) * 7,
        scratch_shapes=[pltpu.VMEM(out.shape, out.dtype) for out in outs] + [pltpu.SemaphoreType.DMA((14,))],
        name="place_results",
    )(*outs)
    return (branch[None, None], g_hidden[None, None], g_wq, g_wk, g_wv, g_wo, g_gain.reshape(-1))


def solution(mesh):
    in_specs = (
        P("dp", "pair", None, None),
        P("dp", "pair", None, None),
        P(),
        P(("dp", "pair"), "head"),
        P(("dp", "pair"), "head"),
        P(("dp", "pair"), "head"),
        P("head", ("dp", "pair")),
        P("dp"),
        P("dp", "pair"),
    )
    out_specs = (
        P("dp", "pair", None, "head"),
        P("dp", "pair", None, "head"),
        P(("dp", "pair"), "head"),
        P(("dp", "pair"), "head"),
        P(("dp", "pair"), "head"),
        P("head", ("dp", "pair")),
        P(),
    )
    return jax.shard_map(shards, mesh=mesh, in_specs=in_specs, out_specs=out_specs, check_vma=False)
```
